32 devices in a mesh: aux: 8 (over z, x), pair: 4 (over y, core).
Axes of the slice: x: 2, y: 2, z: 4, core: 2. Of those that a mesh axis runs over, the one named last changes fastest.
Arguments:
- shell_ints: bfloat16 [2048, 16, 64, 64], P('aux', 'pair'), may hold values from -0.119628906 to 0.119628906
- block_ids: int32 [16, 2], P('pair'), may hold values from 0 to 15
- block_count: int32 [4], P('pair'), may hold values from 1 to 4, 10 in all
- occ_coef: bfloat16 [16, 64, 512], replicated, may hold values from -0.75 to 0.75
- occ_pick: int32 [512], replicated, may hold values from 0 to 511, each once
- vir_coef: bfloat16 [16, 64, 384], replicated, may hold values from -0.1875 to 0.1875
- occ_energy: float32 [512], replicated, may hold values from -1.5 to -0.3
- vir_energy: float32 [384], replicated, may hold values from 0.2 to 3
Outputs:
- pair_energy: float32 [8], P('aux')
- vir_density: float32 [384, 384], P('pair')
The draws below stay inside these ranges and needn't reach their ends.
Inputs may be any that keep to these rules, and one draw needn't show every extreme that they name: `block_ids`: basis block numbers of the mu and nu side. `block_count`: the busiest group holds exactly 4 live blocks. `occ_pick`: each of the 512 numbers appears once.
All inputs are finite; a program needn't handle non-finite values.
Results may differ from the reference program's by a relative error of at most 0.01.
Values may be sent and summed in bfloat16 or wider, within the bound.
No kernel may reach another device: no remote copies, remote signals or barrier semaphores. Data moves between devices by JAX's collectives and lax.ppermute only.
A program may use at most 128 MiB of HBM per device.

```python
import math
import jax
import jax.numpy as jnp
import numpy as np
from jax import lax

Q_DEV = 256
BF = 64
NB_DEV = 4
NAOB = 16
NOCC = 512
VB = 384
NAUX = 2048
NBLK = 16
NGROUP = 4
N_AUX = 8
N_PAIR = 4


def plant(entries, own_key, smallest, top_value):
    spot = [jax.random.randint(jax.random.fold_in(own_key, axis), (), 0, length) for axis, length in enumerate(entries.shape)]
    widest = entries.shape.index(max(entries.shape))
    next_to = spot[:widest] + [(spot[widest] + 1) % entries.shape[widest]] + spot[widest + 1:]
    return entries.at[tuple(spot)].set(smallest).at[tuple(next_to)].set(top_value)


def block_levels(rng, shape, cuts, low, top_value):
    loudness = 1.0
    for axis_at, blocks in cuts:
        steps = jax.random.uniform(jax.random.fold_in(jax.random.fold_in(rng, 6), axis_at), (blocks,), jnp.float32, low / len(cuts), top_value / len(cuts))
        loudness = loudness * jnp.repeat(jnp.exp(steps), shape[axis_at] // blocks).reshape((-1,) + (1,) * (len(shape) - 1 - axis_at))
    return loudness


def split_up(amount, total, bound, slope):
    portions = [(1 << 20) // math.isqrt(grade ** slope) + 1 for grade in range(2, amount + 1)]
    spare, counts = total - bound - (amount - 1), [1] * (amount - 1)
    while spare > 0:
        candidates = [i for i in range(amount - 1) if counts[i] < bound]
        mass, budget = sum([portions[i] for i in candidates]), spare
        for i in candidates:
            addition = min(bound - counts[i], max(1, budget * portions[i] // mass), spare)
            counts[i] = counts[i] + addition
            spare = spare - addition
    return np.array([bound] + counts)


def ragged_sizes(stream_key, amount, total, reach, skew):
    if amount == 2:
        one = jax.random.randint(stream_key, (), max(1, total - reach), min(reach, total - 1) + 1)
        return jnp.stack([one, total - one])
    tallies = jnp.asarray(split_up(amount, total, reach, skew), jnp.int32)
    pairs = (amount - 1) // 2
    source_of, receiver = tallies[1:1 + 2 * pairs:2], tallies[2:2 + 2 * pairs:2]
    margin = jnp.minimum(source_of - 1, reach - receiver)
    passed = jax.random.randint(jax.random.fold_in(stream_key, 1), (pairs,), 0, 1 << 20) % (margin + 1)
    tallies = tallies.at[1:1 + 2 * pairs:2].set(source_of - passed).at[2:2 + 2 * pairs:2].set(receiver + passed)
    return tallies[jax.random.permutation(jax.random.fold_in(stream_key, 2), amount)]


def normal_values(key, shape, spread, most, split=(), held_as=jnp.bfloat16):
    array = spread * jax.random.normal(key, shape, jnp.float32)
    if split:
        array = array * block_levels(key, shape, split, -0.22, 0.18)
    return jnp.clip(array, -most, most).astype(held_as)


def setup_inputs(seed: int = 0) -> dict:
    arg_keys = jax.random.split(jax.random.key(seed), 9)
    return {
        "shell_ints": normal_values(arg_keys[0], (NAUX, NBLK, BF, BF), 0.02, 0.119628906, ((0, 8), (1, 4))),
        "block_ids": plant(jax.random.randint(arg_keys[1], (NBLK, 2), 0, NAOB), jax.random.fold_in(arg_keys[1], 1), 0, NAOB - 1).astype(jnp.int32),
        "block_count": ragged_sizes(arg_keys[2], NGROUP, NB_DEV * NGROUP * 5 // 8, NB_DEV, 2).astype(jnp.int32),
        "occ_coef": normal_values(arg_keys[3], (NAOB, BF, NOCC), BF ** -0.5, 0.75),
        "occ_pick": jax.random.permutation(arg_keys[4], NOCC).astype(jnp.int32),
        "vir_coef": normal_values(arg_keys[5], (NAOB, BF, VB), (NBLK * BF) ** -0.5, 0.1875),
        "occ_energy": jnp.clip(jax.random.uniform(arg_keys[6], (NOCC,), jnp.float32, -1.5, -0.3), -1.5, -0.3),
        "vir_energy": jnp.clip(jax.random.uniform(arg_keys[7], (VB,), jnp.float32, 0.2, 3.0), 0.2, 3.0),
    }


def reference(shell_ints, block_ids, block_count, occ_coef, occ_pick, vir_coef, occ_energy, vir_energy):
    batch = occ_pick[:N_AUX]
    occ_rows = occ_coef[block_ids[:, 1]][:, :, batch]
    slot_index = jnp.arange(NBLK, dtype=jnp.int32) % NB_DEV
    group_index = jnp.arange(NBLK, dtype=jnp.int32) // NB_DEV
    live = (slot_index < block_count[group_index]).astype(jnp.bfloat16)
    vir_rows = vir_coef[block_ids[:, 0]] * live[:, None, None]
    vir_groups = vir_rows.reshape(N_PAIR, NB_DEV * BF, VB).astype(jnp.float32)
    shards = shell_ints.reshape(N_AUX, Q_DEV, NBLK, BF, BF)

    def one_shard(ints):
        half = jnp.einsum("qkmn,kni->qikm", ints.astype(jnp.float32), occ_rows.astype(jnp.float32)).astype(jnp.bfloat16)
        half = half.reshape(Q_DEV, N_AUX, N_PAIR, NB_DEV * BF).astype(jnp.float32)
        parts = jnp.einsum("qigk,gka->gqia", half, vir_groups)
        parts = lax.optimization_barrier(parts.astype(jnp.bfloat16)).astype(jnp.float32)
        return jnp.sum(parts, axis=0).astype(jnp.bfloat16)

    fitted = lax.map(one_shard, shards).reshape(NAUX, N_AUX, VB)
    levels = occ_energy[batch]
    partners = (jnp.arange(N_AUX, dtype=jnp.int32) - N_AUX // 2) % N_AUX

    def pair_terms(total, g):
        h = partners[g]
        left = lax.dynamic_index_in_dim(fitted, g, 1, keepdims=False)
        right = lax.dynamic_index_in_dim(fitted, h, 1, keepdims=False)
        coulomb = jnp.dot(left.T, right, preferred_element_type=jnp.float32)
        denom = levels[g] + levels[h] - vir_energy[:, None] - vir_energy[None, :]
        amplitude = coulomb / denom
        energy = jnp.sum(amplitude * (2.0 * coulomb - coulomb.T))
        density = jnp.dot(2.0 * amplitude - amplitude.T, amplitude.T, precision=lax.Precision.HIGHEST)
        return total + density, energy

    vir_density, pair_energy = lax.scan(pair_terms, jnp.zeros((VB, VB), jnp.float32), jnp.arange(N_AUX, dtype=jnp.int32))
    return pair_energy, vir_density
```

```python
import functools

import jax
import jax.numpy as jnp
from jax import lax
from jax.experimental import pallas as pl
from jax.experimental.pallas import tpu as pltpu
from jax.sharding import PartitionSpec as P

VMEM = pltpu.VMEM
SMEM = pltpu.SMEM


def swapped(value, axis, mask):
    count = lax.axis_size(axis)
    return lax.ppermute(value, axis, [(source, source ^ mask) for source in range(count)])


def coulomb_kernel(ids_ref, place_ref, vir_ref, *refs):
    n_pair = (len(refs) - 3) // 2
    parts_in, parts_out = refs[:n_pair], refs[n_pair:-3]
    rows_ref, left_ref, right_ref = refs[-3:]
    slots = ids_ref.shape[0] // n_pair
    width, virtual = vir_ref.shape[1], vir_ref.shape[2]
    span = slots * width

    @pl.when(pl.program_id(0) == 0)
    def _():
        for at in range(n_pair * slots):
            block = ids_ref[at]
            row = vir_ref[jnp.maximum(block, 0)]
            rows_ref[pl.ds(at * width, width), :] = jnp.where(block >= 0, row, jnp.zeros_like(row))

    for side, target in enumerate((left_ref, right_ref)):
        total = jnp.zeros((virtual, parts_in[0].shape[-1]), jnp.float32)
        for group in range(n_pair):
            total += lax.dot_general(
                rows_ref[pl.ds(group * span, span), :],
                parts_in[group][0, side],
                (((0,), (0,)), ((), ())),
                preferred_element_type=jnp.float32,
            )
        target[...] = total.astype(jnp.bfloat16)
    share = virtual // len(parts_out)
    for part, out in enumerate(parts_out):
        first = pl.multiple_of((place_ref[0] ^ part) * share, share)
        out[0] = lax.dot_general(
            left_ref[pl.ds(first, share), :],
            right_ref[...],
            (((1,), (1,)), ((), ())),
            preferred_element_type=jnp.float32,
        ).astype(jnp.bfloat16)


def coulomb_parts(ids, place, vir_coef, parts, quad):
    pairs, _, span, aux_rows = parts[0].shape
    virtual = vir_coef.shape[2]
    share = virtual // quad
    n_pair = len(parts)
    return pl.pallas_call(
        coulomb_kernel,
        grid=(pairs,),
        in_specs=[
            pl.BlockSpec(memory_space=SMEM),
            pl.BlockSpec(memory_space=SMEM),
            pl.BlockSpec(vir_coef.shape, lambda r: (0, 0, 0)),
        ]
        + [pl.BlockSpec((1, 2, span, aux_rows), lambda r: (r, 0, 0, 0))] * n_pair,
        out_specs=[pl.BlockSpec((1, share, virtual), lambda r: (r, 0, 0))] * quad,
        out_shape=[jax.ShapeDtypeStruct((pairs, share, virtual), jnp.bfloat16)] * quad,
        scratch_shapes=[
            VMEM((n_pair * span, virtual), jnp.bfloat16),
            VMEM((virtual, aux_rows), jnp.bfloat16),
            VMEM((virtual, aux_rows), jnp.bfloat16),
        ],
        compiler_params=pltpu.CompilerParams(vmem_limit_bytes=48 * 1024 * 1024),
        name="coulomb_parts",
    )(ids, place, vir_coef, *parts)


def density_kernel(place_ref, level_ref, vir_ref, virt_ref, *refs):
    quad, n_pair, pairs = refs[0], refs[1], refs[2]
    chunks = refs[3 : 3 + quad]
    own_ref, outs = refs[3 + quad], refs[4 + quad : 3 + quad + n_pair]
    energy_ref, block_ref, even_ref, odd_ref, total_ref = refs[3 + quad + n_pair :]
    virtual = block_ref.shape[0]
    share = virtual // quad
    rows = virtual // n_pair
    step = pl.program_id(0)
    for part in range(quad):
        first = pl.multiple_of((place_ref[0] ^ part) * share, share)
        block_ref[pl.ds(first, share), :] = chunks[part][0].astype(jnp.float32)
    block = block_ref[...]
    flipped = block.T
    inverse = 1.0 / (level_ref[step] - vir_ref[...] - virt_ref[...])
    energy = jnp.sum(block * (2.0 * block - flipped) * inverse)
    even = ((block + flipped) * inverse).astype(jnp.bfloat16)
    odd = ((block - flipped) * inverse).astype(jnp.bfloat16)
    even_ref[...] = even
    odd_ref[...] = odd
    for part in range(n_pair):
        first = pl.multiple_of((place_ref[1] ^ part) * rows, rows)
        term = 0.5 * jnp.dot(even_ref[pl.ds(first, rows), :], even, preferred_element_type=jnp.float32)
        term -= 1.5 * jnp.dot(odd_ref[pl.ds(first, rows), :], odd, preferred_element_type=jnp.float32)
        if pairs > 1:
            term += jnp.where(step == 0, 0.0, total_ref[part])
            total_ref[part] = term
        if part == 0:
            own_ref[...] = term
        else:
            outs[part - 1][pl.ds(0, rows), :] = term.astype(jnp.bfloat16)
    high = jnp.full((16, virtual), energy, jnp.float32).astype(jnp.bfloat16)
    rest = energy - high.astype(jnp.float32)
    middle = rest.astype(jnp.bfloat16)
    low = (rest - middle.astype(jnp.float32)).astype(jnp.bfloat16)
    kind = lax.broadcasted_iota(jnp.int32, (16, virtual), 0)
    lane = lax.broadcasted_iota(jnp.int32, (16, virtual), 1)
    packed = jnp.where(kind == 0, high, jnp.where(kind == 1, middle, jnp.where(kind == 2, low, jnp.zeros_like(low))))
    held = jnp.where(lane == step, packed, jnp.where(step == 0, jnp.zeros_like(packed), energy_ref[...]))
    energy_ref[...] = held
    for out in outs:
        out[pl.ds(rows, 16), :] = held


def density_parts(place, levels, vir_energy, chunks, n_pair):
    quad = len(chunks)
    pairs, share, virtual = chunks[0].shape
    rows = virtual // n_pair

    def kernel(place_ref, level_ref, vir_ref, virt_ref, *refs):
        density_kernel(place_ref, level_ref, vir_ref, virt_ref, quad, n_pair, pairs, *refs)

    fixed = lambda shape: pl.BlockSpec(shape, lambda r: (0,) * len(shape))
    return pl.pallas_call(
        kernel,
        grid=(pairs,),
        in_specs=[
            pl.BlockSpec(memory_space=SMEM),
            pl.BlockSpec(memory_space=SMEM),
            fixed((virtual, 1)),
            fixed((1, virtual)),
        ]
        + [pl.BlockSpec((1, share, virtual), lambda r: (r, 0, 0))] * quad,
        out_specs=[fixed((rows, virtual))] + [fixed((rows + 16, virtual))] * (n_pair - 1) + [fixed((16, virtual))],
        out_shape=[jax.ShapeDtypeStruct((rows, virtual), jnp.float32)]
        + [jax.ShapeDtypeStruct((rows + 16, virtual), jnp.bfloat16)] * (n_pair - 1)
        + [jax.ShapeDtypeStruct((16, virtual), jnp.bfloat16)],
        scratch_shapes=[
            VMEM((virtual, virtual), jnp.float32),
            VMEM((virtual, virtual), jnp.bfloat16),
            VMEM((virtual, virtual), jnp.bfloat16),
            VMEM((n_pair, rows, virtual) if pairs > 1 else (1, 8, 128), jnp.float32),
        ],
        compiler_params=pltpu.CompilerParams(vmem_limit_bytes=48 * 1024 * 1024),
        name="density_parts",
    )(place, levels, vir_energy[:, None], vir_energy[None, :], *chunks)


def summed(value, axis, low, bits):
    if bits == 0:
        return value
    if bits == 1:
        other = swapped(value, axis, 1 << low)
        return (value.astype(jnp.float32) + other.astype(jnp.float32)).astype(jnp.bfloat16)
    place = (lax.axis_index(axis) >> low) & 3
    share = value.shape[1] // 4
    parts = [lax.dynamic_slice_in_dim(value, (place ^ d) * share, share, 1) for d in range(4)]
    chunks = scattered(parts, axis, low, bits)
    out = jnp.zeros_like(value)
    for d in range(4):
        out = lax.dynamic_update_slice_in_dim(out, chunks[d], (place ^ d) * share, 1)
    return out


def scattered(parts, axis, low, bits):
    total = parts[0].astype(jnp.float32)
    for d in (3, 2, 1):
        total += swapped(parts[d], axis, d << low).astype(jnp.float32)
    total = summed(total.astype(jnp.bfloat16), axis, low + 2, bits - 2)
    return [total] + [swapped(total, axis, d << low) for d in (1, 2, 3)]


def per_device(
    shell_ints, block_ids, block_count, occ_coef, occ_pick, vir_coef, occ_energy, vir_energy
):
    aux_rows, slots, width, _ = shell_ints.shape
    n_aux = lax.axis_size("aux")
    n_pair = lax.axis_size("pair")
    nocc = occ_coef.shape[2]
    virtual = vir_coef.shape[2]
    n_half = n_aux // 2
    pairs = n_half // n_pair
    aux_at = lax.axis_index("aux")
    pair_at = lax.axis_index("pair")

    live = jnp.arange(slots, dtype=jnp.int32) < block_count[0]
    mu_ids = jnp.where(live, block_ids[:, 0], -1)
    ids = jnp.concatenate([mu_ids] + [swapped(mu_ids, "pair", d) for d in range(1, n_pair)])

    mates = pair_at ^ jnp.arange(n_pair, dtype=jnp.int32)
    order = (mates[:, None] * pairs + jnp.arange(pairs, dtype=jnp.int32)[None, :])[:, :, None]
    order = (order + jnp.array([0, n_half], jnp.int32)[None, None, :]).reshape(n_aux)
    spots = jnp.arange(n_aux, dtype=jnp.int32)
    batch = jnp.sum(jnp.where(order[:, None] == spots[None, :], occ_pick[:n_aux][None, :], 0), axis=1)
    orbitals = jnp.arange(nocc, dtype=jnp.int32)
    chosen = orbitals[:, None] == batch[None, :]
    levels = jnp.sum(jnp.where(chosen[:, : 2 * pairs], occ_energy[:, None], 0.0), axis=0)
    levels = jnp.sum(levels.reshape(pairs, 2), axis=1)

    blocks = jnp.arange(occ_coef.shape[0], dtype=jnp.int32)
    nu_onehot = (block_ids[:, 1][:, None] == blocks[None, :]).astype(jnp.bfloat16)
    occ_rows = jnp.einsum("kt,tno->kno", nu_onehot, occ_coef, preferred_element_type=jnp.float32).astype(jnp.bfloat16)
    occ_sel = jnp.einsum(
        "kno,oi->kni", occ_rows, chosen.astype(jnp.bfloat16), preferred_element_type=jnp.float32
    ).astype(jnp.bfloat16)
    half = jnp.einsum(
        "qkmn,kni->ikmq", shell_ints, occ_sel, preferred_element_type=jnp.float32
    ).astype(jnp.bfloat16)
    half = half.reshape(n_pair, pairs, 2, slots * width, aux_rows)
    sent = [half[d] for d in range(n_pair)]
    got = [sent[0]] + [swapped(sent[d], "pair", d) for d in range(1, n_pair)]

    bits = n_aux.bit_length() - 1
    quad = 4 if bits >= 2 else 1
    place = jnp.stack([aux_at & (quad - 1), pair_at]).astype(jnp.int32)
    parts = coulomb_parts(ids, place, vir_coef, got, quad)
    chunks = scattered(parts, "aux", 0, bits)
    outs = density_parts(place, levels, vir_energy, chunks, n_pair)
    own, sent, energies = outs[0], outs[1:-1], outs[-1]
    rows = virtual // n_pair
    density = own
    energy = [energies]
    for d in range(1, n_pair):
        other = swapped(sent[d - 1], "pair", d)
        density += other[:rows].astype(jnp.float32)
        energy.append(other[rows:])
    found = jnp.stack(energy)[:, :3, :pairs].astype(jnp.float32).sum(axis=1)
    wanted = aux_at % n_half
    mine = mates[:, None] * pairs + jnp.arange(pairs, dtype=jnp.int32)[None, :] == wanted
    return (jnp.sum(jnp.where(mine, found, 0.0)).reshape(1), density)


def solution(mesh):
    placed = (P("aux", "pair", None, None), P("pair", None), P("pair"), P(), P(), P(), P(), P())
    return jax.shard_map(
        per_device,
        mesh=mesh,
        in_specs=placed,
        out_specs=(P("aux"), P("pair", None)),
        check_vma=False,
    )
```

```python
import jax
import jax.numpy as jnp
from jax import lax
from jax.experimental import pallas as pl
from jax.experimental.pallas import tpu as pltpu
from jax.sharding import PartitionSpec as P

VMEM = pltpu.VMEM
SMEM = pltpu.SMEM
TILE = 16
PARAMS = pltpu.CompilerParams(vmem_limit_bytes=48 * 1024 * 1024)


def swapped(value, axis, mask):
    count = lax.axis_size(axis)
    return lax.ppermute(value, axis, [(source, source ^ mask) for source in range(count)])


def whole(count):
    return [pl.BlockSpec(memory_space=VMEM)] * count


def half_blocks(ints, block_ids, block_count, occ_pick, occ_coef, first, count, n_aux, n_pair):
    slots, width, _, aux_rows = ints.shape
    nocc = occ_coef.shape[2]
    n_half = n_aux // 2
    pairs = n_half // n_pair
    steps = width // TILE
    depth = TILE * width
    rows = 2 * pairs * count * width

    def kernel(ids_hbm, count_hbm, pick_hbm, occ_ref, ints_hbm, *refs):
        outs, (ids_ref, count_ref, pick_ref, held, small, large) = refs[:n_pair], refs[n_pair:]
        copies = []
        for at in range(count * steps):
            copy = pltpu.make_async_copy(
                ints_hbm.at[pl.ds((first * steps + at) * depth, depth), :],
                held.at[pl.ds(at * depth, depth), :],
                large.at[at],
            )
            copy.start()
            copies.append(copy)
        tables = [
            pltpu.make_async_copy(source, target, small.at[at])
            for at, (source, target) in enumerate(
                ((ids_hbm, ids_ref), (count_hbm, count_ref), (pick_hbm, pick_ref))
            )
        ]
        for copy in tables:
            copy.start()
        for copy in tables:
            copy.wait()
        pair_at = lax.axis_index("pair")
        lane = lax.broadcasted_iota(jnp.int32, (TILE, nocc), 1)
        chosen = []
        for mate in range(n_pair):
            for pair in range(pairs):
                for side in range(2):
                    orbital = pick_ref[(pair_at ^ mate) * pairs + pair + side * n_half]
                    chosen.append(jnp.where(lane == orbital, 1.0, 0.0))
        chosen = jnp.concatenate(chosen, axis=0).astype(jnp.bfloat16)
        shape = (n_aux * TILE, depth)
        diagonal = lax.broadcasted_iota(jnp.int32, shape, 0) % TILE == lax.broadcasted_iota(jnp.int32, shape, 1) // width
        row = lax.broadcasted_iota(jnp.int32, (TILE, aux_rows), 0)
        blocks = jnp.full((TILE, aux_rows), -1.0, jnp.float32)
        for slot in range(slots):
            block = jnp.where(slot < count_ref[0], ids_ref[0, slot], -1).astype(jnp.float32)
            blocks = jnp.where(row == slot, block, blocks)
        for out in outs:
            out[pl.ds(rows, TILE), :] = blocks.astype(jnp.bfloat16)
        for slot in range(count):
            table = occ_ref[ids_ref[1, first + slot]]
            table = jnp.concatenate([table] * (128 // width), axis=0)
            spread = lax.dot_general(chosen, table, (((1,), (1,)), ((), ())), preferred_element_type=jnp.float32)
            spread = jnp.concatenate([spread] * (depth // 128), axis=1)
            weights = jnp.where(diagonal, spread, 0.0).astype(jnp.bfloat16)
            for step in range(steps):
                at = slot * steps + step
                copies[at].wait()
                made = jnp.dot(weights, held[pl.ds(at * depth, depth), :], preferred_element_type=jnp.float32)
                made = made.astype(jnp.bfloat16)
                for mate in range(n_pair):
                    for orbital in range(2 * pairs):
                        source = (mate * 2 * pairs + orbital) * TILE
                        target = orbital * count * width + at * TILE
                        outs[mate][pl.ds(target, TILE), :] = made[source : source + TILE]

    anywhere = pl.BlockSpec(memory_space=pl.ANY)
    return pl.pallas_call(
        kernel,
        in_specs=[anywhere, anywhere, anywhere, pl.BlockSpec(memory_space=VMEM), anywhere],
        out_specs=whole(n_pair),
        out_shape=[jax.ShapeDtypeStruct((rows + TILE, aux_rows), jnp.bfloat16)] * n_pair,
        scratch_shapes=[
            SMEM((2, slots), jnp.int32),
            SMEM((1,), jnp.int32),
            SMEM((nocc,), jnp.int32),
            VMEM((count * width * width, aux_rows), jnp.bfloat16),
            pltpu.SemaphoreType.DMA((3,)),
            pltpu.SemaphoreType.DMA((count * steps,)),
        ],
        compiler_params=PARAMS,
        cost_estimate=pl.CostEstimate(
            flops=2 * n_aux * width * width * count * aux_rows,
            bytes_accessed=2 * count * width * width * aux_rows,
            transcendentals=0,
        ),
        name="half_blocks",
    )(block_ids.T, block_count, occ_pick, occ_coef, ints.reshape(-1, aux_rows))


def fitted_first(vir_coef, parts, pairs, counts):
    n_pair = len(parts)
    aux_rows = parts[0].shape[1]
    width, virtual = vir_coef.shape[1], vir_coef.shape[2]
    span = counts[0] * width

    def kernel(vir_ref, *refs):
        held, (fitted_ref, rest_ref, own_ref) = refs[:n_pair], refs[n_pair:]
        rows, later = [], []
        for part in held:
            tail = part[pl.ds(2 * pairs * span, TILE), :][:, :128].astype(jnp.float32)
            for slot in range(sum(counts)):
                block = tail[slot, 0].astype(jnp.int32)
                row = vir_ref[jnp.maximum(block, 0)]
                row = jnp.where(block >= 0, row, jnp.zeros_like(row))
                (rows if slot < counts[0] else later).append(row)
        own_ref[...] = jnp.concatenate(rows, axis=0).T
        rest_ref[...] = jnp.concatenate(later, axis=0).T
        for orbital in range(2 * pairs):
            blocks = jnp.concatenate([part[pl.ds(orbital * span, span), :] for part in held], axis=0)
            fitted_ref[orbital] = jnp.dot(own_ref[...], blocks, preferred_element_type=jnp.float32)

    return pl.pallas_call(
        kernel,
        in_specs=whole(1 + n_pair),
        out_specs=whole(2),
        out_shape=[
            jax.ShapeDtypeStruct((2 * pairs, virtual, aux_rows), jnp.float32),
            jax.ShapeDtypeStruct((virtual, n_pair * counts[1] * width), jnp.bfloat16),
        ],
        scratch_shapes=[VMEM((virtual, n_pair * span), jnp.bfloat16)],
        compiler_params=PARAMS,
        name="fitted_first",
    )(vir_coef, *parts)


def coulomb_parts(fitted, rest, parts, pairs, span, quad):
    n_pair = len(parts)
    virtual, aux_rows = fitted.shape[1:]
    share = virtual // quad

    def kernel(fitted_ref, rest_ref, *refs):
        held, outs, left_ref = refs[:n_pair], refs[n_pair:-1], refs[-1]
        place = lax.axis_index("aux") % quad
        for pair in range(pairs):
            sides = []
            for orbital in (2 * pair, 2 * pair + 1):
                blocks = jnp.concatenate([part[pl.ds(orbital * span, span), :] for part in held], axis=0)
                total = jnp.dot(rest_ref[...], blocks, preferred_element_type=jnp.float32)
                sides.append((fitted_ref[orbital] + total).astype(jnp.bfloat16))
            left_ref[...] = sides[0]
            for part, out in enumerate(outs):
                at = pl.multiple_of((place ^ part) * share, share)
                out[pair] = lax.dot_general(
                    left_ref[pl.ds(at, share), :],
                    sides[1],
                    (((1,), (1,)), ((), ())),
                    preferred_element_type=jnp.float32,
                ).astype(jnp.bfloat16)

    return pl.pallas_call(
        kernel,
        in_specs=whole(2 + n_pair),
        out_specs=whole(quad),
        out_shape=[jax.ShapeDtypeStruct((pairs, share, virtual), jnp.bfloat16)] * quad,
        scratch_shapes=[VMEM((virtual, aux_rows), jnp.bfloat16)],
        compiler_params=PARAMS,
        name="coulomb_parts",
    )(fitted, rest, *parts)


def density_parts(inverse, chunks, n_pair):
    quad = len(chunks)
    pairs, share, virtual = chunks[0].shape
    rows = virtual // n_pair

    def kernel(inverse_ref, *refs):
        held, own_ref, outs = refs[:quad], refs[quad], refs[quad + 1 : quad + n_pair]
        energy_ref, block_ref, even_ref, odd_ref = refs[quad + n_pair :]
        place = lax.axis_index("aux") % quad
        pair_at = lax.axis_index("pair")
        kind = lax.broadcasted_iota(jnp.int32, (TILE, virtual), 0)
        lane = lax.broadcasted_iota(jnp.int32, (TILE, virtual), 1)
        energies = jnp.zeros((TILE, virtual), jnp.float32)
        totals = [None] * n_pair
        for pair in range(pairs):
            for part in range(quad):
                at = pl.multiple_of((place ^ part) * share, share)
                block_ref[pl.ds(at, share), :] = held[part][pair].astype(jnp.float32)
            block = block_ref[...]
            flipped = block.T
            inverse = inverse_ref[pair]
            energy = jnp.sum(block * (2.0 * block - flipped) * inverse)
            even = ((block + flipped) * inverse).astype(jnp.bfloat16)
            odd = ((block - flipped) * inverse).astype(jnp.bfloat16)
            even_ref[...] = even
            odd_ref[...] = odd
            for part in range(n_pair):
                at = pl.multiple_of((pair_at ^ part) * rows, rows)
                term = 0.5 * jnp.dot(even_ref[pl.ds(at, rows), :], even, preferred_element_type=jnp.float32)
                term -= 1.5 * jnp.dot(odd_ref[pl.ds(at, rows), :], odd, preferred_element_type=jnp.float32)
                totals[part] = term if pair == 0 else totals[part] + term
            energies = jnp.where(lane == pair, energy, energies)
        own_ref[...] = totals[0]
        high = energies.astype(jnp.bfloat16)
        rest = energies - high.astype(jnp.float32)
        middle = rest.astype(jnp.bfloat16)
        low = (rest - middle.astype(jnp.float32)).astype(jnp.bfloat16)
        zero = jnp.zeros_like(high)
        packed = jnp.where(kind == 0, high, jnp.where(kind == 1, middle, jnp.where(kind == 2, low, zero)))
        energy_ref[...] = packed
        for part in range(1, n_pair):
            outs[part - 1][pl.ds(0, rows), :] = totals[part].astype(jnp.bfloat16)
            outs[part - 1][pl.ds(rows, TILE), :] = packed

    return pl.pallas_call(
        kernel,
        in_specs=whole(1 + quad),
        out_specs=whole(n_pair + 1),
        out_shape=[jax.ShapeDtypeStruct((rows, virtual), jnp.float32)]
        + [jax.ShapeDtypeStruct((rows + TILE, virtual), jnp.bfloat16)] * (n_pair - 1)
        + [jax.ShapeDtypeStruct((TILE, virtual), jnp.bfloat16)],
        scratch_shapes=[
            VMEM((virtual, virtual), jnp.float32),
            VMEM((virtual, virtual), jnp.bfloat16),
            VMEM((virtual, virtual), jnp.bfloat16),
        ],
        compiler_params=PARAMS,
        name="density_parts",
    )(inverse, *chunks)


def closing(own, energies, others, pairs, n_half):
    rows, virtual = own.shape

    def kernel(own_ref, energy_ref, *refs):
        held, (density_ref, value_ref) = refs[: len(others)], refs[len(others) :]
        wanted = lax.axis_index("aux") % n_half
        pair_at = lax.axis_index("pair")
        lane = lax.broadcasted_iota(jnp.int32, (TILE, virtual), 1)
        tails = [energy_ref[...]] + [ref[pl.ds(rows, TILE), :] for ref in held]
        found = jnp.zeros((TILE, virtual), jnp.float32)
        for mate, tail in enumerate(tails):
            at = wanted - (pair_at ^ mate) * pairs
            at = jnp.where((at >= 0) & (at < pairs), at, -1)
            found += jnp.where(lane == at, tail.astype(jnp.float32), 0.0)
        value_ref[0] = jnp.sum(found)
        total = own_ref[...]
        for ref in held:
            total += ref[pl.ds(0, rows), :].astype(jnp.float32)
        density_ref[...] = total

    return pl.pallas_call(
        kernel,
        in_specs=whole(2 + len(others)),
        out_specs=[pl.BlockSpec(memory_space=VMEM), pl.BlockSpec(memory_space=SMEM)],
        out_shape=[jax.ShapeDtypeStruct((rows, virtual), jnp.float32), jax.ShapeDtypeStruct((1,), jnp.float32)],
        compiler_params=PARAMS,
        name="closing",
    )(own, energies, *others)


def summed(value, axis, low, bits):
    if bits == 0:
        return value
    if bits == 1:
        other = swapped(value, axis, 1 << low)
        return (value.astype(jnp.float32) + other.astype(jnp.float32)).astype(jnp.bfloat16)
    place = (lax.axis_index(axis) >> low) & 3
    share = value.shape[1] // 4
    parts = [lax.dynamic_slice_in_dim(value, (place ^ d) * share, share, 1) for d in range(4)]
    chunks = scattered(parts, axis, low, bits)
    out = jnp.zeros_like(value)
    for d in range(4):
        out = lax.dynamic_update_slice_in_dim(out, chunks[d], (place ^ d) * share, 1)
    return out


def scattered(parts, axis, low, bits):
    total = parts[0].astype(jnp.float32)
    for d in range(1, len(parts)):
        total += swapped(parts[d], axis, d << low).astype(jnp.float32)
    total = summed(total.astype(jnp.bfloat16), axis, low + 2, bits - 2)
    return [total] + [swapped(total, axis, d << low) for d in range(1, len(parts))]


def per_device(
    shell_ints, block_ids, block_count, occ_coef, occ_pick, vir_coef, occ_energy, vir_energy
):
    _, slots, width, _ = shell_ints.shape
    n_aux = lax.axis_size("aux")
    n_pair = lax.axis_size("pair")
    n_half = n_aux // 2
    pairs = n_half // n_pair
    bits = n_aux.bit_length() - 1

    ints = jnp.transpose(shell_ints, (1, 2, 3, 0))
    counts = (slots // 2, slots - slots // 2)
    sent, got = [], []
    for first, count in ((0, counts[0]), (counts[0], counts[1])):
        made = half_blocks(ints, block_ids, block_count, occ_pick, occ_coef, first, count, n_aux, n_pair)
        sent.append(made)
        got.append([made[0]] + [swapped(made[d], "pair", d) for d in range(1, n_pair)])

    fitted, rest = fitted_first(vir_coef, got[0], pairs, counts)
    parts = coulomb_parts(fitted, rest, got[1], pairs, counts[1] * width, 4)

    occ_pick, occ_energy, vir_energy, _ = lax.optimization_barrier((occ_pick, occ_energy, vir_energy, sent[1][0]))
    own_pairs = lax.axis_index("pair") * pairs + jnp.arange(pairs, dtype=jnp.int32)
    spots = jnp.arange(n_aux, dtype=jnp.int32)
    batch = occ_pick[:n_aux]
    orbitals = jnp.arange(occ_energy.shape[0], dtype=jnp.int32)
    energies = jnp.sum(jnp.where(batch[:, None] == orbitals[None, :], occ_energy[None, :], 0.0), axis=1)
    levels = jnp.sum(jnp.where(own_pairs[:, None] == spots[None, :] % n_half, energies[None, :], 0.0), axis=1)
    inverse = 1.0 / (levels[:, None, None] - vir_energy[None, :, None] - vir_energy[None, None, :])

    chunks = scattered(parts, "aux", 0, bits)
    outs = density_parts(inverse, chunks, n_pair)
    others = [swapped(outs[d], "pair", d) for d in range(1, n_pair)]
    density, energy = closing(outs[0], outs[-1], others, pairs, n_half)
    return (energy, density)


def solution(mesh):
    placed = (P("aux", "pair", None, None), P("pair", None), P("pair"), P(), P(), P(), P(), P())
    return jax.shard_map(
        per_device,
        mesh=mesh,
        in_specs=placed,
        out_specs=(P("aux"), P("pair", None)),
        check_vma=False,
    )
```

```python
import jax
import jax.numpy as jnp
from jax import lax
from jax.experimental import pallas as pl
from jax.experimental.pallas import tpu as pltpu
from jax.sharding import PartitionSpec as P

VMEM = pltpu.VMEM
SMEM = pltpu.SMEM
TILE = 16
SUB = 8
PARAMS = pltpu.CompilerParams(vmem_limit_bytes=48 * 1024 * 1024)


def order(count):
    return sorted(range(1, count), reverse=True)


def swapped(value, axis, mask):
    count = lax.axis_size(axis)
    return lax.ppermute(value, axis, [(source, source ^ mask) for source in range(count)])


def in_hbm(*values):
    return [pltpu.with_memory_space_constraint(value, pltpu.HBM) for value in values]


def whole(count):
    return [pl.BlockSpec(memory_space=VMEM)] * count


def half_blocks(ints, block_ids, block_count, occ_pick, occ_coef, n_aux, n_pair):
    slots, width, _, aux_rows = ints.shape
    nocc = occ_coef.shape[2]
    n_half = n_aux // 2
    pairs = n_half // n_pair
    rows = 2 * pairs * slots * width

    def kernel(count_ref, ids_hbm, pick_hbm, occ_hbm, ints_hbm, *refs):
        outs, (ids_ref, pick_ref, occ_ref, held, small, large) = refs[:n_pair], refs[n_pair:]
        tables = [
            pltpu.make_async_copy(source, target, small.at[at])
            for at, (source, target) in enumerate(((ids_hbm, ids_ref), (pick_hbm, pick_ref), (occ_hbm, occ_ref)))
        ]
        for copy in tables:
            copy.start()
        copies = started(ints_hbm, held, large, slots, width * width)
        for copy in tables:
            copy.wait()
        pair_at = lax.axis_index("pair")
        lane = lax.broadcasted_iota(jnp.int32, (SUB, nocc), 1)
        chosen = []
        for mate in range(n_pair):
            for pair in range(pairs):
                for side in range(2):
                    orbital = pick_ref[(pair_at ^ mate) * pairs + pair + side * n_half]
                    chosen.append(jnp.where(lane == orbital, 1.0, 0.0))
        chosen = jnp.concatenate(chosen, axis=0).astype(jnp.bfloat16)
        row = lax.broadcasted_iota(jnp.int32, (TILE, aux_rows), 0)
        blocks = jnp.full((TILE, aux_rows), -1.0, jnp.float32)
        for slot in range(slots):
            block = jnp.where(slot < count_ref[0], ids_ref[0, slot], -1).astype(jnp.float32)
            blocks = jnp.where(row == slot, block, blocks)
        for out in outs:
            out[pl.ds(rows, TILE), :] = blocks.astype(jnp.bfloat16)
        weights = [slot_weights(chosen, occ_ref[ids_ref[1, slot]]) for slot in range(slots)]
        for slot in range(slots):
            copies[slot].wait()
            halves(weights[slot], held, outs, slot, slots, width, pairs)

    return pl.pallas_call(
        kernel,
        in_specs=[pl.BlockSpec(memory_space=SMEM)] + [pl.BlockSpec(memory_space=pltpu.HBM)] * 4,
        out_specs=whole(n_pair),
        out_shape=[jax.ShapeDtypeStruct((rows + TILE, aux_rows), jnp.bfloat16)] * n_pair,
        scratch_shapes=[
            SMEM((2, slots), jnp.int32),
            SMEM((nocc,), jnp.int32),
            VMEM(occ_coef.shape, jnp.bfloat16),
            VMEM((slots * width * width, aux_rows), jnp.bfloat16),
            pltpu.SemaphoreType.DMA((3,)),
            pltpu.SemaphoreType.DMA((slots,)),
        ],
        compiler_params=PARAMS,
        name="half_blocks",
    )(block_count, *in_hbm(block_ids.T, occ_pick, occ_coef, ints.reshape(-1, aux_rows)))


def started(ints_hbm, held, sems, count, rows):
    copies = []
    for slot in range(count):
        span = pl.ds(slot * rows, rows)
        copies.append(pltpu.make_async_copy(ints_hbm.at[span, :], held.at[span, :], sems.at[slot]))
        copies[-1].start()
    return copies


def slot_weights(chosen, table):
    width = table.shape[0]
    table = jnp.concatenate([table] * (128 // width), axis=0)
    spread = lax.dot_general(chosen, table, (((1,), (1,)), ((), ())), preferred_element_type=jnp.float32)
    spread = jnp.concatenate([spread] * (SUB * width // 128), axis=1)
    row = lax.broadcasted_iota(jnp.int32, spread.shape, 0)
    column = lax.broadcasted_iota(jnp.int32, spread.shape, 1)
    return jnp.where(row % SUB == column // width, spread, 0.0).astype(jnp.bfloat16)


def halves(weights, ints, outs, slot, count, width, pairs):
    depth = SUB * width
    for step in range(width // TILE):
        at = slot * (width // TILE) + step
        made = [
            jnp.dot(weights, ints[pl.ds((2 * at + part) * depth, depth), :], preferred_element_type=jnp.float32)
            for part in range(2)
        ]
        for mate, out in enumerate(outs):
            for orbital in range(2 * pairs):
                source = (mate * 2 * pairs + orbital) * SUB
                both = jnp.concatenate([part[source : source + SUB] for part in made], axis=0)
                out[pl.ds(orbital * count * width + at * TILE, TILE), :] = both.astype(jnp.bfloat16)


def virtual_rows(vir_ref, parts, slots, span):
    rows = []
    for part in parts:
        tail = part[pl.ds(span, TILE), :][:, :128].astype(jnp.float32)
        for slot in range(slots):
            block = tail[slot, 0].astype(jnp.int32)
            row = vir_ref[jnp.maximum(block, 0)]
            rows.append(jnp.where(block >= 0, row, jnp.zeros_like(row)))
    return jnp.concatenate(rows, axis=0).T


def fitted_rows(virtuals, parts, orbital, span):
    blocks = jnp.concatenate([part[pl.ds(orbital * span, span), :] for part in parts], axis=0)
    return jnp.dot(virtuals, blocks, preferred_element_type=jnp.float32)


def fitted_first(vir_coef, parts, pairs, slots):
    aux_rows = parts[0].shape[1]
    width, virtual = vir_coef.shape[1], vir_coef.shape[2]
    span = slots * width

    def kernel(vir_ref, *refs):
        held, fitted_ref, rows_ref = refs[:-2], refs[-2], refs[-1]
        rows_ref[...] = virtual_rows(vir_ref, held, slots, 2 * pairs * span)
        for orbital in range(2 * pairs):
            fitted_ref[orbital] = fitted_rows(rows_ref[...], held, orbital, span)

    return pl.pallas_call(
        kernel,
        in_specs=whole(1 + len(parts)),
        out_specs=pl.BlockSpec(memory_space=VMEM),
        out_shape=jax.ShapeDtypeStruct((2 * pairs, virtual, aux_rows), jnp.float32),
        scratch_shapes=[VMEM((virtual, len(parts) * span), jnp.bfloat16)],
        compiler_params=PARAMS,
        name="fitted_first",
    )(vir_coef, *parts)


def coulomb_parts(fitted, vir_coef, parts, slots, quad):
    pairs = fitted.shape[0] // 2
    virtual, aux_rows = fitted.shape[1:]
    span = slots * vir_coef.shape[1]
    share = virtual // quad

    def kernel(fitted_ref, vir_ref, *refs):
        held, outs, (left_ref, rows_ref) = refs[: len(parts)], refs[len(parts) : -2], refs[-2:]
        place = lax.axis_index("aux") % quad
        rows_ref[...] = virtual_rows(vir_ref, held, slots, 2 * pairs * span)
        for pair in range(pairs):
            sides = []
            for orbital in (2 * pair, 2 * pair + 1):
                total = fitted_ref[orbital] + fitted_rows(rows_ref[...], held, orbital, span)
                sides.append(total.astype(jnp.bfloat16))
            left_ref[...] = sides[0]
            for part, out in enumerate(outs):
                at = pl.multiple_of((place ^ part) * share, share)
                out[pair] = lax.dot_general(
                    left_ref[pl.ds(at, share), :],
                    sides[1],
                    (((1,), (1,)), ((), ())),
                    preferred_element_type=jnp.float32,
                ).astype(jnp.bfloat16)

    return pl.pallas_call(
        kernel,
        in_specs=whole(2 + len(parts)),
        out_specs=whole(quad),
        out_shape=[jax.ShapeDtypeStruct((pairs, share, virtual), jnp.bfloat16)] * quad,
        scratch_shapes=[
            VMEM((virtual, aux_rows), jnp.bfloat16),
            VMEM((virtual, len(parts) * span), jnp.bfloat16),
        ],
        compiler_params=PARAMS,
        name="coulomb_parts",
    )(fitted, vir_coef, *parts)


def density_parts(inverse, chunks, n_pair):
    quad = len(chunks)
    pairs, share, virtual = chunks[0].shape
    rows = virtual // n_pair

    def kernel(inverse_ref, *refs):
        held, own_ref, outs = refs[:quad], refs[quad], refs[quad + 1 : quad + n_pair]
        energy_ref, block_ref, even_ref, odd_ref = refs[quad + n_pair :]
        place = lax.axis_index("aux") % quad
        pair_at = lax.axis_index("pair")
        kind = lax.broadcasted_iota(jnp.int32, (TILE, virtual), 0)
        lane = lax.broadcasted_iota(jnp.int32, (TILE, virtual), 1)
        energies = jnp.zeros((TILE, virtual), jnp.float32)
        totals = [None] * n_pair
        for pair in range(pairs):
            for part in range(quad):
                at = pl.multiple_of((place ^ part) * share, share)
                block_ref[pl.ds(at, share), :] = held[part][pair].astype(jnp.float32)
            block = block_ref[...]
            flipped = block.T
            inverse = inverse_ref[pair]
            energy = jnp.sum(block * (2.0 * block - flipped) * inverse)
            even = ((block + flipped) * inverse).astype(jnp.bfloat16)
            odd = ((block - flipped) * inverse).astype(jnp.bfloat16)
            even_ref[...] = even
            odd_ref[...] = odd
            for part in range(n_pair):
                at = pl.multiple_of((pair_at ^ part) * rows, rows)
                term = 0.5 * jnp.dot(even_ref[pl.ds(at, rows), :], even, preferred_element_type=jnp.float32)
                term -= 1.5 * jnp.dot(odd_ref[pl.ds(at, rows), :], odd, preferred_element_type=jnp.float32)
                totals[part] = term if pair == 0 else totals[part] + term
            energies = jnp.where(lane == pair, energy, energies)
        own_ref[...] = totals[0]
        high = energies.astype(jnp.bfloat16)
        rest = energies - high.astype(jnp.float32)
        middle = rest.astype(jnp.bfloat16)
        low = (rest - middle.astype(jnp.float32)).astype(jnp.bfloat16)
        zero = jnp.zeros_like(high)
        packed = jnp.where(kind == 0, high, jnp.where(kind == 1, middle, jnp.where(kind == 2, low, zero)))
        energy_ref[...] = packed
        for part in range(1, n_pair):
            outs[part - 1][pl.ds(0, rows), :] = totals[part].astype(jnp.bfloat16)
            outs[part - 1][pl.ds(rows, TILE), :] = packed

    return pl.pallas_call(
        kernel,
        in_specs=whole(1 + quad),
        out_specs=whole(n_pair + 1),
        out_shape=[jax.ShapeDtypeStruct((rows, virtual), jnp.float32)]
        + [jax.ShapeDtypeStruct((rows + TILE, virtual), jnp.bfloat16)] * (n_pair - 1)
        + [jax.ShapeDtypeStruct((TILE, virtual), jnp.bfloat16)],
        scratch_shapes=[
            VMEM((virtual, virtual), jnp.float32),
            VMEM((virtual, virtual), jnp.bfloat16),
            VMEM((virtual, virtual), jnp.bfloat16),
        ],
        compiler_params=PARAMS,
        name="density_parts",
    )(inverse, *chunks)


def closing(own, energies, others, pairs, n_half):
    rows, virtual = own.shape

    def kernel(own_ref, energy_ref, *refs):
        held, (density_ref, value_ref) = refs[: len(others)], refs[len(others) :]
        wanted = lax.axis_index("aux") % n_half
        pair_at = lax.axis_index("pair")
        lane = lax.broadcasted_iota(jnp.int32, (TILE, virtual), 1)
        tails = [energy_ref[...]] + [ref[pl.ds(rows, TILE), :] for ref in held]
        found = jnp.zeros((TILE, virtual), jnp.float32)
        for mate, tail in enumerate(tails):
            at = wanted - (pair_at ^ mate) * pairs
            at = jnp.where((at >= 0) & (at < pairs), at, -1)
            found += jnp.where(lane == at, tail.astype(jnp.float32), 0.0)
        value_ref[0] = jnp.sum(found)
        total = own_ref[...]
        for ref in held:
            total += ref[pl.ds(0, rows), :].astype(jnp.float32)
        density_ref[...] = total

    return pl.pallas_call(
        kernel,
        in_specs=whole(2 + len(others)),
        out_specs=[pl.BlockSpec(memory_space=VMEM), pl.BlockSpec(memory_space=SMEM)],
        out_shape=[jax.ShapeDtypeStruct((rows, virtual), jnp.float32), jax.ShapeDtypeStruct((1,), jnp.float32)],
        compiler_params=PARAMS,
        name="closing",
    )(own, energies, *others)


def exchanged(parts, axis, low=0):
    got = [parts[0]] + [None] * (len(parts) - 1)
    for d in order(len(parts)):
        got[d] = swapped(parts[d], axis, d << low)
    return got


def summed(value, axis, low, bits):
    if bits == 0:
        return value
    if bits == 1:
        other = swapped(value, axis, 1 << low)
        return (value.astype(jnp.float32) + other.astype(jnp.float32)).astype(jnp.bfloat16)
    place = (lax.axis_index(axis) >> low) & 3
    share = value.shape[1] // 4
    parts = [lax.dynamic_slice_in_dim(value, (place ^ d) * share, share, 1) for d in range(4)]
    chunks = scattered(parts, axis, low, bits)
    out = jnp.zeros_like(value)
    for d in range(4):
        out = lax.dynamic_update_slice_in_dim(out, chunks[d], (place ^ d) * share, 1)
    return out


def scattered(parts, axis, low, bits):
    total = sum(part.astype(jnp.float32) for part in exchanged(parts, axis, low))
    total = summed(total.astype(jnp.bfloat16), axis, low + 2, bits - 2)
    return exchanged([total] * len(parts), axis, low)


def per_device(
    shell_ints, block_ids, block_count, occ_coef, occ_pick, vir_coef, occ_energy, vir_energy
):
    slots = shell_ints.shape[1]
    n_aux = lax.axis_size("aux")
    n_pair = lax.axis_size("pair")
    n_half = n_aux // 2
    pairs = n_half // n_pair
    bits = n_aux.bit_length() - 1

    ints = jnp.transpose(shell_ints, (1, 2, 3, 0))
    made = half_blocks(ints, block_ids, block_count, occ_pick, occ_coef, n_aux, n_pair)
    got = exchanged(made, "pair")
    near = n_pair // 2
    fitted = fitted_first(vir_coef, got[:near], pairs, slots)
    parts = coulomb_parts(fitted, vir_coef, got[near:], slots, 4)

    occ_pick, occ_energy, vir_energy, _ = lax.optimization_barrier((occ_pick, occ_energy, vir_energy, made[0]))
    own_pairs = lax.axis_index("pair") * pairs + jnp.arange(pairs, dtype=jnp.int32)
    spots = jnp.arange(n_aux, dtype=jnp.int32)
    batch = occ_pick[:n_aux]
    orbitals = jnp.arange(occ_energy.shape[0], dtype=jnp.int32)
    energies = jnp.sum(jnp.where(batch[:, None] == orbitals[None, :], occ_energy[None, :], 0.0), axis=1)
    levels = jnp.sum(jnp.where(own_pairs[:, None] == spots[None, :] % n_half, energies[None, :], 0.0), axis=1)
    inverse = 1.0 / (levels[:, None, None] - vir_energy[None, :, None] - vir_energy[None, None, :])

    chunks = scattered(parts, "aux", 0, bits)
    outs = density_parts(inverse, chunks, n_pair)
    others = exchanged(outs[:-1], "pair")[1:]
    density, energy = closing(outs[0], outs[-1], others, pairs, n_half)
    return (energy, density)


def solution(mesh):
    placed = (P("aux", "pair", None, None), P("pair", None), P("pair"), P(), P(), P(), P(), P())
    return jax.shard_map(
        per_device,
        mesh=mesh,
        in_specs=placed,
        out_specs=(P("aux"), P("pair", None)),
        check_vma=False,
    )
```

```python
import jax
import jax.numpy as jnp
from jax import lax
from jax.experimental import pallas as pl
from jax.experimental.pallas import tpu as pltpu
from jax.sharding import PartitionSpec as P

VMEM = pltpu.VMEM
SMEM = pltpu.SMEM
TILE = 16
SUB = 8
MARK = 128
PARAMS = pltpu.CompilerParams(vmem_limit_bytes=48 * 1024 * 1024)


def order(count):
    return sorted(range(1, count), reverse=True)


def swapped(value, axis, mask):
    count = lax.axis_size(axis)
    return lax.ppermute(value, axis, [(source, source ^ mask) for source in range(count)])


def in_hbm(*values):
    return [pltpu.with_memory_space_constraint(value, pltpu.HBM) for value in values]


def whole(count):
    return [pl.BlockSpec(memory_space=VMEM)] * count


def half_first(ints, block_ids, occ_pick, occ_coef, count, n_aux, n_pair):
    slots, width, _, aux_rows = ints.shape
    blocks, _, nocc = occ_coef.shape
    n_half = n_aux // 2
    pairs = n_half // n_pair
    rows = 2 * pairs * count * width

    def kernel(ids_hbm, pick_hbm, occ_hbm, ints_hbm, *refs):
        outs, chosen_ref, tables_ref = refs[:n_pair], refs[n_pair], refs[n_pair + 1]
        ids_ref, pick_ref, occ_ref, held, small, large = refs[n_pair + 2 :]
        tables = [
            pltpu.make_async_copy(source, target, small.at[at])
            for at, (source, target) in enumerate(((ids_hbm, ids_ref), (pick_hbm, pick_ref), (occ_hbm, occ_ref)))
        ]
        for copy in tables:
            copy.start()
        copies = started(ints_hbm, held, large, 0, count, width * width)
        for copy in tables:
            copy.wait()
        pair_at = lax.axis_index("pair")
        lane = lax.broadcasted_iota(jnp.int32, (SUB, nocc), 1)
        chosen = []
        for mate in range(n_pair):
            for pair in range(pairs):
                for side in range(2):
                    orbital = pick_ref[(pair_at ^ mate) * pairs + pair + side * n_half]
                    chosen.append(jnp.where(lane == orbital, 1.0, 0.0))
        chosen = jnp.concatenate(chosen, axis=0).astype(jnp.bfloat16)
        weights = [slot_weights(chosen, occ_ref[ids_ref[1, slot]]) for slot in range(count)]
        row = lax.broadcasted_iota(jnp.int32, (TILE, aux_rows), 0)
        blocks = jnp.zeros((TILE, aux_rows), jnp.float32)
        for slot in range(slots):
            blocks = jnp.where(row == slot, ids_ref[0, slot].astype(jnp.float32), blocks)
        for out in outs:
            out[pl.ds(rows, TILE), :] = blocks.astype(jnp.bfloat16)
        chosen_ref[...] = chosen
        for slot in range(count, slots):
            tables_ref[slot - count] = occ_ref[ids_ref[1, slot]]
        for slot in range(count):
            copies[slot].wait()
            halves(weights[slot], held, outs, slot, count, width, pairs)

    return pl.pallas_call(
        kernel,
        in_specs=[pl.BlockSpec(memory_space=pltpu.HBM)] * 4,
        out_specs=whole(n_pair + 2),
        out_shape=[jax.ShapeDtypeStruct((rows + TILE, aux_rows), jnp.bfloat16)] * n_pair
        + [
            jax.ShapeDtypeStruct((n_aux * SUB, nocc), jnp.bfloat16),
            jax.ShapeDtypeStruct((slots - count, width, nocc), jnp.bfloat16),
        ],
        scratch_shapes=[
            SMEM((2, slots), jnp.int32),
            SMEM((nocc,), jnp.int32),
            VMEM(occ_coef.shape, jnp.bfloat16),
            VMEM((count * width * width, aux_rows), jnp.bfloat16),
            pltpu.SemaphoreType.DMA((3,)),
            pltpu.SemaphoreType.DMA((count,)),
        ],
        compiler_params=PARAMS,
        name="half_first",
    )(*in_hbm(block_ids.T, occ_pick, occ_coef, ints.reshape(-1, aux_rows)))


def started(ints_hbm, held, sems, first, count, rows):
    copies = []
    for slot in range(count):
        source = ints_hbm.at[pl.ds((first + slot) * rows, rows), :]
        copies.append(pltpu.make_async_copy(source, held.at[pl.ds(slot * rows, rows), :], sems.at[slot]))
        copies[-1].start()
    return copies


def slot_weights(chosen, table):
    width = table.shape[0]
    table = jnp.concatenate([table] * (128 // width), axis=0)
    spread = lax.dot_general(chosen, table, (((1,), (1,)), ((), ())), preferred_element_type=jnp.float32)
    spread = jnp.concatenate([spread] * (SUB * width // 128), axis=1)
    row = lax.broadcasted_iota(jnp.int32, spread.shape, 0)
    column = lax.broadcasted_iota(jnp.int32, spread.shape, 1)
    return jnp.where(row % SUB == column // width, spread, 0.0).astype(jnp.bfloat16)


def halves(weights, ints, outs, slot, count, width, pairs):
    depth = SUB * width
    for step in range(width // TILE):
        at = slot * (width // TILE) + step
        made = [
            jnp.dot(weights, ints[pl.ds((2 * at + part) * depth, depth), :], preferred_element_type=jnp.float32)
            for part in range(2)
        ]
        for mate, out in enumerate(outs):
            for orbital in range(2 * pairs):
                source = (mate * 2 * pairs + orbital) * SUB
                both = jnp.concatenate([part[source : source + SUB] for part in made], axis=0)
                out[pl.ds(orbital * count * width + at * TILE, TILE), :] = both.astype(jnp.bfloat16)


def half_rest(ints, block_count, chosen, tables, n_pair, pairs):
    slots, width, _, aux_rows = ints.shape
    count = tables.shape[0]

    def kernel(count_ref, chosen_ref, tables_ref, ints_hbm, *refs):
        outs, (held, large) = refs[:n_pair], refs[n_pair:]
        copies = started(ints_hbm, held, large, slots - count, count, width * width)
        weights = [slot_weights(chosen_ref[...], tables_ref[slot]) for slot in range(count)]
        for slot in range(count):
            copies[slot].wait()
            halves(weights[slot], held, outs, slot, count, width, pairs)
        live = count_ref[0]
        mark = jnp.full((TILE, aux_rows), (MARK * (live + 1)).astype(jnp.float32), jnp.float32).astype(jnp.bfloat16)
        for out in outs:
            spot = pl.ds((count - 1) * width, TILE)
            out[spot, :] = jnp.where(live < slots, mark, out[spot, :])

    return pl.pallas_call(
        kernel,
        in_specs=[pl.BlockSpec(memory_space=SMEM)] + whole(2) + [pl.BlockSpec(memory_space=pltpu.HBM)],
        out_specs=whole(n_pair),
        out_shape=[jax.ShapeDtypeStruct((2 * pairs * count * width, aux_rows), jnp.bfloat16)] * n_pair,
        scratch_shapes=[
            VMEM((count * width * width, aux_rows), jnp.bfloat16),
            pltpu.SemaphoreType.DMA((count,)),
        ],
        compiler_params=PARAMS,
        name="half_rest",
    )(block_count, chosen, tables, *in_hbm(ints.reshape(-1, aux_rows)))


def fitted_first(vir_coef, parts, pairs, counts):
    aux_rows = parts[0].shape[1]
    width, virtual = vir_coef.shape[1], vir_coef.shape[2]
    span = counts[0] * width

    def kernel(vir_ref, *refs):
        held, (fitted_ref, rest_ref, own_ref) = refs[: len(parts)], refs[len(parts) :]
        first, rest = [], []
        for part in held:
            tail = part[pl.ds(2 * pairs * span, TILE), :][:, :128].astype(jnp.float32)
            found = [vir_ref[tail[slot, 0].astype(jnp.int32)] for slot in range(sum(counts))]
            first.append(found[0])
            rest += found[1:]
        own_ref[...] = jnp.concatenate(first, axis=0).T
        rest_ref[...] = jnp.concatenate(rest, axis=0).T
        for orbital in range(2 * pairs):
            blocks = jnp.concatenate([part[pl.ds(orbital * span, width), :] for part in held], axis=0)
            fitted_ref[orbital] = jnp.dot(own_ref[...], blocks, preferred_element_type=jnp.float32)

    return pl.pallas_call(
        kernel,
        in_specs=whole(1 + len(parts)),
        out_specs=whole(2),
        out_shape=[
            jax.ShapeDtypeStruct((2 * pairs, virtual, aux_rows), jnp.float32),
            jax.ShapeDtypeStruct((virtual, len(parts) * (sum(counts) - 1) * width), jnp.bfloat16),
        ],
        scratch_shapes=[VMEM((virtual, len(parts) * width), jnp.bfloat16)],
        compiler_params=PARAMS,
        name="fitted_first",
    )(vir_coef, *parts)


def coulomb_parts(fitted, rest, first, later, pairs, counts, quad):
    n_pair = len(first)
    slots = sum(counts)
    virtual, aux_rows = fitted.shape[1:]
    width = rest.shape[1] // (n_pair * (slots - 1))
    share = virtual // quad

    def kernel(fitted_ref, rest_ref, *refs):
        held, outs, block_ref = (refs[:n_pair], refs[n_pair : 2 * n_pair]), refs[2 * n_pair : -1], refs[-1]
        place = lax.axis_index("aux") % quad
        live = []
        for part in held[1]:
            mark = part[pl.ds((counts[1] - 1) * width, TILE), :][:, :128].astype(jnp.float32)[0, 0]
            live.append(jnp.where(mark < MARK, slots, (mark * (1.0 / MARK)).astype(jnp.int32) - 1))
        for pair in range(pairs):
            sides = []
            for orbital in (2 * pair, 2 * pair + 1):
                blocks = []
                for group in range(n_pair):
                    for slot in range(1, slots):
                        chunk = int(slot >= counts[0])
                        at = (orbital * counts[chunk] + slot - chunk * counts[0]) * width
                        block = held[chunk][group][pl.ds(at, width), :]
                        blocks.append(jnp.where(slot < live[group], block, jnp.zeros_like(block)))
                total = jnp.dot(rest_ref[...], jnp.concatenate(blocks, axis=0), preferred_element_type=jnp.float32)
                sides.append((fitted_ref[orbital] + total).astype(jnp.bfloat16))
            block = lax.dot_general(*sides, (((1,), (1,)), ((), ())), preferred_element_type=jnp.float32)
            block_ref[...] = block.astype(jnp.bfloat16)
            for part, out in enumerate(outs):
                at = pl.multiple_of((place ^ part) * share, share)
                out[pair] = block_ref[pl.ds(at, share), :]

    return pl.pallas_call(
        kernel,
        in_specs=whole(2 + 2 * n_pair),
        out_specs=whole(quad),
        out_shape=[jax.ShapeDtypeStruct((pairs, share, virtual), jnp.bfloat16)] * quad,
        scratch_shapes=[VMEM((virtual, virtual), jnp.bfloat16)],
        compiler_params=PARAMS,
        name="coulomb_parts",
    )(fitted, rest, *first, *later)


def density_parts(inverse, chunks, n_pair):
    quad = len(chunks)
    pairs, share, virtual = chunks[0].shape
    rows = virtual // n_pair

    def kernel(inverse_ref, *refs):
        held, own_ref, outs = refs[:quad], refs[quad], refs[quad + 1 : quad + n_pair]
        energy_ref, block_ref, total_ref = refs[quad + n_pair :]
        place = lax.axis_index("aux") % quad
        pair_at = lax.axis_index("pair")
        lane = lax.broadcasted_iota(jnp.int32, (1, virtual), 1)
        energies = []
        totals = [None] * n_pair
        for pair in range(pairs):
            for part in range(quad):
                at = pl.multiple_of((place ^ part) * share, share)
                block_ref[pl.ds(at, share), :] = held[part][pair]
            block = block_ref[...].astype(jnp.float32)
            flipped = block_ref[...].T.astype(jnp.float32)
            inverse = inverse_ref[pair]
            energy = jnp.sum(block * (2.0 * block - flipped) * inverse)
            even = ((block + flipped) * inverse).astype(jnp.bfloat16)
            odd = ((block - flipped) * inverse).astype(jnp.bfloat16)
            term = 0.5 * jnp.dot(even, even, preferred_element_type=jnp.float32)
            term -= 1.5 * jnp.dot(odd, odd, preferred_element_type=jnp.float32)
            total_ref[...] = term if pair == 0 else total_ref[...] + term
        for part in range(n_pair):
            totals[part] = total_ref[pl.ds(pl.multiple_of((pair_at ^ part) * rows, rows), rows), :]
            energies.append(energy)
        own_ref[...] = totals[0]
        energy_ref[...] = jnp.zeros_like(energy_ref)
        for pair, energy in enumerate(energies):
            energy_ref[...] = jnp.where(lane == pair, energy, energy_ref[...])
        for part in range(1, n_pair):
            outs[part - 1][...] = totals[part].astype(jnp.bfloat16)
            first = (pair_at ^ part) * rows
            last = totals[part][rows - TILE :]
            row = lax.broadcasted_iota(jnp.int32, (TILE, virtual), 0)
            corner = jnp.zeros((1, virtual), jnp.float32)
            for pair, energy in enumerate(energies):
                rest = jnp.full((1, virtual), energy, jnp.float32)
                for at in range(3):
                    piece = rest.astype(jnp.bfloat16).astype(jnp.float32)
                    corner = jnp.where(lane == first + 3 * pair + at, piece, corner)
                    rest = rest - piece
            inside = (lane >= first) & (lane < first + 3 * pairs) & (row == TILE - 1)
            outs[part - 1][pl.ds(rows - TILE, TILE), :] = jnp.where(inside, corner, last).astype(jnp.bfloat16)

    return pl.pallas_call(
        kernel,
        in_specs=whole(1 + quad),
        out_specs=whole(n_pair + 1),
        out_shape=[jax.ShapeDtypeStruct((rows, virtual), jnp.float32)]
        + [jax.ShapeDtypeStruct((rows, virtual), jnp.bfloat16)] * (n_pair - 1)
        + [jax.ShapeDtypeStruct((1, virtual), jnp.float32)],
        scratch_shapes=[
            VMEM((virtual, virtual), jnp.bfloat16),
            VMEM((virtual, virtual), jnp.float32),
        ],
        compiler_params=PARAMS,
        name="density_parts",
    )(inverse, *chunks)


def closing(own, energies, others, pairs, n_half):
    rows, virtual = own.shape

    def kernel(own_ref, energy_ref, *refs):
        held, (density_ref, value_ref) = refs[: len(others)], refs[len(others) :]
        wanted = lax.axis_index("aux") % n_half
        pair_at = lax.axis_index("pair")
        lane = lax.broadcasted_iota(jnp.int32, (1, virtual), 1)
        first = pair_at * rows
        found = jnp.zeros((1, virtual), jnp.float32)
        total = own_ref[...]
        for mate in range(len(held) + 1):
            at = wanted - (pair_at ^ mate) * pairs
            here = (at >= 0) & (at < pairs)
            if mate == 0:
                found += jnp.where(here & (lane == at), energy_ref[...], 0.0)
            else:
                part = held[mate - 1][...].astype(jnp.float32)
                spot = lane - first - 3 * at
                found += jnp.where(here & (spot >= 0) & (spot < 3), part[rows - 1 :], 0.0)
                total += part
        value_ref[0] = jnp.sum(found)
        density_ref[...] = total
        head = -(-3 * pairs // TILE) * TILE
        top = total[:head]
        wide = lax.broadcasted_iota(jnp.int32, (head, virtual), 1)
        row = lax.broadcasted_iota(jnp.int32, (head, virtual), 0)
        column = jnp.sum(jnp.where(wide == first + rows - 1, top, 0.0), axis=1, keepdims=True)
        turned = jnp.sum(jnp.where(wide == first + row, column, 0.0), axis=0, keepdims=True)
        last = total[rows - SUB :]
        inside = (lane >= first) & (lane < first + 3 * pairs)
        inside = inside & (lax.broadcasted_iota(jnp.int32, (SUB, virtual), 0) == SUB - 1)
        density_ref[pl.ds(rows - SUB, SUB), :] = jnp.where(inside, turned, last)

    return pl.pallas_call(
        kernel,
        in_specs=whole(2 + len(others)),
        out_specs=[pl.BlockSpec(memory_space=VMEM), pl.BlockSpec(memory_space=SMEM)],
        out_shape=[jax.ShapeDtypeStruct((rows, virtual), jnp.float32), jax.ShapeDtypeStruct((1,), jnp.float32)],
        compiler_params=PARAMS,
        name="closing",
    )(own, energies, *others)


def exchanged(parts, axis, low=0):
    got = [parts[0]] + [None] * (len(parts) - 1)
    for d in order(len(parts)):
        if parts[d] is not None:
            got[d] = swapped(parts[d], axis, d << low)
    return got


def summed(value, axis, low, bits):
    if bits == 0:
        return value
    if bits == 1:
        other = swapped(value, axis, 1 << low)
        return (value.astype(jnp.float32) + other.astype(jnp.float32)).astype(jnp.bfloat16)
    place = (lax.axis_index(axis) >> low) & 3
    share = value.shape[1] // 4
    parts = [lax.dynamic_slice_in_dim(value, (place ^ d) * share, share, 1) for d in range(4)]
    chunks = scattered(parts, axis, low, bits)
    out = jnp.zeros_like(value)
    for d in range(4):
        out = lax.dynamic_update_slice_in_dim(out, chunks[d], (place ^ d) * share, 1)
    return out


def scattered(parts, axis, low, bits):
    total = sum(part.astype(jnp.float32) for part in exchanged(parts, axis, low))
    total = summed(total.astype(jnp.bfloat16), axis, low + 2, bits - 2)
    return exchanged([total] * len(parts), axis, low)


def per_device(
    shell_ints, block_ids, block_count, occ_coef, occ_pick, vir_coef, occ_energy, vir_energy
):
    _, slots, width, _ = shell_ints.shape
    n_aux = lax.axis_size("aux")
    n_pair = lax.axis_size("pair")
    n_half = n_aux // 2
    pairs = n_half // n_pair
    bits = n_aux.bit_length() - 1

    ints = jnp.transpose(shell_ints, (1, 2, 3, 0))
    counts = (slots // 2, slots - slots // 2)
    *first, chosen, tables = half_first(
        ints, block_ids, occ_pick, occ_coef, counts[0], n_aux, n_pair
    )
    block_count, _ = lax.optimization_barrier((block_count, first[0]))
    later = list(half_rest(ints, block_count, chosen, tables, n_pair, pairs))
    got = [exchanged(first, "pair"), exchanged(later, "pair")]

    fitted, rest = fitted_first(vir_coef, got[0], pairs, counts)
    parts = coulomb_parts(fitted, rest, got[0], got[1], pairs, counts, 4)

    occ_pick, occ_energy, vir_energy, _ = lax.optimization_barrier((occ_pick, occ_energy, vir_energy, later[0]))
    own_pairs = lax.axis_index("pair") * pairs + jnp.arange(pairs, dtype=jnp.int32)
    spots = jnp.arange(n_aux, dtype=jnp.int32)
    batch = occ_pick[:n_aux]
    orbitals = jnp.arange(occ_energy.shape[0], dtype=jnp.int32)
    energies = jnp.sum(jnp.where(batch[:, None] == orbitals[None, :], occ_energy[None, :], 0.0), axis=1)
    levels = jnp.sum(jnp.where(own_pairs[:, None] == spots[None, :] % n_half, energies[None, :], 0.0), axis=1)
    inverse = 1.0 / (levels[:, None, None] - vir_energy[None, :, None] - vir_energy[None, None, :])

    chunks = scattered(parts, "aux", 0, bits)
    outs = density_parts(inverse, chunks, n_pair)
    others = exchanged(outs[:-1], "pair")[1:]
    density, energy = closing(outs[0], outs[-1], others, pairs, n_half)
    return (energy, density)


def solution(mesh):
    placed = (P("aux", "pair", None, None), P("pair", None), P("pair"), P(), P(), P(), P(), P())
    return jax.shard_map(
        per_device,
        mesh=mesh,
        in_specs=placed,
        out_specs=(P("aux"), P("pair", None)),
        check_vma=False,
    )
```

```python
import jax
import jax.numpy as jnp
from jax import lax
from jax.experimental import pallas as pl
from jax.experimental.pallas import tpu as pltpu
from jax.sharding import PartitionSpec as P

VMEM = pltpu.VMEM
SMEM = pltpu.SMEM
TILE = 16
SUB = 8
MARK = 128
PARAMS = pltpu.CompilerParams(vmem_limit_bytes=48 * 1024 * 1024)


PAIR_ORDER = (2, 3, 1)
SUM_ORDER = (3, 1, 2)
GATHER_ORDER = (3, 1, 2)
ROW_ORDER = (2, 1, 3)


def swapped(value, axis, mask):
    count = lax.axis_size(axis)
    return lax.ppermute(value, axis, [(source, source ^ mask) for source in range(count)])


def in_hbm(*values):
    return [pltpu.with_memory_space_constraint(value, pltpu.HBM) for value in values]


def whole(count):
    return [pl.BlockSpec(memory_space=VMEM)] * count


def half_first(ints, block_ids, occ_pick, occ_coef, count, n_aux, n_pair):
    slots, width, _, aux_rows = ints.shape
    blocks, _, nocc = occ_coef.shape
    n_half = n_aux // 2
    pairs = n_half // n_pair
    rows = 2 * pairs * count * width

    def kernel(ids_hbm, pick_hbm, occ_hbm, ints_hbm, *refs):
        outs, chosen_ref, tables_ref = refs[:n_pair], refs[n_pair], refs[n_pair + 1]
        ids_ref, pick_ref, occ_ref, held, small, large = refs[n_pair + 2 :]
        tables = [
            pltpu.make_async_copy(source, target, small.at[at])
            for at, (source, target) in enumerate(((ids_hbm, ids_ref), (pick_hbm, pick_ref), (occ_hbm, occ_ref)))
        ]
        for copy in tables:
            copy.start()
        copies = started(ints_hbm, held, large, 0, count, width * width)
        for copy in tables:
            copy.wait()
        pair_at = lax.axis_index("pair")
        lane = lax.broadcasted_iota(jnp.int32, (SUB, nocc), 1)
        chosen = []
        for mate in range(n_pair):
            for pair in range(pairs):
                for side in range(2):
                    orbital = pick_ref[(pair_at ^ mate) * pairs + pair + side * n_half]
                    chosen.append(jnp.where(lane == orbital, 1.0, 0.0))
        chosen = jnp.concatenate(chosen, axis=0).astype(jnp.bfloat16)
        weights = [slot_weights(chosen, occ_ref[ids_ref[1, slot]]) for slot in range(count)]
        row = lax.broadcasted_iota(jnp.int32, (TILE, aux_rows), 0)
        blocks = jnp.zeros((TILE, aux_rows), jnp.float32)
        for slot in range(slots):
            blocks = jnp.where(row == slot, ids_ref[0, slot].astype(jnp.float32), blocks)
        for out in outs:
            out[pl.ds(rows, TILE), :] = blocks.astype(jnp.bfloat16)
        chosen_ref[...] = chosen
        for slot in range(count, slots):
            tables_ref[slot - count] = occ_ref[ids_ref[1, slot]]
        for slot in range(count):
            copies[slot].wait()
            halves(weights[slot], held, outs, slot, count, width, pairs)

    return pl.pallas_call(
        kernel,
        in_specs=[pl.BlockSpec(memory_space=pltpu.HBM)] * 4,
        out_specs=whole(n_pair + 2),
        out_shape=[jax.ShapeDtypeStruct((rows + TILE, aux_rows), jnp.bfloat16)] * n_pair
        + [
            jax.ShapeDtypeStruct((n_aux * SUB, nocc), jnp.bfloat16),
            jax.ShapeDtypeStruct((slots - count, width, nocc), jnp.bfloat16),
        ],
        scratch_shapes=[
            SMEM((2, slots), jnp.int32),
            SMEM((nocc,), jnp.int32),
            VMEM(occ_coef.shape, jnp.bfloat16),
            VMEM((count * width * width, aux_rows), jnp.bfloat16),
            pltpu.SemaphoreType.DMA((3,)),
            pltpu.SemaphoreType.DMA((count,)),
        ],
        compiler_params=PARAMS,
        name="half_first",
    )(*in_hbm(block_ids.T, occ_pick, occ_coef, ints.reshape(-1, aux_rows)))


def started(ints_hbm, held, sems, first, count, rows):
    copies = []
    for slot in range(count):
        source = ints_hbm.at[pl.ds((first + slot) * rows, rows), :]
        copies.append(pltpu.make_async_copy(source, held.at[pl.ds(slot * rows, rows), :], sems.at[slot]))
        copies[-1].start()
    return copies


def slot_weights(chosen, table):
    width = table.shape[0]
    table = jnp.concatenate([table] * (128 // width), axis=0)
    spread = lax.dot_general(chosen, table, (((1,), (1,)), ((), ())), preferred_element_type=jnp.float32)
    spread = jnp.concatenate([spread] * (SUB * width // 128), axis=1)
    row = lax.broadcasted_iota(jnp.int32, spread.shape, 0)
    column = lax.broadcasted_iota(jnp.int32, spread.shape, 1)
    return jnp.where(row % SUB == column // width, spread, 0.0).astype(jnp.bfloat16)


def halves(weights, ints, outs, slot, count, width, pairs):
    depth = SUB * width
    for step in range(width // TILE):
        at = slot * (width // TILE) + step
        made = [
            jnp.dot(weights, ints[pl.ds((2 * at + part) * depth, depth), :], preferred_element_type=jnp.float32)
            for part in range(2)
        ]
        for mate, out in enumerate(outs):
            for orbital in range(2 * pairs):
                source = (mate * 2 * pairs + orbital) * SUB
                both = jnp.concatenate([part[source : source + SUB] for part in made], axis=0)
                out[pl.ds(orbital * count * width + at * TILE, TILE), :] = both.astype(jnp.bfloat16)


def half_rest(ints, block_count, chosen, tables, n_pair, pairs):
    slots, width, _, aux_rows = ints.shape
    count = tables.shape[0]

    def kernel(count_ref, chosen_ref, tables_ref, ints_hbm, *refs):
        outs, (held, large) = refs[:n_pair], refs[n_pair:]
        copies = started(ints_hbm, held, large, slots - count, count, width * width)
        weights = [slot_weights(chosen_ref[...], tables_ref[slot]) for slot in range(count)]
        for slot in range(count):
            copies[slot].wait()
            halves(weights[slot], held, outs, slot, count, width, pairs)
        live = count_ref[0]
        mark = jnp.full((TILE, aux_rows), (MARK * (live + 1)).astype(jnp.float32), jnp.float32).astype(jnp.bfloat16)
        for out in outs:
            spot = pl.ds((count - 1) * width, TILE)
            out[spot, :] = jnp.where(live < slots, mark, out[spot, :])

    return pl.pallas_call(
        kernel,
        in_specs=[pl.BlockSpec(memory_space=SMEM)] + whole(2) + [pl.BlockSpec(memory_space=pltpu.HBM)],
        out_specs=whole(n_pair),
        out_shape=[jax.ShapeDtypeStruct((2 * pairs * count * width, aux_rows), jnp.bfloat16)] * n_pair,
        scratch_shapes=[
            VMEM((count * width * width, aux_rows), jnp.bfloat16),
            pltpu.SemaphoreType.DMA((count,)),
        ],
        compiler_params=PARAMS,
        name="half_rest",
    )(block_count, chosen, tables, *in_hbm(ints.reshape(-1, aux_rows)))


def fitted_first(vir_coef, parts, pairs, counts):
    aux_rows = parts[0].shape[1]
    width, virtual = vir_coef.shape[1], vir_coef.shape[2]
    span = counts[0] * width

    def kernel(vir_ref, *refs):
        held, (fitted_ref, rest_ref, own_ref) = refs[: len(parts)], refs[len(parts) :]
        first, rest = [], []
        for part in held:
            tail = part[pl.ds(2 * pairs * span, TILE), :][:, :128].astype(jnp.float32)
            found = [vir_ref[tail[slot, 0].astype(jnp.int32)] for slot in range(sum(counts))]
            first.append(found[0])
            rest += found[1:]
        own_ref[...] = jnp.concatenate(first, axis=0).T
        rest_ref[...] = jnp.concatenate(rest, axis=0).T
        for orbital in range(2 * pairs):
            blocks = jnp.concatenate([part[pl.ds(orbital * span, width), :] for part in held], axis=0)
            fitted_ref[orbital] = jnp.dot(own_ref[...], blocks, preferred_element_type=jnp.float32)

    return pl.pallas_call(
        kernel,
        in_specs=whole(1 + len(parts)),
        out_specs=whole(2),
        out_shape=[
            jax.ShapeDtypeStruct((2 * pairs, virtual, aux_rows), jnp.float32),
            jax.ShapeDtypeStruct((virtual, len(parts) * (sum(counts) - 1) * width), jnp.bfloat16),
        ],
        scratch_shapes=[VMEM((virtual, len(parts) * width), jnp.bfloat16)],
        compiler_params=PARAMS,
        name="fitted_first",
    )(vir_coef, *parts)


def coulomb_parts(fitted, rest, first, later, pairs, counts, quad):
    n_pair = len(first)
    slots = sum(counts)
    virtual, aux_rows = fitted.shape[1:]
    width = rest.shape[1] // (n_pair * (slots - 1))
    share = virtual // quad

    def kernel(fitted_ref, rest_ref, *refs):
        held, outs, block_ref = (refs[:n_pair], refs[n_pair : 2 * n_pair]), refs[2 * n_pair : -1], refs[-1]
        place = lax.axis_index("aux") % quad
        live = []
        for part in held[1]:
            mark = part[pl.ds((counts[1] - 1) * width, TILE), :][:, :128].astype(jnp.float32)[0, 0]
            live.append(jnp.where(mark < MARK, slots, (mark * (1.0 / MARK)).astype(jnp.int32) - 1))
        for pair in range(pairs):
            sides = []
            for orbital in (2 * pair, 2 * pair + 1):
                blocks = []
                for group in range(n_pair):
                    for slot in range(1, slots):
                        chunk = int(slot >= counts[0])
                        at = (orbital * counts[chunk] + slot - chunk * counts[0]) * width
                        block = held[chunk][group][pl.ds(at, width), :]
                        blocks.append(jnp.where(slot < live[group], block, jnp.zeros_like(block)))
                total = jnp.dot(rest_ref[...], jnp.concatenate(blocks, axis=0), preferred_element_type=jnp.float32)
                sides.append((fitted_ref[orbital] + total).astype(jnp.bfloat16))
            block = lax.dot_general(*sides, (((1,), (1,)), ((), ())), preferred_element_type=jnp.float32)
            block_ref[...] = block.astype(jnp.bfloat16)
            for part, out in enumerate(outs):
                at = pl.multiple_of((place ^ part) * share, share)
                out[pair] = block_ref[pl.ds(at, share), :]

    return pl.pallas_call(
        kernel,
        in_specs=whole(2 + 2 * n_pair),
        out_specs=whole(quad),
        out_shape=[jax.ShapeDtypeStruct((pairs, share, virtual), jnp.bfloat16)] * quad,
        scratch_shapes=[VMEM((virtual, virtual), jnp.bfloat16)],
        compiler_params=PARAMS,
        name="coulomb_parts",
    )(fitted, rest, *first, *later)


def density_parts(inverse, chunks, n_pair):
    quad = len(chunks)
    pairs, share, virtual = chunks[0].shape
    rows = virtual // n_pair

    def kernel(inverse_ref, *refs):
        held, own_ref, outs = refs[:quad], refs[quad], refs[quad + 1 : quad + n_pair]
        energy_ref, block_ref, total_ref = refs[quad + n_pair :]
        place = lax.axis_index("aux") % quad
        pair_at = lax.axis_index("pair")
        lane = lax.broadcasted_iota(jnp.int32, (1, virtual), 1)
        energies = []
        totals = [None] * n_pair
        for pair in range(pairs):
            for part, chunk in zip((0, *GATHER_ORDER), held):
                at = pl.multiple_of((place ^ part) * share, share)
                block_ref[pl.ds(at, share), :] = chunk[pair]
            block = block_ref[...].astype(jnp.float32)
            flipped = block_ref[...].T.astype(jnp.float32)
            inverse = inverse_ref[pair]
            energy = jnp.sum(block * (2.0 * block - flipped) * inverse)
            even = ((block + flipped) * inverse).astype(jnp.bfloat16)
            odd = ((block - flipped) * (inverse * 3.0**0.5)).astype(jnp.bfloat16)
            left = jnp.concatenate([even, odd], axis=1)
            right = jnp.concatenate([even, -odd], axis=0)
            term = 0.5 * jnp.dot(left, right, preferred_element_type=jnp.float32)
            total_ref[...] = term if pair == 0 else total_ref[...] + term
        for part in range(n_pair):
            totals[part] = total_ref[pl.ds(pl.multiple_of((pair_at ^ part) * rows, rows), rows), :]
            energies.append(energy)
        own_ref[...] = totals[0]
        energy_ref[...] = jnp.zeros_like(energy_ref)
        for pair, energy in enumerate(energies):
            energy_ref[...] = jnp.where(lane == pair, energy, energy_ref[...])
        for part in range(1, n_pair):
            outs[part - 1][...] = totals[part].astype(jnp.bfloat16)
            first = (pair_at ^ part) * rows
            last = totals[part][rows - TILE :]
            row = lax.broadcasted_iota(jnp.int32, (TILE, virtual), 0)
            corner = jnp.zeros((1, virtual), jnp.float32)
            for pair, energy in enumerate(energies):
                rest = jnp.full((1, virtual), energy, jnp.float32)
                for at in range(3):
                    piece = rest.astype(jnp.bfloat16).astype(jnp.float32)
                    corner = jnp.where(lane == first + 3 * pair + at, piece, corner)
                    rest = rest - piece
            inside = (lane >= first) & (lane < first + 3 * pairs) & (row == TILE - 1)
            outs[part - 1][pl.ds(rows - TILE, TILE), :] = jnp.where(inside, corner, last).astype(jnp.bfloat16)

    return pl.pallas_call(
        kernel,
        in_specs=whole(1 + quad),
        out_specs=whole(n_pair + 1),
        out_shape=[jax.ShapeDtypeStruct((rows, virtual), jnp.float32)]
        + [jax.ShapeDtypeStruct((rows, virtual), jnp.bfloat16)] * (n_pair - 1)
        + [jax.ShapeDtypeStruct((1, virtual), jnp.float32)],
        scratch_shapes=[
            VMEM((virtual, virtual), jnp.bfloat16),
            VMEM((virtual, virtual), jnp.float32),
        ],
        compiler_params=PARAMS,
        name="density_parts",
    )(inverse, *chunks)


def closing(own, energies, others, pairs, n_half):
    rows, virtual = own.shape

    def kernel(own_ref, energy_ref, *refs):
        held, (density_ref, value_ref) = refs[: len(others)], refs[len(others) :]
        wanted = lax.axis_index("aux") % n_half
        pair_at = lax.axis_index("pair")
        lane = lax.broadcasted_iota(jnp.int32, (1, virtual), 1)
        first = pair_at * rows
        found = jnp.zeros((1, virtual), jnp.float32)
        total = own_ref[...]
        for mate, ref in zip((0, *ROW_ORDER), (None, *held)):
            at = wanted - (pair_at ^ mate) * pairs
            here = (at >= 0) & (at < pairs)
            if mate == 0:
                found += jnp.where(here & (lane == at), energy_ref[...], 0.0)
            else:
                part = ref[...].astype(jnp.float32)
                spot = lane - first - 3 * at
                found += jnp.where(here & (spot >= 0) & (spot < 3), part[rows - 1 :], 0.0)
                total += part
        value_ref[0] = jnp.sum(found)
        density_ref[...] = total
        head = -(-3 * pairs // TILE) * TILE
        top = total[:head]
        wide = lax.broadcasted_iota(jnp.int32, (head, virtual), 1)
        row = lax.broadcasted_iota(jnp.int32, (head, virtual), 0)
        column = jnp.sum(jnp.where(wide == first + rows - 1, top, 0.0), axis=1, keepdims=True)
        turned = jnp.sum(jnp.where(wide == first + row, column, 0.0), axis=0, keepdims=True)
        last = total[rows - SUB :]
        inside = (lane >= first) & (lane < first + 3 * pairs)
        inside = inside & (lax.broadcasted_iota(jnp.int32, (SUB, virtual), 0) == SUB - 1)
        density_ref[pl.ds(rows - SUB, SUB), :] = jnp.where(inside, turned, last)

    return pl.pallas_call(
        kernel,
        in_specs=whole(2 + len(others)),
        out_specs=[pl.BlockSpec(memory_space=VMEM), pl.BlockSpec(memory_space=SMEM)],
        out_shape=[jax.ShapeDtypeStruct((rows, virtual), jnp.float32), jax.ShapeDtypeStruct((1,), jnp.float32)],
        compiler_params=PARAMS,
        name="closing",
    )(own, energies, *others)


def exchanged(parts, axis, order, low=0):
    return [swapped(parts[d], axis, d << low) for d in order]


def summed(value, axis, low, bits):
    if bits == 0:
        return value
    if bits == 1:
        other = swapped(value, axis, 1 << low)
        return (value.astype(jnp.float32) + other.astype(jnp.float32)).astype(jnp.bfloat16)
    place = (lax.axis_index(axis) >> low) & 3
    share = value.shape[1] // 4
    parts = [lax.dynamic_slice_in_dim(value, (place ^ d) * share, share, 1) for d in range(4)]
    chunks = scattered(parts, axis, low, bits)
    out = jnp.zeros_like(value)
    for d, chunk in zip((0, *GATHER_ORDER), chunks):
        out = lax.dynamic_update_slice_in_dim(out, chunk, (place ^ d) * share, 1)
    return out


def scattered(parts, axis, low, bits):
    total = parts[0].astype(jnp.float32)
    for part in exchanged(parts, axis, SUM_ORDER, low):
        total += part.astype(jnp.float32)
    total = summed(total.astype(jnp.bfloat16), axis, low + 2, bits - 2)
    return [total] + exchanged([total] * len(parts), axis, GATHER_ORDER, low)


def per_device(
    shell_ints, block_ids, block_count, occ_coef, occ_pick, vir_coef, occ_energy, vir_energy
):
    _, slots, width, _ = shell_ints.shape
    n_aux = lax.axis_size("aux")
    n_pair = lax.axis_size("pair")
    n_half = n_aux // 2
    pairs = n_half // n_pair
    bits = n_aux.bit_length() - 1

    ints = jnp.transpose(shell_ints, (1, 2, 3, 0))
    counts = (slots // 2, slots - slots // 2)
    *first, chosen, tables = half_first(
        ints, block_ids, occ_pick, occ_coef, counts[0], n_aux, n_pair
    )
    block_count, _ = lax.optimization_barrier((block_count, first[0]))
    later = list(half_rest(ints, block_count, chosen, tables, n_pair, pairs))
    got = [made[:1] + exchanged(made, "pair", PAIR_ORDER) for made in (first, later)]

    fitted, rest = fitted_first(vir_coef, got[0], pairs, counts)
    parts = coulomb_parts(fitted, rest, got[0], got[1], pairs, counts, 4)

    occ_pick, occ_energy, vir_energy, _ = lax.optimization_barrier((occ_pick, occ_energy, vir_energy, later[0]))
    own_pairs = lax.axis_index("pair") * pairs + jnp.arange(pairs, dtype=jnp.int32)
    spots = jnp.arange(n_aux, dtype=jnp.int32)
    batch = occ_pick[:n_aux]
    orbitals = jnp.arange(occ_energy.shape[0], dtype=jnp.int32)
    energies = jnp.sum(jnp.where(batch[:, None] == orbitals[None, :], occ_energy[None, :], 0.0), axis=1)
    levels = jnp.sum(jnp.where(own_pairs[:, None] == spots[None, :] % n_half, energies[None, :], 0.0), axis=1)
    inverse = 1.0 / (levels[:, None, None] - vir_energy[None, :, None] - vir_energy[None, None, :])

    chunks = scattered(parts, "aux", 0, bits)
    outs = density_parts(inverse, chunks, n_pair)
    others = exchanged(outs, "pair", ROW_ORDER)
    density, energy = closing(outs[0], outs[-1], others, pairs, n_half)
    return (energy, density)


def solution(mesh):
    placed = (P("aux", "pair", None, None), P("pair", None), P("pair"), P(), P(), P(), P(), P())
    return jax.shard_map(
        per_device,
        mesh=mesh,
        in_specs=placed,
        out_specs=(P("aux"), P("pair", None)),
        check_vma=False,
    )
```

```python
import jax
import jax.numpy as jnp
from jax import lax
from jax.experimental import pallas as pl
from jax.experimental.pallas import tpu as pltpu
from jax.sharding import PartitionSpec as P

VMEM = pltpu.VMEM
SMEM = pltpu.SMEM
TILE = 16
SUB = 8
MARK = 128
PARAMS = pltpu.CompilerParams(vmem_limit_bytes=48 * 1024 * 1024)


PAIR_ORDER = (2, 3, 1)
SUM_ORDER = (3, 1, 2)
GATHER_ORDER = (3, 1, 2)
ROW_ORDER = (2, 1, 3)


def swapped(value, axis, mask):
    count = lax.axis_size(axis)
    return lax.ppermute(value, axis, [(source, source ^ mask) for source in range(count)])


def in_hbm(*values):
    return [pltpu.with_memory_space_constraint(value, pltpu.HBM) for value in values]


def whole(count):
    return [pl.BlockSpec(memory_space=VMEM)] * count


def half_first(ints, block_ids, occ_pick, occ_coef, count, n_aux, n_pair):
    slots, width, _, aux_rows = ints.shape
    blocks, _, nocc = occ_coef.shape
    n_half = n_aux // 2
    pairs = n_half // n_pair
    rows = 2 * pairs * count * width

    def kernel(ids_hbm, pick_hbm, occ_hbm, ints_hbm, *refs):
        outs, chosen_ref, tables_ref = refs[:n_pair], refs[n_pair], refs[n_pair + 1]
        ids_ref, pick_ref, occ_ref, held, small, large = refs[n_pair + 2 :]
        tables = [
            pltpu.make_async_copy(source, target, small.at[at])
            for at, (source, target) in enumerate(((ids_hbm, ids_ref), (pick_hbm, pick_ref), (occ_hbm, occ_ref)))
        ]
        for copy in tables:
            copy.start()
        copies = started(ints_hbm, held, large, 0, count, width * width)
        for copy in tables:
            copy.wait()
        pair_at = lax.axis_index("pair")
        lane = lax.broadcasted_iota(jnp.int32, (SUB, nocc), 1)
        chosen = []
        for mate in range(n_pair):
            for pair in range(pairs):
                for side in range(2):
                    orbital = pick_ref[(pair_at ^ mate) * pairs + pair + side * n_half]
                    chosen.append(jnp.where(lane == orbital, 1.0, 0.0))
        chosen = jnp.concatenate(chosen, axis=0).astype(jnp.bfloat16)
        weights = [slot_weights(chosen, occ_ref[ids_ref[1, slot]]) for slot in range(count)]
        row = lax.broadcasted_iota(jnp.int32, (TILE, aux_rows), 0)
        blocks = jnp.zeros((TILE, aux_rows), jnp.float32)
        for slot in range(slots):
            blocks = jnp.where(row == slot, ids_ref[0, slot].astype(jnp.float32), blocks)
        for out in outs:
            out[pl.ds(rows, TILE), :] = blocks.astype(jnp.bfloat16)
        chosen_ref[...] = chosen
        for slot in range(count, slots):
            tables_ref[slot - count] = occ_ref[ids_ref[1, slot]]
        for slot in range(count):
            copies[slot].wait()
            halves(weights[slot], held, outs, slot, count, width, pairs)

    return pl.pallas_call(
        kernel,
        in_specs=[pl.BlockSpec(memory_space=pltpu.HBM)] * 4,
        out_specs=whole(n_pair + 2),
        out_shape=[jax.ShapeDtypeStruct((rows + TILE, aux_rows), jnp.bfloat16)] * n_pair
        + [
            jax.ShapeDtypeStruct((n_aux * SUB, nocc), jnp.bfloat16),
            jax.ShapeDtypeStruct((slots - count, width, nocc), jnp.bfloat16),
        ],
        scratch_shapes=[
            SMEM((2, slots), jnp.int32),
            SMEM((nocc,), jnp.int32),
            VMEM(occ_coef.shape, jnp.bfloat16),
            VMEM((count * width * width, aux_rows), jnp.bfloat16),
            pltpu.SemaphoreType.DMA((3,)),
            pltpu.SemaphoreType.DMA((count,)),
        ],
        compiler_params=PARAMS,
        name="half_first",
    )(*in_hbm(block_ids.T, occ_pick, occ_coef, ints.reshape(-1, aux_rows)))


def started(ints_hbm, held, sems, first, count, rows):
    copies = []
    for slot in range(count):
        source = ints_hbm.at[pl.ds((first + slot) * rows, rows), :]
        copies.append(pltpu.make_async_copy(source, held.at[pl.ds(slot * rows, rows), :], sems.at[slot]))
        copies[-1].start()
    return copies


def slot_weights(chosen, table):
    width = table.shape[0]
    table = jnp.concatenate([table] * (128 // width), axis=0)
    spread = lax.dot_general(chosen, table, (((1,), (1,)), ((), ())), preferred_element_type=jnp.float32)
    spread = jnp.concatenate([spread] * (SUB * width // 128), axis=1)
    row = lax.broadcasted_iota(jnp.int32, spread.shape, 0)
    column = lax.broadcasted_iota(jnp.int32, spread.shape, 1)
    return jnp.where(row % SUB == column // width, spread, 0.0).astype(jnp.bfloat16)


def halves(weights, ints, outs, slot, count, width, pairs):
    depth = SUB * width
    for step in range(width // TILE):
        at = slot * (width // TILE) + step
        made = [
            jnp.dot(weights, ints[pl.ds((2 * at + part) * depth, depth), :], preferred_element_type=jnp.float32)
            for part in range(2)
        ]
        for mate, out in enumerate(outs):
            for orbital in range(2 * pairs):
                source = (mate * 2 * pairs + orbital) * SUB
                both = jnp.concatenate([part[source : source + SUB] for part in made], axis=0)
                out[pl.ds(orbital * count * width + at * TILE, TILE), :] = both.astype(jnp.bfloat16)


def half_rest(ints, block_count, chosen, tables, n_pair, pairs):
    slots, width, _, aux_rows = ints.shape
    count = tables.shape[0]

    def kernel(count_ref, chosen_ref, tables_ref, ints_hbm, *refs):
        outs, (held, large) = refs[:n_pair], refs[n_pair:]
        copies = started(ints_hbm, held, large, slots - count, count, width * width)
        weights = [slot_weights(chosen_ref[...], tables_ref[slot]) for slot in range(count)]
        for slot in range(count):
            copies[slot].wait()
            halves(weights[slot], held, outs, slot, count, width, pairs)
        live = count_ref[0]
        mark = jnp.full((TILE, aux_rows), (MARK * (live + 1)).astype(jnp.float32), jnp.float32).astype(jnp.bfloat16)
        for out in outs:
            spot = pl.ds((count - 1) * width, TILE)
            out[spot, :] = jnp.where(live < slots, mark, out[spot, :])

    return pl.pallas_call(
        kernel,
        in_specs=[pl.BlockSpec(memory_space=SMEM)] + whole(2) + [pl.BlockSpec(memory_space=pltpu.HBM)],
        out_specs=whole(n_pair),
        out_shape=[jax.ShapeDtypeStruct((2 * pairs * count * width, aux_rows), jnp.bfloat16)] * n_pair,
        scratch_shapes=[
            VMEM((count * width * width, aux_rows), jnp.bfloat16),
            pltpu.SemaphoreType.DMA((count,)),
        ],
        compiler_params=PARAMS,
        name="half_rest",
    )(block_count, chosen, tables, *in_hbm(ints.reshape(-1, aux_rows)))


def fitted_first(vir_coef, parts, pairs, counts):
    aux_rows = parts[0].shape[1]
    width, virtual = vir_coef.shape[1], vir_coef.shape[2]
    span = counts[0] * width
    rest_rows = (sum(counts) - 1) * width

    def kernel(vir_ref, *refs):
        held, (fitted_ref, rest_ref, last_ref, own_ref) = refs[: len(parts)], refs[len(parts) :]
        first, rest = [], []
        for part in held:
            tail = part[pl.ds(2 * pairs * span, TILE), :][:, :128].astype(jnp.float32)
            found = [vir_ref[tail[slot, 0].astype(jnp.int32)] for slot in range(sum(counts))]
            first.append(found[0])
            rest.append(jnp.concatenate(found[1:], axis=0))
        own_ref[...] = jnp.concatenate(first, axis=0).T
        rest_ref[...] = jnp.concatenate(rest[:-1], axis=0).T
        last_ref[...] = rest[-1].T
        for orbital in range(2 * pairs):
            blocks = jnp.concatenate([part[pl.ds(orbital * span, width), :] for part in held], axis=0)
            fitted_ref[orbital] = jnp.dot(own_ref[...], blocks, preferred_element_type=jnp.float32)

    return pl.pallas_call(
        kernel,
        in_specs=whole(1 + len(parts)),
        out_specs=whole(3),
        out_shape=[
            jax.ShapeDtypeStruct((2 * pairs, virtual, aux_rows), jnp.float32),
            jax.ShapeDtypeStruct((virtual, (len(parts) - 1) * rest_rows), jnp.bfloat16),
            jax.ShapeDtypeStruct((virtual, rest_rows), jnp.bfloat16),
        ],
        scratch_shapes=[VMEM((virtual, len(parts) * width), jnp.bfloat16)],
        compiler_params=PARAMS,
        name="fitted_first",
    )(vir_coef, *parts)


def live_slots(later, counts, width):
    mark = later[pl.ds((counts[1] - 1) * width, TILE), :][:, :128].astype(jnp.float32)[0, 0]
    return jnp.where(mark < MARK, sum(counts), (mark * (1.0 / MARK)).astype(jnp.int32) - 1)


def live_blocks(first, later, live, orbital, counts, width):
    blocks = []
    for slot in range(1, sum(counts)):
        chunk = int(slot >= counts[0])
        at = (orbital * counts[chunk] + slot - chunk * counts[0]) * width
        block = (first, later)[chunk][pl.ds(at, width), :]
        blocks.append(jnp.where(slot < live, block, jnp.zeros_like(block)))
    return blocks


def fitted_more(fitted, rest, first, later, counts, width):
    count = len(first)

    def kernel(fitted_ref, rest_ref, *refs):
        held, out_ref = list(zip(refs[:count], refs[count : 2 * count])), refs[-1]
        live = [live_slots(part[1], counts, width) for part in held]
        for orbital in range(fitted.shape[0]):
            blocks = []
            for part, alive in zip(held, live):
                blocks += live_blocks(*part, alive, orbital, counts, width)
            total = jnp.dot(rest_ref[...], jnp.concatenate(blocks, axis=0), preferred_element_type=jnp.float32)
            out_ref[orbital] = fitted_ref[orbital] + total

    return pl.pallas_call(
        kernel,
        in_specs=whole(2 + 2 * count),
        out_specs=pl.BlockSpec(memory_space=VMEM),
        out_shape=jax.ShapeDtypeStruct(fitted.shape, fitted.dtype),
        compiler_params=PARAMS,
        name="fitted_more",
    )(fitted, rest, *first, *later)


def coulomb_parts(fitted, last, first, later, pairs, counts, width, quad):
    virtual = fitted.shape[1]
    share = virtual // quad

    def kernel(fitted_ref, last_ref, first_ref, later_ref, *refs):
        outs, block_ref = refs[:-1], refs[-1]
        place = lax.axis_index("aux") % quad
        live = live_slots(later_ref, counts, width)
        for pair in range(pairs):
            sides = []
            for orbital in (2 * pair, 2 * pair + 1):
                blocks = jnp.concatenate(live_blocks(first_ref, later_ref, live, orbital, counts, width), axis=0)
                total = jnp.dot(last_ref[...], blocks, preferred_element_type=jnp.float32)
                sides.append((fitted_ref[orbital] + total).astype(jnp.bfloat16))
            block = lax.dot_general(*sides, (((1,), (1,)), ((), ())), preferred_element_type=jnp.float32)
            block_ref[...] = block.astype(jnp.bfloat16)
            for part, out in enumerate(outs):
                at = pl.multiple_of((place ^ part) * share, share)
                out[pair] = block_ref[pl.ds(at, share), :]

    return pl.pallas_call(
        kernel,
        in_specs=whole(4),
        out_specs=whole(quad),
        out_shape=[jax.ShapeDtypeStruct((pairs, share, virtual), jnp.bfloat16)] * quad,
        scratch_shapes=[VMEM((virtual, virtual), jnp.bfloat16)],
        compiler_params=PARAMS,
        name="coulomb_parts",
    )(fitted, last, first, later)


def density_parts(inverse, chunks, n_pair):
    quad = len(chunks)
    pairs, share, virtual = chunks[0].shape
    rows = virtual // n_pair

    def kernel(inverse_ref, *refs):
        held, own_ref, outs = refs[:quad], refs[quad], refs[quad + 1 : quad + n_pair]
        energy_ref, block_ref, total_ref = refs[quad + n_pair :]
        place = lax.axis_index("aux") % quad
        pair_at = lax.axis_index("pair")
        lane = lax.broadcasted_iota(jnp.int32, (1, virtual), 1)
        energies = []
        totals = [None] * n_pair
        for pair in range(pairs):
            for part, chunk in zip((0, *GATHER_ORDER), held):
                at = pl.multiple_of((place ^ part) * share, share)
                block_ref[pl.ds(at, share), :] = chunk[pair]
            block = block_ref[...].astype(jnp.float32)
            flipped = block_ref[...].T.astype(jnp.float32)
            inverse = inverse_ref[pair]
            energy = jnp.sum(block * (2.0 * block - flipped) * inverse)
            even = ((block + flipped) * inverse).astype(jnp.bfloat16)
            odd = ((block - flipped) * (inverse * 3.0**0.5)).astype(jnp.bfloat16)
            left = jnp.concatenate([even, odd], axis=1)
            right = jnp.concatenate([even, -odd], axis=0)
            term = 0.5 * jnp.dot(left, right, preferred_element_type=jnp.float32)
            total_ref[...] = term if pair == 0 else total_ref[...] + term
        for part in range(n_pair):
            totals[part] = total_ref[pl.ds(pl.multiple_of((pair_at ^ part) * rows, rows), rows), :]
            energies.append(energy)
        own_ref[...] = totals[0]
        energy_ref[...] = jnp.zeros_like(energy_ref)
        for pair, energy in enumerate(energies):
            energy_ref[...] = jnp.where(lane == pair, energy, energy_ref[...])
        for part in range(1, n_pair):
            outs[part - 1][...] = totals[part].astype(jnp.bfloat16)
            first = (pair_at ^ part) * rows
            last = totals[part][rows - TILE :]
            row = lax.broadcasted_iota(jnp.int32, (TILE, virtual), 0)
            corner = jnp.zeros((1, virtual), jnp.float32)
            for pair, energy in enumerate(energies):
                rest = jnp.full((1, virtual), energy, jnp.float32)
                for at in range(3):
                    piece = rest.astype(jnp.bfloat16).astype(jnp.float32)
                    corner = jnp.where(lane == first + 3 * pair + at, piece, corner)
                    rest = rest - piece
            inside = (lane >= first) & (lane < first + 3 * pairs) & (row == TILE - 1)
            outs[part - 1][pl.ds(rows - TILE, TILE), :] = jnp.where(inside, corner, last).astype(jnp.bfloat16)

    return pl.pallas_call(
        kernel,
        in_specs=whole(1 + quad),
        out_specs=whole(n_pair + 1),
        out_shape=[jax.ShapeDtypeStruct((rows, virtual), jnp.float32)]
        + [jax.ShapeDtypeStruct((rows, virtual), jnp.bfloat16)] * (n_pair - 1)
        + [jax.ShapeDtypeStruct((1, virtual), jnp.float32)],
        scratch_shapes=[
            VMEM((virtual, virtual), jnp.bfloat16),
            VMEM((virtual, virtual), jnp.float32),
        ],
        compiler_params=PARAMS,
        name="density_parts",
    )(inverse, *chunks)


def closing(own, energies, others, pairs, n_half):
    rows, virtual = own.shape

    def kernel(own_ref, energy_ref, *refs):
        held, (density_ref, value_ref) = refs[: len(others)], refs[len(others) :]
        wanted = lax.axis_index("aux") % n_half
        pair_at = lax.axis_index("pair")
        lane = lax.broadcasted_iota(jnp.int32, (1, virtual), 1)
        first = pair_at * rows
        found = jnp.zeros((1, virtual), jnp.float32)
        total = own_ref[...]
        for mate, ref in zip((0, *ROW_ORDER), (None, *held)):
            at = wanted - (pair_at ^ mate) * pairs
            here = (at >= 0) & (at < pairs)
            if mate == 0:
                found += jnp.where(here & (lane == at), energy_ref[...], 0.0)
            else:
                part = ref[...].astype(jnp.float32)
                spot = lane - first - 3 * at
                found += jnp.where(here & (spot >= 0) & (spot < 3), part[rows - 1 :], 0.0)
                total += part
        value_ref[0] = jnp.sum(found)
        density_ref[...] = total
        head = -(-3 * pairs // TILE) * TILE
        top = total[:head]
        wide = lax.broadcasted_iota(jnp.int32, (head, virtual), 1)
        row = lax.broadcasted_iota(jnp.int32, (head, virtual), 0)
        column = jnp.sum(jnp.where(wide == first + rows - 1, top, 0.0), axis=1, keepdims=True)
        turned = jnp.sum(jnp.where(wide == first + row, column, 0.0), axis=0, keepdims=True)
        last = total[rows - SUB :]
        inside = (lane >= first) & (lane < first + 3 * pairs)
        inside = inside & (lax.broadcasted_iota(jnp.int32, (SUB, virtual), 0) == SUB - 1)
        density_ref[pl.ds(rows - SUB, SUB), :] = jnp.where(inside, turned, last)

    return pl.pallas_call(
        kernel,
        in_specs=whole(2 + len(others)),
        out_specs=[pl.BlockSpec(memory_space=VMEM), pl.BlockSpec(memory_space=SMEM)],
        out_shape=[jax.ShapeDtypeStruct((rows, virtual), jnp.float32), jax.ShapeDtypeStruct((1,), jnp.float32)],
        compiler_params=PARAMS,
        name="closing",
    )(own, energies, *others)


def exchanged(parts, axis, order, low=0):
    return [swapped(parts[d], axis, d << low) for d in order]


def summed(value, axis, low, bits):
    if bits == 0:
        return value
    if bits == 1:
        other = swapped(value, axis, 1 << low)
        return (value.astype(jnp.float32) + other.astype(jnp.float32)).astype(jnp.bfloat16)
    place = (lax.axis_index(axis) >> low) & 3
    share = value.shape[1] // 4
    parts = [lax.dynamic_slice_in_dim(value, (place ^ d) * share, share, 1) for d in range(4)]
    chunks = scattered(parts, axis, low, bits)
    out = jnp.zeros_like(value)
    for d, chunk in zip((0, *GATHER_ORDER), chunks):
        out = lax.dynamic_update_slice_in_dim(out, chunk, (place ^ d) * share, 1)
    return out


def scattered(parts, axis, low, bits):
    total = parts[0].astype(jnp.float32)
    for part in exchanged(parts, axis, SUM_ORDER, low):
        total += part.astype(jnp.float32)
    total = summed(total.astype(jnp.bfloat16), axis, low + 2, bits - 2)
    return [total] + exchanged([total] * len(parts), axis, GATHER_ORDER, low)


def per_device(
    shell_ints, block_ids, block_count, occ_coef, occ_pick, vir_coef, occ_energy, vir_energy
):
    _, slots, width, _ = shell_ints.shape
    n_aux = lax.axis_size("aux")
    n_pair = lax.axis_size("pair")
    n_half = n_aux // 2
    pairs = n_half // n_pair
    bits = n_aux.bit_length() - 1

    ints = jnp.transpose(shell_ints, (1, 2, 3, 0))
    counts = (slots // 2, slots - slots // 2)
    *first, chosen, tables = half_first(
        ints, block_ids, occ_pick, occ_coef, counts[0], n_aux, n_pair
    )
    block_count, _ = lax.optimization_barrier((block_count, first[0]))
    later = list(half_rest(ints, block_count, chosen, tables, n_pair, pairs))
    got = [made[:1] + exchanged(made, "pair", PAIR_ORDER) for made in (first, later)]

    slowest = 1 + PAIR_ORDER.index(max(PAIR_ORDER))
    ends = [group.pop(slowest) for group in got]
    fitted, rest, last = fitted_first(vir_coef, got[0] + ends[:1], pairs, counts)
    fitted = fitted_more(fitted, rest, *got, counts, width)
    parts = coulomb_parts(fitted, last, *ends, pairs, counts, width, 4)

    occ_pick, occ_energy, vir_energy, _ = lax.optimization_barrier((occ_pick, occ_energy, vir_energy, later[0]))
    own_pairs = lax.axis_index("pair") * pairs + jnp.arange(pairs, dtype=jnp.int32)
    spots = jnp.arange(n_aux, dtype=jnp.int32)
    batch = occ_pick[:n_aux]
    orbitals = jnp.arange(occ_energy.shape[0], dtype=jnp.int32)
    energies = jnp.sum(jnp.where(batch[:, None] == orbitals[None, :], occ_energy[None, :], 0.0), axis=1)
    levels = jnp.sum(jnp.where(own_pairs[:, None] == spots[None, :] % n_half, energies[None, :], 0.0), axis=1)
    inverse = 1.0 / (levels[:, None, None] - vir_energy[None, :, None] - vir_energy[None, None, :])

    chunks = scattered(parts, "aux", 0, bits)
    outs = density_parts(inverse, chunks, n_pair)
    others = exchanged(outs, "pair", ROW_ORDER)
    density, energy = closing(outs[0], outs[-1], others, pairs, n_half)
    return (energy, density)


def solution(mesh):
    placed = (P("aux", "pair", None, None), P("pair", None), P("pair"), P(), P(), P(), P(), P())
    return jax.shard_map(
        per_device,
        mesh=mesh,
        in_specs=placed,
        out_specs=(P("aux"), P("pair", None)),
        check_vma=False,
    )
```

```python
import jax
import jax.numpy as jnp
from jax import lax
from jax.experimental import pallas as pl
from jax.experimental.pallas import tpu as pltpu
from jax.sharding import PartitionSpec as P

VMEM = pltpu.VMEM
SMEM = pltpu.SMEM
TILE = 16
SUB = 8
MARK = 128
PARAMS = pltpu.CompilerParams(vmem_limit_bytes=48 * 1024 * 1024)


PAIR_ORDER = (2, 3, 1)
SUM_ORDER = (3, 1, 2)
GATHER_ORDER = (3, 1, 2)
ROW_ORDER = (2, 1, 3)


def swapped(value, axis, mask):
    count = lax.axis_size(axis)
    return lax.ppermute(value, axis, [(source, source ^ mask) for source in range(count)])


def in_hbm(*values):
    return [pltpu.with_memory_space_constraint(value, pltpu.HBM) for value in values]


def whole(count):
    return [pl.BlockSpec(memory_space=VMEM)] * count


def half_first(ints, block_ids, occ_pick, occ_coef, count, n_aux, n_pair):
    slots, width, _, aux_rows = ints.shape
    blocks, _, nocc = occ_coef.shape
    n_half = n_aux // 2
    pairs = n_half // n_pair
    rows = 2 * pairs * count * width

    def kernel(ids_hbm, pick_hbm, occ_hbm, ints_hbm, *refs):
        outs, chosen_ref, tables_ref = refs[:n_pair], refs[n_pair], refs[n_pair + 1]
        ids_ref, pick_ref, occ_ref, held, small, large = refs[n_pair + 2 :]
        tables = [
            pltpu.make_async_copy(source, target, small.at[at])
            for at, (source, target) in enumerate(((ids_hbm, ids_ref), (pick_hbm, pick_ref), (occ_hbm, occ_ref)))
        ]
        for copy in tables:
            copy.start()
        copies = started(ints_hbm, held, large, 0, count, width * width)
        for copy in tables:
            copy.wait()
        pair_at = lax.axis_index("pair")
        lane = lax.broadcasted_iota(jnp.int32, (SUB, nocc), 1)
        chosen = []
        for mate in range(n_pair):
            for pair in range(pairs):
                for side in range(2):
                    orbital = pick_ref[(pair_at ^ mate) * pairs + pair + side * n_half]
                    chosen.append(jnp.where(lane == orbital, 1.0, 0.0))
        chosen = jnp.concatenate(chosen, axis=0).astype(jnp.bfloat16)
        weights = [slot_weights(chosen, occ_ref[ids_ref[1, slot]]) for slot in range(count)]
        row = lax.broadcasted_iota(jnp.int32, (TILE, aux_rows), 0)
        blocks = jnp.zeros((TILE, aux_rows), jnp.float32)
        for slot in range(slots):
            blocks = jnp.where(row == slot, ids_ref[0, slot].astype(jnp.float32), blocks)
        for out in outs:
            out[pl.ds(rows, TILE), :] = blocks.astype(jnp.bfloat16)
        chosen_ref[...] = chosen
        for slot in range(count, slots):
            tables_ref[slot - count] = occ_ref[ids_ref[1, slot]]
        for slot in range(count):
            copies[slot].wait()
            halves(weights[slot], held, outs, slot, count, width, pairs)

    return pl.pallas_call(
        kernel,
        in_specs=[pl.BlockSpec(memory_space=pltpu.HBM)] * 4,
        out_specs=whole(n_pair + 2),
        out_shape=[jax.ShapeDtypeStruct((rows + TILE, aux_rows), jnp.bfloat16)] * n_pair
        + [
            jax.ShapeDtypeStruct((n_aux * SUB, nocc), jnp.bfloat16),
            jax.ShapeDtypeStruct((slots - count, width, nocc), jnp.bfloat16),
        ],
        scratch_shapes=[
            SMEM((2, slots), jnp.int32),
            SMEM((nocc,), jnp.int32),
            VMEM(occ_coef.shape, jnp.bfloat16),
            VMEM((count * width * width, aux_rows), jnp.bfloat16),
            pltpu.SemaphoreType.DMA((3,)),
            pltpu.SemaphoreType.DMA((count,)),
        ],
        compiler_params=PARAMS,
        name="half_first",
    )(*in_hbm(block_ids.T, occ_pick, occ_coef, ints.reshape(-1, aux_rows)))


def started(ints_hbm, held, sems, first, count, rows):
    copies = []
    for slot in range(count):
        source = ints_hbm.at[pl.ds((first + slot) * rows, rows), :]
        copies.append(pltpu.make_async_copy(source, held.at[pl.ds(slot * rows, rows), :], sems.at[slot]))
        copies[-1].start()
    return copies


def slot_weights(chosen, table):
    width = table.shape[0]
    table = jnp.concatenate([table] * (128 // width), axis=0)
    spread = lax.dot_general(chosen, table, (((1,), (1,)), ((), ())), preferred_element_type=jnp.float32)
    spread = jnp.concatenate([spread] * (SUB * width // 128), axis=1)
    row = lax.broadcasted_iota(jnp.int32, spread.shape, 0)
    column = lax.broadcasted_iota(jnp.int32, spread.shape, 1)
    return jnp.where(row % SUB == column // width, spread, 0.0).astype(jnp.bfloat16)


def halves(weights, ints, outs, slot, count, width, pairs):
    depth = SUB * width
    for step in range(width // TILE):
        at = slot * (width // TILE) + step
        made = [
            jnp.dot(weights, ints[pl.ds((2 * at + part) * depth, depth), :], preferred_element_type=jnp.float32)
            for part in range(2)
        ]
        for mate, out in enumerate(outs):
            for orbital in range(2 * pairs):
                source = (mate * 2 * pairs + orbital) * SUB
                both = jnp.concatenate([part[source : source + SUB] for part in made], axis=0)
                out[pl.ds(orbital * count * width + at * TILE, TILE), :] = both.astype(jnp.bfloat16)


def half_rest(ints, block_count, chosen, tables, n_pair, pairs):
    slots, width, _, aux_rows = ints.shape
    count = tables.shape[0]

    def kernel(count_ref, chosen_ref, tables_ref, ints_hbm, *refs):
        outs, (held, large) = refs[:n_pair], refs[n_pair:]
        copies = started(ints_hbm, held, large, slots - count, count, width * width)
        weights = [slot_weights(chosen_ref[...], tables_ref[slot]) for slot in range(count)]
        for slot in range(count):
            copies[slot].wait()
            halves(weights[slot], held, outs, slot, count, width, pairs)
        live = count_ref[0]
        mark = jnp.full((TILE, aux_rows), (MARK * (live + 1)).astype(jnp.float32), jnp.float32).astype(jnp.bfloat16)
        for out in outs:
            spot = pl.ds((count - 1) * width, TILE)
            out[spot, :] = jnp.where(live < slots, mark, out[spot, :])

    return pl.pallas_call(
        kernel,
        in_specs=[pl.BlockSpec(memory_space=SMEM)] + whole(2) + [pl.BlockSpec(memory_space=pltpu.HBM)],
        out_specs=whole(n_pair),
        out_shape=[jax.ShapeDtypeStruct((2 * pairs * count * width, aux_rows), jnp.bfloat16)] * n_pair,
        scratch_shapes=[
            VMEM((count * width * width, aux_rows), jnp.bfloat16),
            pltpu.SemaphoreType.DMA((count,)),
        ],
        compiler_params=PARAMS,
        name="half_rest",
    )(block_count, chosen, tables, *in_hbm(ints.reshape(-1, aux_rows)))


def fitted_first(vir_coef, parts, pairs, counts):
    aux_rows = parts[0].shape[1]
    width, virtual = vir_coef.shape[1], vir_coef.shape[2]
    span = counts[0] * width
    rest_rows = (sum(counts) - 1) * width

    def kernel(vir_ref, *refs):
        held, (fitted_ref, rest_ref, last_ref, own_ref) = refs[: len(parts)], refs[len(parts) :]
        first, rest = [], []
        for part in held:
            tail = part[pl.ds(2 * pairs * span, TILE), :][:, :128].astype(jnp.float32)
            found = [vir_ref[tail[slot, 0].astype(jnp.int32)] for slot in range(sum(counts))]
            first.append(found[0])
            rest.append(jnp.concatenate(found[1:], axis=0))
        own_ref[...] = jnp.concatenate(first, axis=0).T
        rest_ref[...] = jnp.concatenate(rest[:-1], axis=0).T
        last_ref[...] = rest[-1].T
        for orbital in range(2 * pairs):
            blocks = jnp.concatenate([part[pl.ds(orbital * span, width), :] for part in held], axis=0)
            fitted_ref[orbital] = jnp.dot(own_ref[...], blocks, preferred_element_type=jnp.float32)

    return pl.pallas_call(
        kernel,
        in_specs=whole(1 + len(parts)),
        out_specs=whole(3),
        out_shape=[
            jax.ShapeDtypeStruct((2 * pairs, virtual, aux_rows), jnp.float32),
            jax.ShapeDtypeStruct((virtual, (len(parts) - 1) * rest_rows), jnp.bfloat16),
            jax.ShapeDtypeStruct((virtual, rest_rows), jnp.bfloat16),
        ],
        scratch_shapes=[VMEM((virtual, len(parts) * width), jnp.bfloat16)],
        compiler_params=PARAMS,
        name="fitted_first",
    )(vir_coef, *parts)


def live_slots(later, counts, width):
    mark = later[pl.ds((counts[1] - 1) * width, TILE), :][:, :128].astype(jnp.float32)[0, 0]
    return jnp.where(mark < MARK, sum(counts), (mark * (1.0 / MARK)).astype(jnp.int32) - 1)


def live_blocks(first, later, live, orbital, counts, width):
    blocks = []
    for slot in range(1, sum(counts)):
        chunk = int(slot >= counts[0])
        at = (orbital * counts[chunk] + slot - chunk * counts[0]) * width
        block = (first, later)[chunk][pl.ds(at, width), :]
        blocks.append(jnp.where(slot < live, block, jnp.zeros_like(block)))
    return blocks


def fitted_more(fitted, rest, first, later, counts, width):
    count = len(first)

    def kernel(fitted_ref, rest_ref, *refs):
        held, out_ref = list(zip(refs[:count], refs[count : 2 * count])), refs[-1]
        live = [live_slots(part[1], counts, width) for part in held]
        for orbital in range(fitted.shape[0]):
            blocks = []
            for part, alive in zip(held, live):
                blocks += live_blocks(*part, alive, orbital, counts, width)
            total = jnp.dot(rest_ref[...], jnp.concatenate(blocks, axis=0), preferred_element_type=jnp.float32)
            out_ref[orbital] = fitted_ref[orbital] + total

    return pl.pallas_call(
        kernel,
        in_specs=whole(2 + 2 * count),
        out_specs=pl.BlockSpec(memory_space=VMEM),
        out_shape=jax.ShapeDtypeStruct(fitted.shape, fitted.dtype),
        compiler_params=PARAMS,
        name="fitted_more",
    )(fitted, rest, *first, *later)


def coulomb_parts(fitted, last, first, later, pairs, counts, width, quad):
    virtual = fitted.shape[1]
    share = virtual // quad

    def kernel(fitted_ref, last_ref, first_ref, later_ref, *refs):
        outs, block_ref = refs[:-1], refs[-1]
        place = lax.axis_index("aux") % quad
        live = live_slots(later_ref, counts, width)
        for pair in range(pairs):
            sides = []
            for orbital in (2 * pair, 2 * pair + 1):
                blocks = jnp.concatenate(live_blocks(first_ref, later_ref, live, orbital, counts, width), axis=0)
                total = jnp.dot(last_ref[...], blocks, preferred_element_type=jnp.float32)
                sides.append((fitted_ref[orbital] + total).astype(jnp.bfloat16))
            block = lax.dot_general(*sides, (((1,), (1,)), ((), ())), preferred_element_type=jnp.float32)
            block_ref[...] = block.astype(jnp.bfloat16)
            for part, out in enumerate(outs):
                at = pl.multiple_of((place ^ part) * share, share)
                out[pair] = block_ref[pl.ds(at, share), :]

    return pl.pallas_call(
        kernel,
        in_specs=whole(4),
        out_specs=whole(quad),
        out_shape=[jax.ShapeDtypeStruct((pairs, share, virtual), jnp.bfloat16)] * quad,
        scratch_shapes=[VMEM((virtual, virtual), jnp.bfloat16)],
        compiler_params=PARAMS,
        name="coulomb_parts",
    )(fitted, last, first, later)


def density_parts(inverse, chunks, n_pair):
    quad = len(chunks)
    pairs, share, virtual = chunks[0].shape
    rows = virtual // n_pair

    def kernel(inverse_ref, *refs):
        held, own_ref, outs = refs[:quad], refs[quad], refs[quad + 1 : quad + n_pair]
        energy_ref, block_ref, total_ref = refs[quad + n_pair :]
        place = lax.axis_index("aux") % quad
        pair_at = lax.axis_index("pair")
        lane = lax.broadcasted_iota(jnp.int32, (1, virtual), 1)
        energies = []
        totals = [None] * n_pair
        for pair in range(pairs):
            for part, chunk in zip((0, *GATHER_ORDER), held):
                at = pl.multiple_of((place ^ part) * share, share)
                block_ref[pl.ds(at, share), :] = chunk[pair]
            block = block_ref[...].astype(jnp.float32)
            flipped = block_ref[...].T.astype(jnp.float32)
            inverse = inverse_ref[pair]
            energies.append(jnp.sum(block * (2.0 * block - flipped) * inverse))
            even = ((block + flipped) * inverse).astype(jnp.bfloat16)
            odd = ((block - flipped) * (inverse * 3.0**0.5)).astype(jnp.bfloat16)
            left = jnp.concatenate([even, odd], axis=1)
            right = jnp.concatenate([even, -odd], axis=0)
            term = 0.5 * jnp.dot(left, right, preferred_element_type=jnp.float32)
            total_ref[...] = term if pair == 0 else total_ref[...] + term
        for part in range(n_pair):
            totals[part] = total_ref[pl.ds(pl.multiple_of((pair_at ^ part) * rows, rows), rows), :]
        own_ref[...] = totals[0]
        energy_ref[...] = jnp.zeros_like(energy_ref)
        for pair, energy in enumerate(energies):
            energy_ref[...] = jnp.where(lane == pair, energy, energy_ref[...])
        for part in range(1, n_pair):
            outs[part - 1][...] = totals[part].astype(jnp.bfloat16)
            first = (pair_at ^ part) * rows
            last = totals[part][rows - TILE :]
            row = lax.broadcasted_iota(jnp.int32, (TILE, virtual), 0)
            corner = jnp.zeros((1, virtual), jnp.float32)
            for pair, energy in enumerate(energies):
                rest = jnp.full((1, virtual), energy, jnp.float32)
                for at in range(3):
                    piece = rest.astype(jnp.bfloat16).astype(jnp.float32)
                    corner = jnp.where(lane == first + 3 * pair + at, piece, corner)
                    rest = rest - piece
            inside = (lane >= first) & (lane < first + 3 * pairs) & (row == TILE - 1)
            outs[part - 1][pl.ds(rows - TILE, TILE), :] = jnp.where(inside, corner, last).astype(jnp.bfloat16)

    return pl.pallas_call(
        kernel,
        in_specs=whole(1 + quad),
        out_specs=whole(n_pair + 1),
        out_shape=[jax.ShapeDtypeStruct((rows, virtual), jnp.float32)]
        + [jax.ShapeDtypeStruct((rows, virtual), jnp.bfloat16)] * (n_pair - 1)
        + [jax.ShapeDtypeStruct((1, virtual), jnp.float32)],
        scratch_shapes=[
            VMEM((virtual, virtual), jnp.bfloat16),
            VMEM((virtual, virtual), jnp.float32),
        ],
        compiler_params=PARAMS,
        name="density_parts",
    )(inverse, *chunks)


def closing(own, energies, others, pairs, n_half):
    rows, virtual = own.shape

    def kernel(own_ref, energy_ref, *refs):
        held, (density_ref, value_ref) = refs[: len(others)], refs[len(others) :]
        wanted = lax.axis_index("aux") % n_half
        pair_at = lax.axis_index("pair")
        lane = lax.broadcasted_iota(jnp.int32, (1, virtual), 1)
        first = pair_at * rows
        found = jnp.zeros((1, virtual), jnp.float32)
        total = own_ref[...]
        for mate, ref in zip((0, *ROW_ORDER), (None, *held)):
            at = wanted - (pair_at ^ mate) * pairs
            here = (at >= 0) & (at < pairs)
            if mate == 0:
                found += jnp.where(here & (lane == at), energy_ref[...], 0.0)
            else:
                part = ref[...].astype(jnp.float32)
                spot = lane - first - 3 * at
                found += jnp.where(here & (spot >= 0) & (spot < 3), part[rows - 1 :], 0.0)
                total += part
        value_ref[...] = jnp.sum(found, axis=1, keepdims=True)
        density_ref[...] = total
        head = -(-3 * pairs // TILE) * TILE
        top = total[:head]
        wide = lax.broadcasted_iota(jnp.int32, (head, virtual), 1)
        row = lax.broadcasted_iota(jnp.int32, (head, virtual), 0)
        column = jnp.sum(jnp.where(wide == first + rows - 1, top, 0.0), axis=1, keepdims=True)
        turned = jnp.sum(jnp.where(wide == first + row, column, 0.0), axis=0, keepdims=True)
        last = total[rows - SUB :]
        inside = (lane >= first) & (lane < first + 3 * pairs)
        inside = inside & (lax.broadcasted_iota(jnp.int32, (SUB, virtual), 0) == SUB - 1)
        density_ref[pl.ds(rows - SUB, SUB), :] = jnp.where(inside, turned, last)

    return pl.pallas_call(
        kernel,
        in_specs=whole(2 + len(others)),
        out_specs=whole(2),
        out_shape=[jax.ShapeDtypeStruct((rows, virtual), jnp.float32), jax.ShapeDtypeStruct((1, 1), jnp.float32)],
        compiler_params=PARAMS,
        name="closing",
    )(own, energies, *others)


def exchanged(parts, axis, order, low=0):
    return [swapped(parts[d], axis, d << low) for d in order]


def summed(value, axis, low, bits):
    if bits == 0:
        return value
    if bits == 1:
        other = swapped(value, axis, 1 << low)
        return (value.astype(jnp.float32) + other.astype(jnp.float32)).astype(jnp.bfloat16)
    place = (lax.axis_index(axis) >> low) & 3
    share = value.shape[1] // 4
    parts = [lax.dynamic_slice_in_dim(value, (place ^ d) * share, share, 1) for d in range(4)]
    chunks = scattered(parts, axis, low, bits)
    out = jnp.zeros_like(value)
    for d, chunk in zip((0, *GATHER_ORDER), chunks):
        out = lax.dynamic_update_slice_in_dim(out, chunk, (place ^ d) * share, 1)
    return out


def scattered(parts, axis, low, bits):
    total = parts[0].astype(jnp.float32)
    for part in exchanged(parts, axis, SUM_ORDER, low):
        total += part.astype(jnp.float32)
    total = summed(total.astype(jnp.bfloat16), axis, low + 2, bits - 2)
    return [total] + exchanged([total] * len(parts), axis, GATHER_ORDER, low)


def per_device(
    shell_ints, block_ids, block_count, occ_coef, occ_pick, vir_coef, occ_energy, vir_energy
):
    _, slots, width, _ = shell_ints.shape
    n_aux = lax.axis_size("aux")
    n_pair = lax.axis_size("pair")
    n_half = n_aux // 2
    pairs = n_half // n_pair
    bits = n_aux.bit_length() - 1

    ints = jnp.transpose(shell_ints, (1, 2, 3, 0))
    counts = (slots // 2, slots - slots // 2)
    *first, chosen, tables = half_first(
        ints, block_ids, occ_pick, occ_coef, counts[0], n_aux, n_pair
    )
    block_count, _ = lax.optimization_barrier((block_count, first[0]))
    later = list(half_rest(ints, block_count, chosen, tables, n_pair, pairs))
    got = [made[:1] + exchanged(made, "pair", PAIR_ORDER) for made in (first, later)]

    slowest = 1 + PAIR_ORDER.index(max(PAIR_ORDER))
    ends = [group.pop(slowest) for group in got]
    fitted, rest, last = fitted_first(vir_coef, got[0] + ends[:1], pairs, counts)
    fitted = fitted_more(fitted, rest, *got, counts, width)
    parts = coulomb_parts(fitted, last, *ends, pairs, counts, width, 4)

    occ_pick, occ_energy, vir_energy, _ = lax.optimization_barrier((occ_pick, occ_energy, vir_energy, later[0]))
    own_pairs = lax.axis_index("pair") * pairs + jnp.arange(pairs, dtype=jnp.int32)
    spots = jnp.arange(n_aux, dtype=jnp.int32)
    batch = occ_pick[:n_aux]
    orbitals = jnp.arange(occ_energy.shape[0], dtype=jnp.int32)
    energies = jnp.sum(jnp.where(batch[:, None] == orbitals[None, :], occ_energy[None, :], 0.0), axis=1)
    levels = jnp.sum(jnp.where(own_pairs[:, None] == spots[None, :] % n_half, energies[None, :], 0.0), axis=1)
    inverse = 1.0 / (levels[:, None, None] - vir_energy[None, :, None] - vir_energy[None, None, :])

    chunks = scattered(parts, "aux", 0, bits)
    outs = density_parts(inverse, chunks, n_pair)
    others = exchanged(outs, "pair", ROW_ORDER)
    density, energy = closing(outs[0], outs[-1], others, pairs, n_half)
    return (energy.reshape(1), density)


def solution(mesh):
    placed = (P("aux", "pair", None, None), P("pair", None), P("pair"), P(), P(), P(), P(), P())
    return jax.shard_map(
        per_device,
        mesh=mesh,
        in_specs=placed,
        out_specs=(P("aux"), P("pair", None)),
        check_vma=False,
    )
```

```python
import jax
import jax.numpy as jnp
from jax import lax
from jax.experimental import pallas as pl
from jax.experimental.pallas import tpu as pltpu
from jax.sharding import PartitionSpec as P

VMEM = pltpu.VMEM
SMEM = pltpu.SMEM
TILE = 16
SUB = 8
MARK = 128
FAR = 3
PARAMS = pltpu.CompilerParams(vmem_limit_bytes=48 * 1024 * 1024)


PAIR_ORDER = (2, 3, 1)
SUM_ORDER = (3, 1, 2)
GATHER_ORDER = (3, 1, 2)
ROW_ORDER = (2, 1, 3)


def swapped(value, axis, mask):
    count = lax.axis_size(axis)
    return lax.ppermute(value, axis, [(source, source ^ mask) for source in range(count)])


def in_hbm(*values):
    return [pltpu.with_memory_space_constraint(value, pltpu.HBM) for value in values]


def whole(count):
    return [pl.BlockSpec(memory_space=VMEM)] * count


def half_first(ints, block_ids, occ_pick, occ_coef, count, n_aux, n_pair):
    slots, width, _, aux_rows = ints.shape
    blocks, _, nocc = occ_coef.shape
    n_half = n_aux // 2
    pairs = n_half // n_pair
    rows = 2 * pairs * count * width

    def kernel(ids_hbm, pick_hbm, occ_hbm, ints_hbm, *refs):
        outs, chosen_ref, tables_ref = refs[:n_pair], refs[n_pair], refs[n_pair + 1]
        ids_ref, pick_ref, occ_ref, held, small, large = refs[n_pair + 2 :]
        tables = [
            pltpu.make_async_copy(source, target, small.at[at])
            for at, (source, target) in enumerate(((ids_hbm, ids_ref), (pick_hbm, pick_ref), (occ_hbm, occ_ref)))
        ]
        for copy in tables:
            copy.start()
        copies = started(ints_hbm, held, large, 0, count, width * width)
        for copy in tables:
            copy.wait()
        pair_at = lax.axis_index("pair")
        lane = lax.broadcasted_iota(jnp.int32, (SUB, nocc), 1)
        chosen = []
        for mate in range(n_pair):
            for pair in range(pairs):
                for side in range(2):
                    orbital = pick_ref[(pair_at ^ mate) * pairs + pair + side * n_half]
                    chosen.append(jnp.where(lane == orbital, 1.0, 0.0))
        chosen = jnp.concatenate(chosen, axis=0).astype(jnp.bfloat16)
        weights = [slot_weights(chosen, occ_ref[ids_ref[1, slot]]) for slot in range(count)]
        row = lax.broadcasted_iota(jnp.int32, (TILE, aux_rows), 0)
        blocks = jnp.zeros((TILE, aux_rows), jnp.float32)
        for slot in range(slots):
            blocks = jnp.where(row == slot, ids_ref[0, slot].astype(jnp.float32), blocks)
        for out in outs[:FAR]:
            out[pl.ds(rows, TILE), :] = blocks.astype(jnp.bfloat16)
        chosen_ref[...] = chosen
        for slot in range(count, slots):
            tables_ref[slot - count] = occ_ref[ids_ref[1, slot]]
        for slot in range(count):
            copies[slot].wait()
            halves(weights[slot], held, outs, slot, count, width, pairs)

    return pl.pallas_call(
        kernel,
        in_specs=[pl.BlockSpec(memory_space=pltpu.HBM)] * 4,
        out_specs=whole(n_pair + 2),
        out_shape=[jax.ShapeDtypeStruct((rows + TILE * (mate < FAR), aux_rows), jnp.bfloat16) for mate in range(n_pair)]
        + [
            jax.ShapeDtypeStruct((n_aux * SUB, nocc), jnp.bfloat16),
            jax.ShapeDtypeStruct((slots - count, width, nocc), jnp.bfloat16),
        ],
        scratch_shapes=[
            SMEM((2, slots), jnp.int32),
            SMEM((nocc,), jnp.int32),
            VMEM(occ_coef.shape, jnp.bfloat16),
            VMEM((count * width * width, aux_rows), jnp.bfloat16),
            pltpu.SemaphoreType.DMA((3,)),
            pltpu.SemaphoreType.DMA((count,)),
        ],
        compiler_params=PARAMS,
        name="half_first",
    )(*in_hbm(block_ids.T, occ_pick, occ_coef, ints.reshape(-1, aux_rows)))


def started(ints_hbm, held, sems, first, count, rows):
    copies = []
    for slot in range(count):
        source = ints_hbm.at[pl.ds((first + slot) * rows, rows), :]
        copies.append(pltpu.make_async_copy(source, held.at[pl.ds(slot * rows, rows), :], sems.at[slot]))
        copies[-1].start()
    return copies


def slot_weights(chosen, table):
    width = table.shape[0]
    table = jnp.concatenate([table] * (128 // width), axis=0)
    spread = lax.dot_general(chosen, table, (((1,), (1,)), ((), ())), preferred_element_type=jnp.float32)
    spread = jnp.concatenate([spread] * (SUB * width // 128), axis=1)
    row = lax.broadcasted_iota(jnp.int32, spread.shape, 0)
    column = lax.broadcasted_iota(jnp.int32, spread.shape, 1)
    return jnp.where(row % SUB == column // width, spread, 0.0).astype(jnp.bfloat16)


def halves(weights, ints, outs, slot, count, width, pairs):
    depth = SUB * width
    for step in range(width // TILE):
        at = slot * (width // TILE) + step
        made = [
            jnp.dot(weights, ints[pl.ds((2 * at + part) * depth, depth), :], preferred_element_type=jnp.float32)
            for part in range(2)
        ]
        for mate, out in enumerate(outs):
            for orbital in range(2 * pairs):
                source = (mate * 2 * pairs + orbital) * SUB
                both = jnp.concatenate([part[source : source + SUB] for part in made], axis=0)
                out[pl.ds(orbital * count * width + at * TILE, TILE), :] = both.astype(jnp.bfloat16)


def half_rest(ints, block_count, chosen, tables, n_pair, pairs):
    slots, width, _, aux_rows = ints.shape
    count = tables.shape[0]

    def kernel(count_ref, chosen_ref, tables_ref, ints_hbm, *refs):
        outs, (held, large) = refs[:n_pair], refs[n_pair:]
        copies = started(ints_hbm, held, large, slots - count, count, width * width)
        weights = [slot_weights(chosen_ref[...], tables_ref[slot]) for slot in range(count)]
        for slot in range(count):
            copies[slot].wait()
            halves(weights[slot], held, outs, slot, count, width, pairs)
        live = count_ref[0]
        mark = jnp.full((TILE, aux_rows), (MARK * (live + 1)).astype(jnp.float32), jnp.float32).astype(jnp.bfloat16)
        for out in outs:
            spot = pl.ds((count - 1) * width, TILE)
            out[spot, :] = jnp.where(live < slots, mark, out[spot, :])

    return pl.pallas_call(
        kernel,
        in_specs=[pl.BlockSpec(memory_space=SMEM)] + whole(2) + [pl.BlockSpec(memory_space=pltpu.HBM)],
        out_specs=whole(n_pair),
        out_shape=[jax.ShapeDtypeStruct((2 * pairs * count * width, aux_rows), jnp.bfloat16)] * n_pair,
        scratch_shapes=[
            VMEM((count * width * width, aux_rows), jnp.bfloat16),
            pltpu.SemaphoreType.DMA((count,)),
        ],
        compiler_params=PARAMS,
        name="half_rest",
    )(block_count, chosen, tables, *in_hbm(ints.reshape(-1, aux_rows)))


def fitted_first(vir_coef, parts, names, pairs, counts):
    aux_rows = parts[0].shape[1]
    width, virtual = vir_coef.shape[1], vir_coef.shape[2]
    span = counts[0] * width
    rest_rows = (sum(counts) - 1) * width

    def kernel(vir_ref, names_ref, *refs):
        held, (fitted_ref, rest_ref, last_ref, own_ref) = refs[: len(parts)], refs[len(parts) :]
        first, rest = [], []
        for at, part in enumerate(held):
            tail = names_ref[...] if at + 1 == len(held) else part[pl.ds(2 * pairs * span, TILE), :]
            tail = tail[:, :128].astype(jnp.float32)
            found = [vir_ref[tail[slot, 0].astype(jnp.int32)] for slot in range(sum(counts))]
            first.append(found[0])
            rest.append(jnp.concatenate(found[1:], axis=0))
        own_ref[...] = jnp.concatenate(first, axis=0).T
        rest_ref[...] = jnp.concatenate(rest[:-1], axis=0).T
        last_ref[...] = rest[-1].T
        for orbital in range(2 * pairs):
            blocks = jnp.concatenate([part[pl.ds(orbital * span, width), :] for part in held], axis=0)
            fitted_ref[orbital] = jnp.dot(own_ref[...], blocks, preferred_element_type=jnp.float32)

    return pl.pallas_call(
        kernel,
        in_specs=whole(2 + len(parts)),
        out_specs=whole(3),
        out_shape=[
            jax.ShapeDtypeStruct((2 * pairs, virtual, aux_rows), jnp.float32),
            jax.ShapeDtypeStruct((virtual, (len(parts) - 1) * rest_rows), jnp.bfloat16),
            jax.ShapeDtypeStruct((virtual, rest_rows), jnp.bfloat16),
        ],
        scratch_shapes=[VMEM((virtual, len(parts) * width), jnp.bfloat16)],
        compiler_params=PARAMS,
        name="fitted_first",
    )(vir_coef, names, *parts)


def live_slots(later, counts, width):
    mark = later[pl.ds((counts[1] - 1) * width, TILE), :][:, :128].astype(jnp.float32)[0, 0]
    return jnp.where(mark < MARK, sum(counts), (mark * (1.0 / MARK)).astype(jnp.int32) - 1)


def live_blocks(first, later, live, orbital, counts, width):
    blocks = []
    for slot in range(1, sum(counts)):
        chunk = int(slot >= counts[0])
        at = (orbital * counts[chunk] + slot - chunk * counts[0]) * width
        block = (first, later)[chunk][pl.ds(at, width), :]
        blocks.append(jnp.where(slot < live, block, jnp.zeros_like(block)))
    return blocks


def fitted_more(fitted, rest, first, later, counts, width):
    count = len(first)

    def kernel(fitted_ref, rest_ref, *refs):
        held, out_ref = list(zip(refs[:count], refs[count : 2 * count])), refs[-1]
        live = [live_slots(part[1], counts, width) for part in held]
        for orbital in range(fitted.shape[0]):
            blocks = []
            for part, alive in zip(held, live):
                blocks += live_blocks(*part, alive, orbital, counts, width)
            total = jnp.dot(rest_ref[...], jnp.concatenate(blocks, axis=0), preferred_element_type=jnp.float32)
            out_ref[orbital] = fitted_ref[orbital] + total

    return pl.pallas_call(
        kernel,
        in_specs=whole(2 + 2 * count),
        out_specs=pl.BlockSpec(memory_space=VMEM),
        out_shape=jax.ShapeDtypeStruct(fitted.shape, fitted.dtype),
        compiler_params=PARAMS,
        name="fitted_more",
    )(fitted, rest, *first, *later)


def coulomb_parts(fitted, last, first, later, pairs, counts, width, quad):
    virtual = fitted.shape[1]
    share = virtual // quad

    def kernel(fitted_ref, last_ref, first_ref, later_ref, *refs):
        outs, block_ref = refs[:-1], refs[-1]
        place = lax.axis_index("aux") % quad
        live = live_slots(later_ref, counts, width)
        for pair in range(pairs):
            sides = []
            for orbital in (2 * pair, 2 * pair + 1):
                blocks = jnp.concatenate(live_blocks(first_ref, later_ref, live, orbital, counts, width), axis=0)
                total = jnp.dot(last_ref[...], blocks, preferred_element_type=jnp.float32)
                sides.append((fitted_ref[orbital] + total).astype(jnp.bfloat16))
            block = lax.dot_general(*sides, (((1,), (1,)), ((), ())), preferred_element_type=jnp.float32)
            block_ref[...] = block.astype(jnp.bfloat16)
            for part, out in enumerate(outs):
                at = pl.multiple_of((place ^ part) * share, share)
                out[pair] = block_ref[pl.ds(at, share), :]

    return pl.pallas_call(
        kernel,
        in_specs=whole(4),
        out_specs=whole(quad),
        out_shape=[jax.ShapeDtypeStruct((pairs, share, virtual), jnp.bfloat16)] * quad,
        scratch_shapes=[VMEM((virtual, virtual), jnp.bfloat16)],
        compiler_params=PARAMS,
        name="coulomb_parts",
    )(fitted, last, first, later)


def density_parts(inverse, chunks, n_pair):
    quad = len(chunks)
    pairs, share, virtual = chunks[0].shape
    rows = virtual // n_pair

    def kernel(inverse_ref, *refs):
        held, own_ref, outs = refs[:quad], refs[quad], refs[quad + 1 : quad + n_pair]
        energy_ref, block_ref, total_ref = refs[quad + n_pair :]
        place = lax.axis_index("aux") % quad
        pair_at = lax.axis_index("pair")
        lane = lax.broadcasted_iota(jnp.int32, (1, virtual), 1)
        energies = []
        totals = [None] * n_pair
        for pair in range(pairs):
            for part, chunk in zip((0, *GATHER_ORDER), held):
                at = pl.multiple_of((place ^ part) * share, share)
                block_ref[pl.ds(at, share), :] = chunk[pair]
            block = block_ref[...].astype(jnp.float32)
            flipped = block_ref[...].T.astype(jnp.float32)
            inverse = inverse_ref[pair]
            energies.append(jnp.sum(block * (2.0 * block - flipped) * inverse))
            even = ((block + flipped) * inverse).astype(jnp.bfloat16)
            odd = ((block - flipped) * (inverse * 3.0**0.5)).astype(jnp.bfloat16)
            left = jnp.concatenate([even, odd], axis=1)
            right = jnp.concatenate([even, -odd], axis=0)
            term = 0.5 * jnp.dot(left, right, preferred_element_type=jnp.float32)
            total_ref[...] = term if pair == 0 else total_ref[...] + term
        for part in range(n_pair):
            totals[part] = total_ref[pl.ds(pl.multiple_of((pair_at ^ part) * rows, rows), rows), :]
        own_ref[...] = totals[0]
        energy_ref[...] = jnp.zeros_like(energy_ref)
        for pair, energy in enumerate(energies):
            energy_ref[...] = jnp.where(lane == pair, energy, energy_ref[...])
        for part in range(1, n_pair):
            outs[part - 1][...] = totals[part].astype(jnp.bfloat16)
            first = (pair_at ^ part) * rows
            last = totals[part][rows - TILE :]
            row = lax.broadcasted_iota(jnp.int32, (TILE, virtual), 0)
            corner = jnp.zeros((1, virtual), jnp.float32)
            for pair, energy in enumerate(energies):
                rest = jnp.full((1, virtual), energy, jnp.float32)
                for at in range(3):
                    piece = rest.astype(jnp.bfloat16).astype(jnp.float32)
                    corner = jnp.where(lane == first + 3 * pair + at, piece, corner)
                    rest = rest - piece
            inside = (lane >= first) & (lane < first + 3 * pairs) & (row == TILE - 1)
            outs[part - 1][pl.ds(rows - TILE, TILE), :] = jnp.where(inside, corner, last).astype(jnp.bfloat16)

    return pl.pallas_call(
        kernel,
        in_specs=whole(1 + quad),
        out_specs=whole(n_pair + 1),
        out_shape=[jax.ShapeDtypeStruct((rows, virtual), jnp.float32)]
        + [jax.ShapeDtypeStruct((rows, virtual), jnp.bfloat16)] * (n_pair - 1)
        + [jax.ShapeDtypeStruct((1, virtual), jnp.float32)],
        scratch_shapes=[
            VMEM((virtual, virtual), jnp.bfloat16),
            VMEM((virtual, virtual), jnp.float32),
        ],
        compiler_params=PARAMS,
        name="density_parts",
    )(inverse, *chunks)


def closing(own, energies, others, pairs, n_half):
    rows, virtual = own.shape

    def kernel(own_ref, energy_ref, *refs):
        held, (density_ref, value_ref) = refs[: len(others)], refs[len(others) :]
        wanted = lax.axis_index("aux") % n_half
        pair_at = lax.axis_index("pair")
        lane = lax.broadcasted_iota(jnp.int32, (1, virtual), 1)
        first = pair_at * rows
        found = jnp.zeros((1, virtual), jnp.float32)
        total = own_ref[...]
        for mate, ref in zip((0, *ROW_ORDER), (None, *held)):
            at = wanted - (pair_at ^ mate) * pairs
            here = (at >= 0) & (at < pairs)
            if mate == 0:
                found += jnp.where(here & (lane == at), energy_ref[...], 0.0)
            else:
                part = ref[...].astype(jnp.float32)
                spot = lane - first - 3 * at
                found += jnp.where(here & (spot >= 0) & (spot < 3), part[rows - 1 :], 0.0)
                total += part
        value_ref[...] = jnp.sum(found, axis=1, keepdims=True)
        density_ref[...] = total
        head = -(-3 * pairs // TILE) * TILE
        top = total[:head]
        wide = lax.broadcasted_iota(jnp.int32, (head, virtual), 1)
        row = lax.broadcasted_iota(jnp.int32, (head, virtual), 0)
        column = jnp.sum(jnp.where(wide == first + rows - 1, top, 0.0), axis=1, keepdims=True)
        turned = jnp.sum(jnp.where(wide == first + row, column, 0.0), axis=0, keepdims=True)
        last = total[rows - SUB :]
        inside = (lane >= first) & (lane < first + 3 * pairs)
        inside = inside & (lax.broadcasted_iota(jnp.int32, (SUB, virtual), 0) == SUB - 1)
        density_ref[pl.ds(rows - SUB, SUB), :] = jnp.where(inside, turned, last)

    return pl.pallas_call(
        kernel,
        in_specs=whole(2 + len(others)),
        out_specs=whole(2),
        out_shape=[jax.ShapeDtypeStruct((rows, virtual), jnp.float32), jax.ShapeDtypeStruct((1, 1), jnp.float32)],
        compiler_params=PARAMS,
        name="closing",
    )(own, energies, *others)


def exchanged(parts, axis, order, low=0):
    return [swapped(parts[d], axis, d << low) for d in order]


def summed(value, axis, low, bits):
    if bits == 0:
        return value
    if bits == 1:
        other = swapped(value, axis, 1 << low)
        return (value.astype(jnp.float32) + other.astype(jnp.float32)).astype(jnp.bfloat16)
    place = (lax.axis_index(axis) >> low) & 3
    share = value.shape[1] // 4
    parts = [lax.dynamic_slice_in_dim(value, (place ^ d) * share, share, 1) for d in range(4)]
    chunks = scattered(parts, axis, low, bits)
    out = jnp.zeros_like(value)
    for d, chunk in zip((0, *GATHER_ORDER), chunks):
        out = lax.dynamic_update_slice_in_dim(out, chunk, (place ^ d) * share, 1)
    return out


def scattered(parts, axis, low, bits):
    total = parts[0].astype(jnp.float32)
    for part in exchanged(parts, axis, SUM_ORDER, low):
        total += part.astype(jnp.float32)
    total = summed(total.astype(jnp.bfloat16), axis, low + 2, bits - 2)
    return [total] + exchanged([total] * len(parts), axis, GATHER_ORDER, low)


def per_device(
    shell_ints, block_ids, block_count, occ_coef, occ_pick, vir_coef, occ_energy, vir_energy
):
    _, slots, width, _ = shell_ints.shape
    n_aux = lax.axis_size("aux")
    n_pair = lax.axis_size("pair")
    n_half = n_aux // 2
    pairs = n_half // n_pair
    bits = n_aux.bit_length() - 1

    ints = jnp.transpose(shell_ints, (1, 2, 3, 0))
    counts = (slots // 2, slots - slots // 2)
    *first, chosen, tables = half_first(
        ints, block_ids, occ_pick, occ_coef, counts[0], n_aux, n_pair
    )
    block_count, _ = lax.optimization_barrier((block_count, first[0]))
    later = list(half_rest(ints, block_count, chosen, tables, n_pair, pairs))
    got = [made[:1] + exchanged(made, "pair", PAIR_ORDER) for made in (first, later)]

    slowest = 1 + PAIR_ORDER.index(max(PAIR_ORDER))
    ends = [group.pop(slowest) for group in got]
    near = got[0][1 + [d for d in PAIR_ORDER if d != FAR].index(FAR ^ 1)]
    names = swapped(near[-TILE:], "pair", 1)
    fitted, rest, last = fitted_first(vir_coef, got[0] + ends[:1], names, pairs, counts)
    fitted = fitted_more(fitted, rest, *got, counts, width)
    parts = coulomb_parts(fitted, last, *ends, pairs, counts, width, 4)

    occ_pick, occ_energy, vir_energy, _ = lax.optimization_barrier((occ_pick, occ_energy, vir_energy, later[0]))
    own_pairs = lax.axis_index("pair") * pairs + jnp.arange(pairs, dtype=jnp.int32)
    spots = jnp.arange(n_aux, dtype=jnp.int32)
    batch = occ_pick[:n_aux]
    orbitals = jnp.arange(occ_energy.shape[0], dtype=jnp.int32)
    energies = jnp.sum(jnp.where(batch[:, None] == orbitals[None, :], occ_energy[None, :], 0.0), axis=1)
    levels = jnp.sum(jnp.where(own_pairs[:, None] == spots[None, :] % n_half, energies[None, :], 0.0), axis=1)
    inverse = 1.0 / (levels[:, None, None] - vir_energy[None, :, None] - vir_energy[None, None, :])

    chunks = scattered(parts, "aux", 0, bits)
    outs = density_parts(inverse, chunks, n_pair)
    others = exchanged(outs, "pair", ROW_ORDER)
    density, energy = closing(outs[0], outs[-1], others, pairs, n_half)
    return (energy.reshape(1), density)


def solution(mesh):
    placed = (P("aux", "pair", None, None), P("pair", None), P("pair"), P(), P(), P(), P(), P())
    return jax.shard_map(
        per_device,
        mesh=mesh,
        in_specs=placed,
        out_specs=(P("aux"), P("pair", None)),
        check_vma=False,
    )
```

```python
import jax
import jax.numpy as jnp
from jax import lax
from jax.experimental import pallas as pl
from jax.experimental.pallas import tpu as pltpu
from jax.sharding import PartitionSpec as P

VMEM = pltpu.VMEM
SMEM = pltpu.SMEM
TILE = 16
SUB = 8
MARK = 128
PARAMS = pltpu.CompilerParams(vmem_limit_bytes=48 * 1024 * 1024)


PAIR_ORDER = (2, 3, 1)
SUM_ORDER = (3, 1, 2)
GATHER_ORDER = (3, 1, 2)
ROW_ORDER = (2, 1, 3)


def swapped(value, axis, mask):
    count = lax.axis_size(axis)
    return lax.ppermute(value, axis, [(source, source ^ mask) for source in range(count)])


def in_hbm(*values):
    return [pltpu.with_memory_space_constraint(value, pltpu.HBM) for value in values]


def whole(count):
    return [pl.BlockSpec(memory_space=VMEM)] * count


def half_first(ints, block_ids, occ_pick, occ_coef, count, n_aux, n_pair):
    slots, width, _, aux_rows = ints.shape
    blocks, _, nocc = occ_coef.shape
    n_half = n_aux // 2
    pairs = n_half // n_pair
    rows = 2 * pairs * count * width

    def kernel(ids_hbm, pick_hbm, occ_hbm, ints_hbm, *refs):
        outs, chosen_ref, tables_ref = refs[:n_pair], refs[n_pair], refs[n_pair + 1]
        ids_ref, pick_ref, occ_ref, held, small, large = refs[n_pair + 2 :]
        tables = [
            pltpu.make_async_copy(source, target, small.at[at])
            for at, (source, target) in enumerate(((ids_hbm, ids_ref), (pick_hbm, pick_ref), (occ_hbm, occ_ref)))
        ]
        for copy in tables:
            copy.start()
        copies = started(ints_hbm, held, large, 0, count, width * width)
        for copy in tables:
            copy.wait()
        pair_at = lax.axis_index("pair")
        lane = lax.broadcasted_iota(jnp.int32, (SUB, nocc), 1)
        chosen = []
        for mate in range(n_pair):
            for pair in range(pairs):
                for side in range(2):
                    orbital = pick_ref[(pair_at ^ mate) * pairs + pair + side * n_half]
                    chosen.append(jnp.where(lane == orbital, 1.0, 0.0))
        chosen = jnp.concatenate(chosen, axis=0).astype(jnp.bfloat16)
        weights = [slot_weights(chosen, occ_ref[ids_ref[1, slot]]) for slot in range(count)]
        row = lax.broadcasted_iota(jnp.int32, (TILE, aux_rows), 0)
        blocks = jnp.zeros((TILE, aux_rows), jnp.float32)
        for slot in range(slots):
            blocks = jnp.where(row == slot, ids_ref[0, slot].astype(jnp.float32), blocks)
        for out in outs:
            out[pl.ds(rows, TILE), :] = blocks.astype(jnp.bfloat16)
        chosen_ref[...] = chosen
        for slot in range(count, slots):
            tables_ref[slot - count] = occ_ref[ids_ref[1, slot]]
        for slot in range(count):
            copies[slot].wait()
            halves(weights[slot], held, outs, slot, count, width, pairs)

    return pl.pallas_call(
        kernel,
        in_specs=[pl.BlockSpec(memory_space=pltpu.HBM)] * 4,
        out_specs=whole(n_pair + 2),
        out_shape=[jax.ShapeDtypeStruct((rows + TILE, aux_rows), jnp.bfloat16)] * n_pair
        + [
            jax.ShapeDtypeStruct((n_aux * SUB, nocc), jnp.bfloat16),
            jax.ShapeDtypeStruct((slots - count, width, nocc), jnp.bfloat16),
        ],
        scratch_shapes=[
            SMEM((2, slots), jnp.int32),
            SMEM((nocc,), jnp.int32),
            VMEM(occ_coef.shape, jnp.bfloat16),
            VMEM((count * width * width, aux_rows), jnp.bfloat16),
            pltpu.SemaphoreType.DMA((3,)),
            pltpu.SemaphoreType.DMA((count,)),
        ],
        compiler_params=PARAMS,
        name="half_first",
    )(*in_hbm(block_ids.T, occ_pick, occ_coef, ints.reshape(-1, aux_rows)))


def started(ints_hbm, held, sems, first, count, rows):
    copies = []
    for slot in range(count):
        source = ints_hbm.at[pl.ds((first + slot) * rows, rows), :]
        copies.append(pltpu.make_async_copy(source, held.at[pl.ds(slot * rows, rows), :], sems.at[slot]))
        copies[-1].start()
    return copies


def slot_weights(chosen, table):
    width = table.shape[0]
    table = jnp.concatenate([table] * (128 // width), axis=0)
    spread = lax.dot_general(chosen, table, (((1,), (1,)), ((), ())), preferred_element_type=jnp.float32)
    spread = jnp.concatenate([spread] * (SUB * width // 128), axis=1)
    row = lax.broadcasted_iota(jnp.int32, spread.shape, 0)
    column = lax.broadcasted_iota(jnp.int32, spread.shape, 1)
    return jnp.where(row % SUB == column // width, spread, 0.0).astype(jnp.bfloat16)


def halves(weights, ints, outs, slot, count, width, pairs):
    depth = SUB * width
    for step in range(width // TILE):
        at = slot * (width // TILE) + step
        made = [
            jnp.dot(weights, ints[pl.ds((2 * at + part) * depth, depth), :], preferred_element_type=jnp.float32)
            for part in range(2)
        ]
        for mate, out in enumerate(outs):
            for orbital in range(2 * pairs):
                source = (mate * 2 * pairs + orbital) * SUB
                both = jnp.concatenate([part[source : source + SUB] for part in made], axis=0)
                out[pl.ds(orbital * count * width + at * TILE, TILE), :] = both.astype(jnp.bfloat16)


def half_rest(ints, block_count, chosen, tables, n_pair, pairs):
    slots, width, _, aux_rows = ints.shape
    count = tables.shape[0]

    def kernel(count_ref, chosen_ref, tables_ref, ints_hbm, *refs):
        outs, (held, large) = refs[:n_pair], refs[n_pair:]
        copies = started(ints_hbm, held, large, slots - count, count, width * width)
        weights = [slot_weights(chosen_ref[...], tables_ref[slot]) for slot in range(count)]
        for slot in range(count):
            copies[slot].wait()
            halves(weights[slot], held, outs, slot, count, width, pairs)
        live = count_ref[0]
        mark = jnp.full((TILE, aux_rows), (MARK * (live + 1)).astype(jnp.float32), jnp.float32).astype(jnp.bfloat16)
        for out in outs:
            spot = pl.ds((count - 1) * width, TILE)
            out[spot, :] = jnp.where(live < slots, mark, out[spot, :])

    return pl.pallas_call(
        kernel,
        in_specs=[pl.BlockSpec(memory_space=SMEM)] + whole(2) + [pl.BlockSpec(memory_space=pltpu.HBM)],
        out_specs=whole(n_pair),
        out_shape=[jax.ShapeDtypeStruct((2 * pairs * count * width, aux_rows), jnp.bfloat16)] * n_pair,
        scratch_shapes=[
            VMEM((count * width * width, aux_rows), jnp.bfloat16),
            pltpu.SemaphoreType.DMA((count,)),
        ],
        compiler_params=PARAMS,
        name="half_rest",
    )(block_count, chosen, tables, *in_hbm(ints.reshape(-1, aux_rows)))


def fitted_first(vir_coef, parts, pairs, counts):
    aux_rows = parts[0].shape[1]
    width, virtual = vir_coef.shape[1], vir_coef.shape[2]
    span = counts[0] * width
    rest_rows = (sum(counts) - 1) * width

    def kernel(vir_ref, *refs):
        held, (fitted_ref, rest_ref, last_ref, own_ref) = refs[: len(parts)], refs[len(parts) :]
        first, rest = [], []
        for part in held:
            tail = part[pl.ds(2 * pairs * span, TILE), :][:, :128].astype(jnp.float32)
            found = [vir_ref[tail[slot, 0].astype(jnp.int32)] for slot in range(sum(counts))]
            first.append(found[0])
            rest.append(jnp.concatenate(found[1:], axis=0))
        own_ref[...] = jnp.concatenate(first, axis=0).T
        rest_ref[...] = jnp.concatenate(rest[:-1], axis=0).T
        last_ref[...] = rest[-1].T
        for orbital in range(2 * pairs):
            blocks = jnp.concatenate([part[pl.ds(orbital * span, width), :] for part in held], axis=0)
            fitted_ref[orbital] = jnp.dot(own_ref[...], blocks, preferred_element_type=jnp.float32)

    return pl.pallas_call(
        kernel,
        in_specs=whole(1 + len(parts)),
        out_specs=whole(3),
        out_shape=[
            jax.ShapeDtypeStruct((2 * pairs, virtual, aux_rows), jnp.float32),
            jax.ShapeDtypeStruct((virtual, (len(parts) - 1) * rest_rows), jnp.bfloat16),
            jax.ShapeDtypeStruct((virtual, rest_rows), jnp.bfloat16),
        ],
        scratch_shapes=[VMEM((virtual, len(parts) * width), jnp.bfloat16)],
        compiler_params=PARAMS,
        name="fitted_first",
    )(vir_coef, *parts)


def live_slots(later, counts, width):
    mark = later[pl.ds((counts[1] - 1) * width, TILE), :][:, :128].astype(jnp.float32)[0, 0]
    return jnp.where(mark < MARK, sum(counts), (mark * (1.0 / MARK)).astype(jnp.int32) - 1)


def live_blocks(first, later, live, orbital, counts, width):
    blocks = []
    for slot in range(1, sum(counts)):
        chunk = int(slot >= counts[0])
        at = (orbital * counts[chunk] + slot - chunk * counts[0]) * width
        block = (first, later)[chunk][pl.ds(at, width), :]
        blocks.append(jnp.where(slot < live, block, jnp.zeros_like(block)))
    return blocks


def fitted_more(fitted, rest, first, later, counts, width):
    count = len(first)

    def kernel(fitted_ref, rest_ref, *refs):
        held, out_ref = list(zip(refs[:count], refs[count : 2 * count])), refs[-1]
        live = [live_slots(part[1], counts, width) for part in held]
        for orbital in range(fitted.shape[0]):
            blocks = []
            for part, alive in zip(held, live):
                blocks += live_blocks(*part, alive, orbital, counts, width)
            total = jnp.dot(rest_ref[...], jnp.concatenate(blocks, axis=0), preferred_element_type=jnp.float32)
            out_ref[orbital] = fitted_ref[orbital] + total

    return pl.pallas_call(
        kernel,
        in_specs=whole(2 + 2 * count),
        out_specs=pl.BlockSpec(memory_space=VMEM),
        out_shape=jax.ShapeDtypeStruct(fitted.shape, fitted.dtype),
        compiler_params=PARAMS,
        name="fitted_more",
    )(fitted, rest, *first, *later)


def coulomb_parts(fitted, last, first, later, pairs, counts, width, quad):
    virtual = fitted.shape[1]
    share = virtual // quad

    def kernel(fitted_ref, last_ref, first_ref, later_ref, *refs):
        outs, left_ref = refs[:-1], refs[-1]
        place = lax.axis_index("aux") % quad
        live = live_slots(later_ref, counts, width)
        for pair in range(pairs):
            sides = []
            for orbital in (2 * pair, 2 * pair + 1):
                blocks = jnp.concatenate(live_blocks(first_ref, later_ref, live, orbital, counts, width), axis=0)
                total = jnp.dot(last_ref[...], blocks, preferred_element_type=jnp.float32)
                sides.append((fitted_ref[orbital] + total).astype(jnp.bfloat16))
            left_ref[...] = sides[0]
            left = [left_ref[pl.ds(pl.multiple_of((place ^ part) * share, share), share), :] for part in range(quad)]
            block = lax.dot_general(
                jnp.concatenate(left, axis=0), sides[1], (((1,), (1,)), ((), ())), preferred_element_type=jnp.float32
            )
            for part, out in enumerate(outs):
                out[pair] = block[part * share : (part + 1) * share].astype(jnp.bfloat16)

    return pl.pallas_call(
        kernel,
        in_specs=whole(4),
        out_specs=whole(quad),
        out_shape=[jax.ShapeDtypeStruct((pairs, share, virtual), jnp.bfloat16)] * quad,
        scratch_shapes=[VMEM(fitted.shape[1:], jnp.bfloat16)],
        compiler_params=PARAMS,
        name="coulomb_parts",
    )(fitted, last, first, later)


def density_parts(inverse, chunks, n_pair):
    quad = len(chunks)
    pairs, share, virtual = chunks[0].shape
    rows = virtual // n_pair

    def kernel(inverse_ref, *refs):
        held, own_ref, outs = refs[:quad], refs[quad], refs[quad + 1 : quad + n_pair]
        energy_ref, block_ref, left_ref = refs[quad + n_pair :]
        place = lax.axis_index("aux") % quad
        pair_at = lax.axis_index("pair")
        lane = lax.broadcasted_iota(jnp.int32, (1, virtual), 1)
        energies = []
        totals = [None] * n_pair
        for pair in range(pairs):
            for part, chunk in zip((0, *GATHER_ORDER), held):
                at = pl.multiple_of((place ^ part) * share, share)
                block_ref[pl.ds(at, share), :] = chunk[pair]
            block = block_ref[...].astype(jnp.float32)
            flipped = block_ref[...].T.astype(jnp.float32)
            inverse = inverse_ref[pair]
            energies.append(jnp.sum(block * (2.0 * block - flipped) * inverse))
            even = ((block + flipped) * inverse).astype(jnp.bfloat16)
            odd = ((block - flipped) * (inverse * 3.0**0.5)).astype(jnp.bfloat16)
            left_ref[...] = jnp.concatenate([even, odd], axis=1)
            left = [left_ref[pl.ds(pl.multiple_of((pair_at ^ part) * rows, rows), rows), :] for part in range(n_pair)]
            right = jnp.concatenate([even, -odd], axis=0)
            term = 0.5 * jnp.dot(jnp.concatenate(left, axis=0), right, preferred_element_type=jnp.float32)
            for part in range(n_pair):
                piece = term[part * rows : (part + 1) * rows]
                totals[part] = piece if pair == 0 else totals[part] + piece
        own_ref[...] = totals[0]
        energy_ref[...] = jnp.zeros_like(energy_ref)
        for pair, energy in enumerate(energies):
            energy_ref[...] = jnp.where(lane == pair, energy, energy_ref[...])
        for part in range(1, n_pair):
            outs[part - 1][...] = totals[part].astype(jnp.bfloat16)
            first = (pair_at ^ part) * rows
            last = totals[part][rows - TILE :]
            row = lax.broadcasted_iota(jnp.int32, (TILE, virtual), 0)
            corner = jnp.zeros((1, virtual), jnp.float32)
            for pair, energy in enumerate(energies):
                rest = jnp.full((1, virtual), energy, jnp.float32)
                for at in range(3):
                    piece = rest.astype(jnp.bfloat16).astype(jnp.float32)
                    corner = jnp.where(lane == first + 3 * pair + at, piece, corner)
                    rest = rest - piece
            inside = (lane >= first) & (lane < first + 3 * pairs) & (row == TILE - 1)
            outs[part - 1][pl.ds(rows - TILE, TILE), :] = jnp.where(inside, corner, last).astype(jnp.bfloat16)

    return pl.pallas_call(
        kernel,
        in_specs=whole(1 + quad),
        out_specs=whole(n_pair + 1),
        out_shape=[jax.ShapeDtypeStruct((rows, virtual), jnp.float32)]
        + [jax.ShapeDtypeStruct((rows, virtual), jnp.bfloat16)] * (n_pair - 1)
        + [jax.ShapeDtypeStruct((1, virtual), jnp.float32)],
        scratch_shapes=[
            VMEM((virtual, virtual), jnp.bfloat16),
            VMEM((virtual, 2 * virtual), jnp.bfloat16),
        ],
        compiler_params=PARAMS,
        name="density_parts",
    )(inverse, *chunks)


def closing(own, energies, others, pairs, n_half):
    rows, virtual = own.shape

    def kernel(own_ref, energy_ref, *refs):
        held, (density_ref, value_ref) = refs[: len(others)], refs[len(others) :]
        wanted = lax.axis_index("aux") % n_half
        pair_at = lax.axis_index("pair")
        lane = lax.broadcasted_iota(jnp.int32, (1, virtual), 1)
        first = pair_at * rows
        found = jnp.zeros((1, virtual), jnp.float32)
        total = own_ref[...]
        for mate, ref in zip((0, *ROW_ORDER), (None, *held)):
            at = wanted - (pair_at ^ mate) * pairs
            here = (at >= 0) & (at < pairs)
            if mate == 0:
                found += jnp.where(here & (lane == at), energy_ref[...], 0.0)
            else:
                part = ref[...].astype(jnp.float32)
                spot = lane - first - 3 * at
                found += jnp.where(here & (spot >= 0) & (spot < 3), part[rows - 1 :], 0.0)
                total += part
        value_ref[...] = jnp.sum(found, axis=1, keepdims=True)
        density_ref[...] = total
        head = -(-3 * pairs // TILE) * TILE
        top = total[:head]
        wide = lax.broadcasted_iota(jnp.int32, (head, virtual), 1)
        row = lax.broadcasted_iota(jnp.int32, (head, virtual), 0)
        column = jnp.sum(jnp.where(wide == first + rows - 1, top, 0.0), axis=1, keepdims=True)
        turned = jnp.sum(jnp.where(wide == first + row, column, 0.0), axis=0, keepdims=True)
        last = total[rows - SUB :]
        inside = (lane >= first) & (lane < first + 3 * pairs)
        inside = inside & (lax.broadcasted_iota(jnp.int32, (SUB, virtual), 0) == SUB - 1)
        density_ref[pl.ds(rows - SUB, SUB), :] = jnp.where(inside, turned, last)

    return pl.pallas_call(
        kernel,
        in_specs=whole(2 + len(others)),
        out_specs=whole(2),
        out_shape=[jax.ShapeDtypeStruct((rows, virtual), jnp.float32), jax.ShapeDtypeStruct((1, 1), jnp.float32)],
        compiler_params=PARAMS,
        name="closing",
    )(own, energies, *others)


def exchanged(parts, axis, order, low=0):
    return [swapped(parts[d], axis, d << low) for d in order]


def summed(value, axis, low, bits):
    if bits == 0:
        return value
    if bits == 1:
        other = swapped(value, axis, 1 << low)
        return (value.astype(jnp.float32) + other.astype(jnp.float32)).astype(jnp.bfloat16)
    place = (lax.axis_index(axis) >> low) & 3
    share = value.shape[1] // 4
    parts = [lax.dynamic_slice_in_dim(value, (place ^ d) * share, share, 1) for d in range(4)]
    chunks = scattered(parts, axis, low, bits)
    out = jnp.zeros_like(value)
    for d, chunk in zip((0, *GATHER_ORDER), chunks):
        out = lax.dynamic_update_slice_in_dim(out, chunk, (place ^ d) * share, 1)
    return out


def scattered(parts, axis, low, bits):
    total = parts[0].astype(jnp.float32)
    for part in exchanged(parts, axis, SUM_ORDER, low):
        total += part.astype(jnp.float32)
    total = summed(total.astype(jnp.bfloat16), axis, low + 2, bits - 2)
    return [total] + exchanged([total] * len(parts), axis, GATHER_ORDER, low)


def per_device(
    shell_ints, block_ids, block_count, occ_coef, occ_pick, vir_coef, occ_energy, vir_energy
):
    _, slots, width, _ = shell_ints.shape
    n_aux = lax.axis_size("aux")
    n_pair = lax.axis_size("pair")
    n_half = n_aux // 2
    pairs = n_half // n_pair
    bits = n_aux.bit_length() - 1

    ints = jnp.transpose(shell_ints, (1, 2, 3, 0))
    counts = (slots // 2, slots - slots // 2)
    *first, chosen, tables = half_first(
        ints, block_ids, occ_pick, occ_coef, counts[0], n_aux, n_pair
    )
    block_count, _ = lax.optimization_barrier((block_count, first[0]))
    later = list(half_rest(ints, block_count, chosen, tables, n_pair, pairs))
    got = [made[:1] + exchanged(made, "pair", PAIR_ORDER) for made in (first, later)]

    slowest = 1 + PAIR_ORDER.index(max(PAIR_ORDER))
    ends = [group.pop(slowest) for group in got]
    fitted, rest, last = fitted_first(vir_coef, got[0] + ends[:1], pairs, counts)
    fitted = fitted_more(fitted, rest, *got, counts, width)
    parts = coulomb_parts(fitted, last, *ends, pairs, counts, width, 4)

    occ_pick, occ_energy, vir_energy, _ = lax.optimization_barrier((occ_pick, occ_energy, vir_energy, later[0]))
    own_pairs = lax.axis_index("pair") * pairs + jnp.arange(pairs, dtype=jnp.int32)
    spots = jnp.arange(n_aux, dtype=jnp.int32)
    batch = occ_pick[:n_aux]
    orbitals = jnp.arange(occ_energy.shape[0], dtype=jnp.int32)
    energies = jnp.sum(jnp.where(batch[:, None] == orbitals[None, :], occ_energy[None, :], 0.0), axis=1)
    levels = jnp.sum(jnp.where(own_pairs[:, None] == spots[None, :] % n_half, energies[None, :], 0.0), axis=1)
    inverse = 1.0 / (levels[:, None, None] - vir_energy[None, :, None] - vir_energy[None, None, :])

    chunks = scattered(parts, "aux", 0, bits)
    outs = density_parts(inverse, chunks, n_pair)
    others = exchanged(outs, "pair", ROW_ORDER)
    density, energy = closing(outs[0], outs[-1], others, pairs, n_half)
    return (energy.reshape(1), density)


def solution(mesh):
    placed = (P("aux", "pair", None, None), P("pair", None), P("pair"), P(), P(), P(), P(), P())
    return jax.shard_map(
        per_device,
        mesh=mesh,
        in_specs=placed,
        out_specs=(P("aux"), P("pair", None)),
        check_vma=False,
    )
```

```python
import jax
import jax.numpy as jnp
from jax import lax
from jax.experimental import pallas as pl
from jax.experimental.pallas import tpu as pltpu
from jax.sharding import PartitionSpec as P

VMEM = pltpu.VMEM
SMEM = pltpu.SMEM
TILE = 16
SUB = 8
MARK = 128
PARAMS = pltpu.CompilerParams(vmem_limit_bytes=48 * 1024 * 1024)


PAIR_ORDER = (2, 3, 1)
SUM_ORDER = (3, 1, 2)
GATHER_ORDER = (3, 1, 2)
ROW_ORDER = (2, 1, 3)


def swapped(value, axis, mask):
    count = lax.axis_size(axis)
    return lax.ppermute(value, axis, [(source, source ^ mask) for source in range(count)])


def in_hbm(*values):
    return [pltpu.with_memory_space_constraint(value, pltpu.HBM) for value in values]


def whole(count):
    return [pl.BlockSpec(memory_space=VMEM)] * count


def half_first(ints, block_ids, occ_pick, occ_coef, count, n_aux, n_pair):
    slots, width, _, aux_rows = ints.shape
    blocks, _, nocc = occ_coef.shape
    n_half = n_aux // 2
    pairs = n_half // n_pair
    rows = 2 * pairs * count * width

    def kernel(ids_hbm, pick_hbm, occ_hbm, ints_hbm, *refs):
        outs, chosen_ref, tables_ref = refs[:n_pair], refs[n_pair], refs[n_pair + 1]
        ids_ref, pick_ref, occ_ref, held, small, large = refs[n_pair + 2 :]
        names = [
            pltpu.make_async_copy(ids_hbm, ids_ref, small.at[slots]),
            pltpu.make_async_copy(pick_hbm, pick_ref, small.at[slots + 1]),
        ]
        for copy in names:
            copy.start()
        copies = []
        for slot in range(count):
            span = pl.ds(slot * width * width, width * width)
            copies.append(pltpu.make_async_copy(ints_hbm.at[span, :], held.at[span, :], large.at[slot]))
        copies[0].start()
        for copy in names:
            copy.wait()
        tables = []
        for slot in range(slots):
            target = occ_ref.at[slot] if slot < count else tables_ref.at[slot - count]
            tables.append(pltpu.make_async_copy(occ_hbm.at[ids_ref[1, slot]], target, small.at[slot]))
        for copy in tables[:count] + copies[1:] + tables[count:]:
            copy.start()
        pair_at = lax.axis_index("pair")
        lane = lax.broadcasted_iota(jnp.int32, (SUB, nocc), 1)
        chosen = []
        for mate in range(n_pair):
            for pair in range(pairs):
                for side in range(2):
                    orbital = pick_ref[(pair_at ^ mate) * pairs + pair + side * n_half]
                    chosen.append(jnp.where(lane == orbital, 1.0, 0.0))
        chosen = jnp.concatenate(chosen, axis=0).astype(jnp.bfloat16)
        for copy in tables[:count]:
            copy.wait()
        weights = slot_weights(chosen, occ_ref[0])
        for slot in range(count):
            copies[slot].wait()
            if slot + 1 < count:
                following = slot_weights(chosen, occ_ref[slot + 1])
            else:
                row = lax.broadcasted_iota(jnp.int32, (TILE, aux_rows), 0)
                blocks = jnp.zeros((TILE, aux_rows), jnp.float32)
                for at in range(slots):
                    blocks = jnp.where(row == at, ids_ref[0, at].astype(jnp.float32), blocks)
                for out in outs:
                    out[pl.ds(rows, TILE), :] = blocks.astype(jnp.bfloat16)
                chosen_ref[...] = chosen
            halves(weights, held, outs, slot, count, width, pairs)
            weights = following
        for copy in tables[count:]:
            copy.wait()

    return pl.pallas_call(
        kernel,
        in_specs=[pl.BlockSpec(memory_space=pltpu.HBM)] * 4,
        out_specs=whole(n_pair + 2),
        out_shape=[jax.ShapeDtypeStruct((rows + TILE, aux_rows), jnp.bfloat16)] * n_pair
        + [
            jax.ShapeDtypeStruct((n_aux * SUB, nocc), jnp.bfloat16),
            jax.ShapeDtypeStruct((slots - count, width, nocc), jnp.bfloat16),
        ],
        scratch_shapes=[
            SMEM((2, slots), jnp.int32),
            SMEM((nocc,), jnp.int32),
            VMEM((count, width, nocc), jnp.bfloat16),
            VMEM((count * width * width, aux_rows), jnp.bfloat16),
            pltpu.SemaphoreType.DMA((slots + 2,)),
            pltpu.SemaphoreType.DMA((count,)),
        ],
        compiler_params=PARAMS,
        name="half_first",
    )(*in_hbm(block_ids.T, occ_pick, occ_coef, ints.reshape(-1, aux_rows)))


def started(ints_hbm, held, sems, first, count, rows):
    copies = []
    for slot in range(count):
        source = ints_hbm.at[pl.ds((first + slot) * rows, rows), :]
        copies.append(pltpu.make_async_copy(source, held.at[pl.ds(slot * rows, rows), :], sems.at[slot]))
        copies[-1].start()
    return copies


def slot_weights(chosen, table):
    width = table.shape[0]
    table = jnp.concatenate([table] * (128 // width), axis=0)
    spread = lax.dot_general(chosen, table, (((1,), (1,)), ((), ())), preferred_element_type=jnp.float32)
    spread = jnp.concatenate([spread] * (SUB * width // 128), axis=1)
    row = lax.broadcasted_iota(jnp.int32, spread.shape, 0)
    column = lax.broadcasted_iota(jnp.int32, spread.shape, 1)
    return jnp.where(row % SUB == column // width, spread, 0.0).astype(jnp.bfloat16)


def halves(weights, ints, outs, slot, count, width, pairs):
    depth = SUB * width
    for step in range(width // TILE):
        at = slot * (width // TILE) + step
        made = [
            jnp.dot(weights, ints[pl.ds((2 * at + part) * depth, depth), :], preferred_element_type=jnp.float32)
            for part in range(2)
        ]
        for mate, out in enumerate(outs):
            for orbital in range(2 * pairs):
                source = (mate * 2 * pairs + orbital) * SUB
                both = jnp.concatenate([part[source : source + SUB] for part in made], axis=0)
                out[pl.ds(orbital * count * width + at * TILE, TILE), :] = both.astype(jnp.bfloat16)


def half_rest(ints, block_count, chosen, tables, n_pair, pairs):
    slots, width, _, aux_rows = ints.shape
    count = tables.shape[0]

    def kernel(count_ref, chosen_ref, tables_ref, ints_hbm, *refs):
        outs, (held, large) = refs[:n_pair], refs[n_pair:]
        copies = started(ints_hbm, held, large, slots - count, count, width * width)
        weights = [slot_weights(chosen_ref[...], tables_ref[slot]) for slot in range(count)]
        for slot in range(count):
            copies[slot].wait()
            halves(weights[slot], held, outs, slot, count, width, pairs)
        live = count_ref[0]
        mark = jnp.full((TILE, aux_rows), (MARK * (live + 1)).astype(jnp.float32), jnp.float32).astype(jnp.bfloat16)
        for out in outs:
            spot = pl.ds((count - 1) * width, TILE)
            out[spot, :] = jnp.where(live < slots, mark, out[spot, :])

    return pl.pallas_call(
        kernel,
        in_specs=[pl.BlockSpec(memory_space=SMEM)] + whole(2) + [pl.BlockSpec(memory_space=pltpu.HBM)],
        out_specs=whole(n_pair),
        out_shape=[jax.ShapeDtypeStruct((2 * pairs * count * width, aux_rows), jnp.bfloat16)] * n_pair,
        scratch_shapes=[
            VMEM((count * width * width, aux_rows), jnp.bfloat16),
            pltpu.SemaphoreType.DMA((count,)),
        ],
        compiler_params=PARAMS,
        name="half_rest",
    )(block_count, chosen, tables, *in_hbm(ints.reshape(-1, aux_rows)))


def fitted_first(vir_coef, parts, pairs, counts):
    aux_rows = parts[0].shape[1]
    width, virtual = vir_coef.shape[1], vir_coef.shape[2]
    span = counts[0] * width
    rest_rows = (sum(counts) - 1) * width

    def kernel(vir_ref, *refs):
        held, (fitted_ref, rest_ref, last_ref, own_ref) = refs[: len(parts)], refs[len(parts) :]
        first, rest = [], []
        for part in held:
            tail = part[pl.ds(2 * pairs * span, TILE), :][:, :128].astype(jnp.float32)
            found = [vir_ref[tail[slot, 0].astype(jnp.int32)] for slot in range(sum(counts))]
            first.append(found[0])
            rest.append(jnp.concatenate(found[1:], axis=0))
        own_ref[...] = jnp.concatenate(first, axis=0).T
        rest_ref[...] = jnp.concatenate(rest[:-1], axis=0).T
        last_ref[...] = rest[-1].T
        for orbital in range(2 * pairs):
            blocks = jnp.concatenate([part[pl.ds(orbital * span, width), :] for part in held], axis=0)
            fitted_ref[orbital] = jnp.dot(own_ref[...], blocks, preferred_element_type=jnp.float32)

    return pl.pallas_call(
        kernel,
        in_specs=whole(1 + len(parts)),
        out_specs=whole(3),
        out_shape=[
            jax.ShapeDtypeStruct((2 * pairs, virtual, aux_rows), jnp.float32),
            jax.ShapeDtypeStruct((virtual, (len(parts) - 1) * rest_rows), jnp.bfloat16),
            jax.ShapeDtypeStruct((virtual, rest_rows), jnp.bfloat16),
        ],
        scratch_shapes=[VMEM((virtual, len(parts) * width), jnp.bfloat16)],
        compiler_params=PARAMS,
        name="fitted_first",
    )(vir_coef, *parts)


def live_slots(later, counts, width):
    mark = later[pl.ds((counts[1] - 1) * width, TILE), :][:, :128].astype(jnp.float32)[0, 0]
    return jnp.where(mark < MARK, sum(counts), (mark * (1.0 / MARK)).astype(jnp.int32) - 1)


def live_blocks(first, later, live, orbital, counts, width):
    blocks = []
    for slot in range(1, sum(counts)):
        chunk = int(slot >= counts[0])
        at = (orbital * counts[chunk] + slot - chunk * counts[0]) * width
        block = (first, later)[chunk][pl.ds(at, width), :]
        blocks.append(jnp.where(slot < live, block, jnp.zeros_like(block)))
    return blocks


def fitted_more(fitted, rest, first, later, counts, width):
    count = len(first)

    def kernel(fitted_ref, rest_ref, *refs):
        held, out_ref = list(zip(refs[:count], refs[count : 2 * count])), refs[-1]
        live = [live_slots(part[1], counts, width) for part in held]
        for orbital in range(fitted.shape[0]):
            blocks = []
            for part, alive in zip(held, live):
                blocks += live_blocks(*part, alive, orbital, counts, width)
            total = jnp.dot(rest_ref[...], jnp.concatenate(blocks, axis=0), preferred_element_type=jnp.float32)
            out_ref[orbital] = fitted_ref[orbital] + total

    return pl.pallas_call(
        kernel,
        in_specs=whole(2 + 2 * count),
        out_specs=pl.BlockSpec(memory_space=VMEM),
        out_shape=jax.ShapeDtypeStruct(fitted.shape, fitted.dtype),
        compiler_params=PARAMS,
        name="fitted_more",
    )(fitted, rest, *first, *later)


def coulomb_parts(fitted, last, first, later, pairs, counts, width, quad):
    virtual = fitted.shape[1]
    share = virtual // quad

    def kernel(fitted_ref, last_ref, first_ref, later_ref, *refs):
        outs, block_ref = refs[:-1], refs[-1]
        place = lax.axis_index("aux") % quad
        live = live_slots(later_ref, counts, width)
        for pair in range(pairs):
            sides = []
            for orbital in (2 * pair, 2 * pair + 1):
                blocks = jnp.concatenate(live_blocks(first_ref, later_ref, live, orbital, counts, width), axis=0)
                total = jnp.dot(last_ref[...], blocks, preferred_element_type=jnp.float32)
                sides.append((fitted_ref[orbital] + total).astype(jnp.bfloat16))
            block = lax.dot_general(*sides, (((1,), (1,)), ((), ())), preferred_element_type=jnp.float32)
            block_ref[...] = block.astype(jnp.bfloat16)
            for part, out in enumerate(outs):
                at = pl.multiple_of((place ^ part) * share, share)
                out[pair] = block_ref[pl.ds(at, share), :]

    return pl.pallas_call(
        kernel,
        in_specs=whole(4),
        out_specs=whole(quad),
        out_shape=[jax.ShapeDtypeStruct((pairs, share, virtual), jnp.bfloat16)] * quad,
        scratch_shapes=[VMEM((virtual, virtual), jnp.bfloat16)],
        compiler_params=PARAMS,
        name="coulomb_parts",
    )(fitted, last, first, later)


def density_parts(inverse, chunks, n_pair):
    quad = len(chunks)
    pairs, share, virtual = chunks[0].shape
    rows = virtual // n_pair

    def kernel(inverse_ref, *refs):
        held, own_ref, outs = refs[:quad], refs[quad], refs[quad + 1 : quad + n_pair]
        energy_ref, block_ref, total_ref = refs[quad + n_pair :]
        place = lax.axis_index("aux") % quad
        pair_at = lax.axis_index("pair")
        lane = lax.broadcasted_iota(jnp.int32, (1, virtual), 1)
        energies = []
        totals = [None] * n_pair
        for pair in range(pairs):
            for part, chunk in zip((0, *GATHER_ORDER), held):
                at = pl.multiple_of((place ^ part) * share, share)
                block_ref[pl.ds(at, share), :] = chunk[pair]
            block = block_ref[...].astype(jnp.float32)
            flipped = block_ref[...].T.astype(jnp.float32)
            inverse = inverse_ref[pair]
            energies.append(jnp.sum(block * (2.0 * block - flipped) * inverse))
            even = ((block + flipped) * inverse).astype(jnp.bfloat16)
            odd = ((block - flipped) * (inverse * 3.0**0.5)).astype(jnp.bfloat16)
            left = jnp.concatenate([even, odd], axis=1)
            right = jnp.concatenate([even, -odd], axis=0)
            term = 0.5 * jnp.dot(left, right, preferred_element_type=jnp.float32)
            total_ref[...] = term if pair == 0 else total_ref[...] + term
        for part in range(n_pair):
            totals[part] = total_ref[pl.ds(pl.multiple_of((pair_at ^ part) * rows, rows), rows), :]
        own_ref[...] = totals[0]
        energy_ref[...] = jnp.zeros_like(energy_ref)
        for pair, energy in enumerate(energies):
            energy_ref[...] = jnp.where(lane == pair, energy, energy_ref[...])
        for part in range(1, n_pair):
            outs[part - 1][...] = totals[part].astype(jnp.bfloat16)
            first = (pair_at ^ part) * rows
            last = totals[part][rows - TILE :]
            row = lax.broadcasted_iota(jnp.int32, (TILE, virtual), 0)
            corner = jnp.zeros((1, virtual), jnp.float32)
            for pair, energy in enumerate(energies):
                rest = jnp.full((1, virtual), energy, jnp.float32)
                for at in range(3):
                    piece = rest.astype(jnp.bfloat16).astype(jnp.float32)
                    corner = jnp.where(lane == first + 3 * pair + at, piece, corner)
                    rest = rest - piece
            inside = (lane >= first) & (lane < first + 3 * pairs) & (row == TILE - 1)
            outs[part - 1][pl.ds(rows - TILE, TILE), :] = jnp.where(inside, corner, last).astype(jnp.bfloat16)

    return pl.pallas_call(
        kernel,
        in_specs=whole(1 + quad),
        out_specs=whole(n_pair + 1),
        out_shape=[jax.ShapeDtypeStruct((rows, virtual), jnp.float32)]
        + [jax.ShapeDtypeStruct((rows, virtual), jnp.bfloat16)] * (n_pair - 1)
        + [jax.ShapeDtypeStruct((1, virtual), jnp.float32)],
        scratch_shapes=[
            VMEM((virtual, virtual), jnp.bfloat16),
            VMEM((virtual, virtual), jnp.float32),
        ],
        compiler_params=PARAMS,
        name="density_parts",
    )(inverse, *chunks)


def closing(own, energies, others, pairs, n_half):
    rows, virtual = own.shape

    def kernel(own_ref, energy_ref, *refs):
        held, (density_ref, value_ref) = refs[: len(others)], refs[len(others) :]
        wanted = lax.axis_index("aux") % n_half
        pair_at = lax.axis_index("pair")
        lane = lax.broadcasted_iota(jnp.int32, (1, virtual), 1)
        first = pair_at * rows
        found = jnp.zeros((1, virtual), jnp.float32)
        total = own_ref[...]
        for mate, ref in zip((0, *ROW_ORDER), (None, *held)):
            at = wanted - (pair_at ^ mate) * pairs
            here = (at >= 0) & (at < pairs)
            if mate == 0:
                found += jnp.where(here & (lane == at), energy_ref[...], 0.0)
            else:
                part = ref[...].astype(jnp.float32)
                spot = lane - first - 3 * at
                found += jnp.where(here & (spot >= 0) & (spot < 3), part[rows - 1 :], 0.0)
                total += part
        value_ref[...] = jnp.sum(found, axis=1, keepdims=True)
        density_ref[...] = total
        head = -(-3 * pairs // TILE) * TILE
        top = total[:head]
        wide = lax.broadcasted_iota(jnp.int32, (head, virtual), 1)
        row = lax.broadcasted_iota(jnp.int32, (head, virtual), 0)
        column = jnp.sum(jnp.where(wide == first + rows - 1, top, 0.0), axis=1, keepdims=True)
        turned = jnp.sum(jnp.where(wide == first + row, column, 0.0), axis=0, keepdims=True)
        last = total[rows - SUB :]
        inside = (lane >= first) & (lane < first + 3 * pairs)
        inside = inside & (lax.broadcasted_iota(jnp.int32, (SUB, virtual), 0) == SUB - 1)
        density_ref[pl.ds(rows - SUB, SUB), :] = jnp.where(inside, turned, last)

    return pl.pallas_call(
        kernel,
        in_specs=whole(2 + len(others)),
        out_specs=whole(2),
        out_shape=[jax.ShapeDtypeStruct((rows, virtual), jnp.float32), jax.ShapeDtypeStruct((1, 1), jnp.float32)],
        compiler_params=PARAMS,
        name="closing",
    )(own, energies, *others)


def exchanged(parts, axis, order, low=0):
    return [swapped(parts[d], axis, d << low) for d in order]


def summed(value, axis, low, bits):
    if bits == 0:
        return value
    if bits == 1:
        other = swapped(value, axis, 1 << low)
        return (value.astype(jnp.float32) + other.astype(jnp.float32)).astype(jnp.bfloat16)
    place = (lax.axis_index(axis) >> low) & 3
    share = value.shape[1] // 4
    parts = [lax.dynamic_slice_in_dim(value, (place ^ d) * share, share, 1) for d in range(4)]
    chunks = scattered(parts, axis, low, bits)
    out = jnp.zeros_like(value)
    for d, chunk in zip((0, *GATHER_ORDER), chunks):
        out = lax.dynamic_update_slice_in_dim(out, chunk, (place ^ d) * share, 1)
    return out


def scattered(parts, axis, low, bits):
    total = parts[0].astype(jnp.float32)
    for part in exchanged(parts, axis, SUM_ORDER, low):
        total += part.astype(jnp.float32)
    total = summed(total.astype(jnp.bfloat16), axis, low + 2, bits - 2)
    return [total] + exchanged([total] * len(parts), axis, GATHER_ORDER, low)


def per_device(
    shell_ints, block_ids, block_count, occ_coef, occ_pick, vir_coef, occ_energy, vir_energy
):
    _, slots, width, _ = shell_ints.shape
    n_aux = lax.axis_size("aux")
    n_pair = lax.axis_size("pair")
    n_half = n_aux // 2
    pairs = n_half // n_pair
    bits = n_aux.bit_length() - 1

    ints = jnp.transpose(shell_ints, (1, 2, 3, 0))
    counts = (slots // 2, slots - slots // 2)
    *first, chosen, tables = half_first(
        ints, block_ids, occ_pick, occ_coef, counts[0], n_aux, n_pair
    )
    block_count, _ = lax.optimization_barrier((block_count, first[0]))
    later = list(half_rest(ints, block_count, chosen, tables, n_pair, pairs))
    got = [made[:1] + exchanged(made, "pair", PAIR_ORDER) for made in (first, later)]

    slowest = 1 + PAIR_ORDER.index(max(PAIR_ORDER))
    ends = [group.pop(slowest) for group in got]
    fitted, rest, last = fitted_first(vir_coef, got[0] + ends[:1], pairs, counts)
    fitted = fitted_more(fitted, rest, *got, counts, width)
    parts = coulomb_parts(fitted, last, *ends, pairs, counts, width, 4)

    occ_pick, occ_energy, vir_energy, _ = lax.optimization_barrier((occ_pick, occ_energy, vir_energy, later[0]))
    own_pairs = lax.axis_index("pair") * pairs + jnp.arange(pairs, dtype=jnp.int32)
    spots = jnp.arange(n_aux, dtype=jnp.int32)
    batch = occ_pick[:n_aux]
    orbitals = jnp.arange(occ_energy.shape[0], dtype=jnp.int32)
    energies = jnp.sum(jnp.where(batch[:, None] == orbitals[None, :], occ_energy[None, :], 0.0), axis=1)
    levels = jnp.sum(jnp.where(own_pairs[:, None] == spots[None, :] % n_half, energies[None, :], 0.0), axis=1)
    inverse = 1.0 / (levels[:, None, None] - vir_energy[None, :, None] - vir_energy[None, None, :])

    chunks = scattered(parts, "aux", 0, bits)
    outs = density_parts(inverse, chunks, n_pair)
    others = exchanged(outs, "pair", ROW_ORDER)
    density, energy = closing(outs[0], outs[-1], others, pairs, n_half)
    return (energy.reshape(1), density)


def solution(mesh):
    placed = (P("aux", "pair", None, None), P("pair", None), P("pair"), P(), P(), P(), P(), P())
    return jax.shard_map(
        per_device,
        mesh=mesh,
        in_specs=placed,
        out_specs=(P("aux"), P("pair", None)),
        check_vma=False,
    )
```
